256 devices in a mesh: blk: 64 (over z, y, core), sub: 4 (over x).
Axes of the slice: x: 4, y: 4, z: 8, core: 2. Of those that a mesh axis runs over, the one named last changes fastest.
Arguments:
- tracers: float32 [2560, 4, 5400], P(('blk', 'sub')), may hold values from -6 to 6
- velocity: float32 [2560, 4, 5400], P(('blk', 'sub')), may hold values from -3 to 3
- kappa: float32 [2560, 5400], P(('blk', 'sub')), may hold values from 0.1 to 4
- kmt: float32 [2560, 5400], P(('blk', 'sub')), may hold values from -1 to 2.5
- block_owner: int32 [1280], replicated, may hold values from 0 to 2559, as said below
- neighbours: int32 [1280, 4], replicated, may hold values from -1 to 1279, as said below
- fold_partner: int32 [1280], replicated, may hold values from -1 to 1279, as said below
Outputs:
- tracers_out: float32 [2560, 4, 5400], P(('blk', 'sub'))
The draws below stay inside these ranges and needn't reach their ends.
Inputs may be any that keep to these rules, and one draw needn't show every extreme that they name: `block_owner`: the values are distinct. Every device holds between 3 and 10 blocks, in its first slots; devices in index order hold consecutive runs of the blocks taken along a serpentine curve over the block grid. `neighbours`: row b lists the blocks west, east, south and north of block b on a grid of 40 by 40 blocks that is periodic from west to east, or -1 where that place is land or off the grid; the north entry of the northernmost row is -1. The owner of every listed block lies at most 27 devices from the owner of block b. `fold_partner`: for a block of the northernmost row, the block of that row at the mirrored column (39 - column); -1 for all other blocks. Its owner lies at most 27 devices from block b's owner.
All inputs are finite; a program needn't handle non-finite values.
Results may differ from the reference program's by a relative error of at most 0.0003.
Values sent between devices are 32-bit elements; how exact they have to be, the bound alone decides.
A program may use at most 192 MiB of HBM per device.

```python
import math
import jax
import jax.numpy as jnp
from jax import lax

IB = 90
JB = 60
VERTICAL_LEVELS = 2
TRACER_COUNT = 2
STEPS = 1
NBX = 40
DEVICE_SLOTS = 10
REACH = 27
NBY = 40
NBLK = 1280
TOTAL_SLOTS = 2560
BLOCK_COLUMNS = 5400


def device_loads(load_key):
    device_number = TOTAL_SLOTS // DEVICE_SLOTS
    light_count = min(REACH, 5 * device_number // 8)
    deficit = 2 * light_count
    heavy_count = deficit // 5
    extra_load = deficit % 5
    rest_count = device_number - light_count - heavy_count - 1
    pair_count = rest_count // 2
    lone_count = rest_count - 2 * pair_count
    prefix = jnp.array([3] * light_count + [10] * heavy_count + [5 + extra_load], jnp.int32)
    swing = jax.random.randint(load_key, (pair_count,), -2, 3).astype(jnp.int32)
    paired = jnp.stack([5 + swing, 5 - swing], axis=1).reshape(-1)
    trailing = jnp.full((lone_count,), 5, jnp.int32)
    return jnp.concatenate([prefix, paired, trailing])


def build_grid(key):
    key = jax.random.fold_in(key, 17)
    land_key, label_key, load_key = jax.random.split(key, 3)
    places = NBX * NBY
    block_count = NBLK
    land_count = places - block_count
    place_ids = jnp.arange(places, dtype=jnp.int32)
    row_ids = place_ids // NBX
    col_ids = place_ids % NBX
    eligible = (row_ids >= 1) & (row_ids <= NBY - 2)
    shuffled = jax.random.permutation(land_key, places).astype(jnp.int32)
    land_score = jnp.where(eligible, shuffled, places + place_ids)
    land_order = jnp.argsort(land_score)
    is_land = jnp.zeros((places,), jnp.int32).at[land_order[:land_count]].set(1)
    curve_key = row_ids * NBX + jnp.where(row_ids % 2 == 0, col_ids, NBX - 1 - col_ids)
    curve_order = jnp.argsort(jnp.where(is_land == 1, places + curve_key, curve_key)).astype(jnp.int32)
    curve_rank = jnp.zeros((places,), jnp.int32).at[curve_order].set(place_ids)
    labels = jax.random.permutation(label_key, block_count).astype(jnp.int32)
    place_label = jnp.where(is_land == 1, -1, labels[jnp.minimum(curve_rank, block_count - 1)])
    loads = device_loads(load_key)
    ends = jnp.cumsum(loads).astype(jnp.int32)
    starts = ends - loads
    ranks = jnp.arange(block_count, dtype=jnp.int32)
    owner_dev = jnp.sum((ends[None, :] <= ranks[:, None]).astype(jnp.int32), axis=1)
    owner_code = owner_dev * DEVICE_SLOTS + ranks - starts[owner_dev]
    block_owner = jnp.zeros((block_count,), jnp.int32).at[labels].set(owner_code)
    west_place = row_ids * NBX + (col_ids + NBX - 1) % NBX
    east_place = row_ids * NBX + (col_ids + 1) % NBX
    south_place = jnp.where(row_ids > 0, place_ids - NBX, -1)
    north_place = jnp.where(row_ids < NBY - 1, place_ids + NBX, -1)
    mirror_place = jnp.where(row_ids == NBY - 1, row_ids * NBX + NBX - 1 - col_ids, -1)

    def label_of(target):
        return jnp.where(target >= 0, place_label[jnp.maximum(target, 0)], -1)
    table = jnp.stack([label_of(west_place), label_of(east_place), label_of(south_place), label_of(north_place)], axis=1)
    ocean_places = curve_order[:block_count]
    neighbours = jnp.zeros((block_count, 4), jnp.int32).at[labels].set(table[ocean_places])
    fold_partner = jnp.zeros((block_count,), jnp.int32).at[labels].set(label_of(mirror_place)[ocean_places])
    return (block_owner, neighbours, fold_partner)


def draw_block_owner(key, part):
    return build_grid(key)[0]


def draw_neighbours(key, part):
    return build_grid(key)[1]


def draw_fold_partner(key, part):
    return build_grid(key)[2]


def level_of(key, extent, cuts, smallest, largest):
    def one(axis_at, parts):
        steps = jax.random.uniform(jax.random.fold_in(jax.random.fold_in(key, 6), axis_at), (parts,), jnp.float32, smallest / len(cuts), largest / len(cuts))
        return jnp.repeat(jnp.exp(steps), extent[axis_at] // parts).reshape((-1,) + (1,) * (len(extent) - axis_at - 1))

    gain = one(*cuts[0])
    for cut in cuts[1:]:
        gain = gain * one(*cut)
    return gain


def noise(own_key, shape, scale, most, cuts=(), kind=jnp.bfloat16):
    entries = jax.random.normal(own_key, shape, jnp.float32) * scale
    if len(cuts) > 0:
        entries = level_of(own_key, shape, cuts, -0.22, 0.18) * entries
    return jnp.clip(entries, min=-most, max=most).astype(kind)


def setup_inputs(seed: int = 0) -> dict:
    keys = jax.random.split(jax.random.key(seed), 8)
    return {
        "tracers": noise(keys[0], (TOTAL_SLOTS, TRACER_COUNT * VERTICAL_LEVELS, BLOCK_COLUMNS), 1.0, 6.0, ((0, 256),), jnp.float32),
        "velocity": noise(keys[1], (TOTAL_SLOTS, 2 * VERTICAL_LEVELS, BLOCK_COLUMNS), 0.5, 3.0, ((0, 256),), jnp.float32),
        "kappa": jnp.clip(jnp.exp(math.log(4.0) - 3.6888794 * jax.random.uniform(keys[2], (TOTAL_SLOTS, BLOCK_COLUMNS), jnp.float32) ** level_of(keys[2], (TOTAL_SLOTS, BLOCK_COLUMNS), ((0, 256),), -0.2, 0.2)), 0.1, 4.0),
        "kmt": jnp.clip(-1.0 + 3.5 * jax.random.uniform(keys[3], (TOTAL_SLOTS, BLOCK_COLUMNS), jnp.float32) ** level_of(keys[3], (TOTAL_SLOTS, BLOCK_COLUMNS), ((0, 256),), -0.2, 0.2), -1.0, 2.5),
        "block_owner": draw_block_owner(jax.random.fold_in(keys[7], 71), 0),
        "neighbours": draw_neighbours(jax.random.fold_in(keys[7], 71), 0),
        "fold_partner": draw_fold_partner(jax.random.fold_in(keys[7], 71), 0),
    }


COURANT = 0.2


def edge_pack(block_field):
    count, chans, rows, cols = block_field.shape
    west_edge = block_field[:, :, :, 0:2].reshape(count, chans, rows * 2)
    east_edge = block_field[:, :, :, cols - 2:].reshape(count, chans, rows * 2)
    south_edge = block_field[:, :, 0:2, :].reshape(count, chans, 2 * cols)
    north_edge = block_field[:, :, rows - 2:, :].reshape(count, chans, 2 * cols)
    return jnp.concatenate([west_edge, east_edge, south_edge, north_edge], axis=2)


def fetch(source, link_codes):
    safe_codes = jnp.maximum(link_codes, 0)
    picked = jnp.take(source, safe_codes.reshape(-1), axis=0)
    picked = picked.reshape(link_codes.shape + source.shape[1:])
    return jnp.where((link_codes >= 0)[..., None, None], picked, 0.0)


def extend(block_field, sources, fold_sign):
    count, chans, rows, cols = block_field.shape
    strip = 2 * rows
    west_halo = sources[:, 0, :, strip:2 * strip].reshape(count, chans, rows, 2)
    east_halo = sources[:, 1, :, 0:strip].reshape(count, chans, rows, 2)
    south_halo = sources[:, 2, :, 2 * strip + 2 * cols:].reshape(count, chans, 2, cols)
    north_halo = sources[:, 3, :, 2 * strip:2 * strip + 2 * cols].reshape(count, chans, 2, cols)
    mirrored = sources[:, 4, :, 2 * strip + 2 * cols:].reshape(count, chans, 2, cols)[:, :, ::-1, ::-1]
    north_halo = north_halo + fold_sign * mirrored
    middle = jnp.concatenate([west_halo, block_field, east_halo], axis=3)
    corner = jnp.zeros((count, chans, 2, 2), block_field.dtype)
    bottom = jnp.concatenate([corner, south_halo, corner], axis=3)
    top_rows = jnp.concatenate([corner, north_halo, corner], axis=3)
    return jnp.concatenate([bottom, middle, top_rows], axis=2)


def prepare(static_ext, diffusivity):
    levels = (static_ext.shape[1] - 1) // 2
    rows = static_ext.shape[2] - 4
    cols = static_ext.shape[3] - 4
    east_vel = static_ext[:, :levels]
    north_vel = static_ext[:, levels:2 * levels]
    depth = static_ext[:, 2 * levels:]
    level_ids = jnp.arange(levels).astype(static_ext.dtype).reshape(1, levels, 1, 1)
    wet = jnp.clip(depth - level_ids, 0.0, 1.0).astype(static_ext.dtype)
    face_x = 0.5 * (east_vel[:, :, 2:rows + 2, 1:cols + 2] + east_vel[:, :, 2:rows + 2, 2:cols + 3])
    face_x = face_x * wet[:, :, 2:rows + 2, 1:cols + 2] * wet[:, :, 2:rows + 2, 2:cols + 3]
    face_y = 0.5 * (north_vel[:, :, 1:rows + 2, 2:cols + 2] + north_vel[:, :, 2:rows + 3, 2:cols + 2])
    face_y = face_y * wet[:, :, 1:rows + 2, 2:cols + 2] * wet[:, :, 2:rows + 3, 2:cols + 2]
    inner = wet[:, :, 2:rows + 2, 2:cols + 2]
    coupling = diffusivity[:, None] * inner[:, :-1] * inner[:, 1:]
    return face_x, face_y, inner, coupling


def face_flux(velocity_face, left_far, left_near, right_near, right_far):
    centered = (7.0 * (left_near + right_near) - (left_far + right_far)) / 12.0
    upwind = (right_far - 3.0 * right_near + 3.0 * left_near - left_far) / 12.0
    return velocity_face * centered + jnp.abs(velocity_face) * upwind


def vertical_solve(rhs_cols, coupling):
    levels = rhs_cols.shape[2]
    partials = []
    ratios = []
    for level in range(levels):
        coef_below = coupling[:, :, level] if level < levels - 1 else 0.0
        coef_above = coupling[:, :, level - 1] if level > 0 else 0.0
        diagonal = 1.0 + coef_above + coef_below
        if level == 0:
            divider_value = diagonal
            partial_value = rhs_cols[:, :, 0] / divider_value
        else:
            divider_value = diagonal - coef_above * ratios[-1]
            partial_value = (rhs_cols[:, :, level] + coef_above * partials[-1]) / divider_value
        partials.append(partial_value)
        ratios.append(coef_below / divider_value)
    result = [None] * levels
    result[levels - 1] = partials[levels - 1]
    for level in range(levels - 2, -1, -1):
        result[level] = partials[level] + ratios[level] * result[level + 1]
    return jnp.stack(result, axis=2)


def advance(tracer_ext, face_x, face_y, inner, coupling):
    count, chans = tracer_ext.shape[0], tracer_ext.shape[1]
    levels, rows, cols = inner.shape[1], inner.shape[2], inner.shape[3]
    ext_cols = tracer_ext.reshape(count, chans // levels, levels, rows + 4, cols + 4)
    middle = ext_cols[:, :, :, 2:rows + 2]
    flux_x = face_flux(face_x[:, None], middle[..., 0:cols + 1], middle[..., 1:cols + 2], middle[..., 2:cols + 3], middle[..., 3:cols + 4])
    column = ext_cols[..., 2:cols + 2]
    flux_y = face_flux(face_y[:, None], column[:, :, :, 0:rows + 1], column[:, :, :, 1:rows + 2], column[:, :, :, 2:rows + 3], column[:, :, :, 3:rows + 4])
    center = middle[..., 2:cols + 2]
    divergence = (flux_x[..., 1:] - flux_x[..., :-1]) + (flux_y[:, :, :, 1:] - flux_y[:, :, :, :-1])
    explicit = center - COURANT * inner[:, None] * divergence
    solved = vertical_solve(explicit, coupling[:, None])
    return solved.reshape(count, chans, rows, cols)


def reference(tracers, velocity, kappa, kmt, block_owner, neighbours, fold_partner):
    slot_total = tracers.shape[0]
    block_count = block_owner.shape[0]
    slot_block = jnp.full((slot_total,), -1, jnp.int32).at[block_owner].set(jnp.arange(block_count, dtype=jnp.int32))
    live_slot = slot_block >= 0
    safe_ids = jnp.maximum(slot_block, 0)
    links = jnp.concatenate([neighbours[safe_ids], fold_partner[safe_ids][:, None]], axis=1)
    links = jnp.where(live_slot[:, None], links, -1)
    link_codes = jnp.where(links >= 0, block_owner[jnp.maximum(links, 0)], -1).astype(jnp.int32)
    levels = velocity.shape[1] // 2
    statics = jnp.concatenate([velocity, kmt[:, None, :]], axis=1)
    statics = statics.reshape(slot_total, 2 * levels + 1, JB, IB)
    static_pack = edge_pack(statics)
    fold_sign = jnp.concatenate([-jnp.ones((2 * levels,), jnp.float32), jnp.ones((1,), jnp.float32)]).reshape(1, -1, 1, 1)
    groups = slot_total // DEVICE_SLOTS
    chans = tracers.shape[1]
    state = tracers.reshape(slot_total, chans, JB, IB)
    grouped_statics = statics.reshape(groups, DEVICE_SLOTS, 2 * levels + 1, JB, IB)
    grouped_kappa = kappa.reshape(groups, DEVICE_SLOTS, JB, IB)
    grouped_codes = link_codes.reshape(groups, DEVICE_SLOTS, 5)
    for step in range(STEPS):
        tracer_pack = edge_pack(state)

        def one_group(input_arrays):
            block_state, block_static, diffusivity, codes = input_arrays
            static_ext = extend(block_static, fetch(static_pack, codes), fold_sign)
            face_x, face_y, inner, coupling = prepare(static_ext, diffusivity)
            tracer_ext = extend(block_state, fetch(tracer_pack, codes), 1.0)
            return advance(tracer_ext, face_x, face_y, inner, coupling)

        state = lax.map(one_group, (state.reshape(groups, DEVICE_SLOTS, chans, JB, IB), grouped_statics, grouped_kappa, grouped_codes))
        state = state.reshape(slot_total, chans, JB, IB)
    result = state.reshape(slot_total, chans, JB * IB)
    return jnp.where(live_slot[:, None, None], result, 0.0)
```

```python
import jax
import jax.numpy as jnp
from jax import lax
from jax.experimental import pallas as pl
from jax.experimental.pallas import tpu as pltpu
from jax.sharding import PartitionSpec as P

IB = 90
JB = 60
SLOTS = 10
COURANT = 0.2
GROUP = 8
FAR = 3
ROWS = 112
LANES = 128
EAST_LANE = 64
MESH = pl.DeviceIdType.MESH


def padded(parts, lane_parts):
    rows = jnp.concatenate(parts, axis=0)
    return jnp.pad(rows, ((0, ROWS - rows.shape[0]), (0, lane_parts - rows.shape[1])))


def edge_packs(tracers, velocity, kmt):
    def rows_at(near, far):
        def cut(field, row):
            piece = field[..., row * IB : (row + 1) * IB]
            return piece.reshape(-1, IB)

        return padded(
            [cut(tracers, near), cut(tracers, far), cut(velocity[:, 2:4], near), cut(kmt, near)], LANES
        )

    def columns_at(near, far):
        def cut(field, column):
            piece = field.reshape(field.shape[:-1] + (JB, IB))[..., column]
            return piece.reshape(-1, JB)

        return padded(
            [cut(tracers, near), cut(tracers, far), cut(velocity[:, 0:2], near), cut(kmt, near)], EAST_LANE
        )

    south = rows_at(0, 1)
    north = rows_at(JB - 1, JB - 2)
    sides = jnp.concatenate([columns_at(0, 1), columns_at(IB - 1, IB - 2)], axis=1)
    return jnp.stack([south, north, sides])


def link_table(me, total, block_owner, neighbours, fold_partner):
    slots = (me - GROUP // 2) * SLOTS + jnp.arange(GROUP * SLOTS, dtype=jnp.int32)
    slots = jnp.mod(slots, total * SLOTS)
    hit = slots[:, None] == block_owner[None, :]
    links = jnp.concatenate([neighbours, fold_partner[:, None]], axis=1)
    picked = jnp.sum(jnp.where(hit[:, :, None], links[None] + 1, 0), axis=1) - 1
    ids = jnp.arange(block_owner.shape[0], dtype=jnp.int32)
    same = picked[:, :, None] == ids
    codes = jnp.sum(jnp.where(same, block_owner + 1, 0), axis=2) - 1
    away = jnp.mod(codes // SLOTS - me + GROUP * FAR, total)
    usable = (codes >= 0) & (away % GROUP == 0) & (away >= 0) & (away <= 2 * GROUP * FAR)
    source = jnp.where(usable, away // GROUP * SLOTS + codes % SLOTS, -1)
    live = jnp.any(hit, axis=1)
    return source, live


def pick(hot, packed):
    count = packed.shape[0]
    lanes = packed.shape[-1]

    def one(start, chans):
        rows = packed[:, start : start + SLOTS * chans].reshape(count * SLOTS, chans, lanes)
        out = jnp.einsum("xy,ycl->xcl", hot, rows, precision=lax.Precision.HIGHEST)
        return out.reshape(GROUP, SLOTS * chans, lanes)

    return jnp.concatenate([one(0, 4), one(40, 4), one(80, 2), one(100, 1)], axis=1)


def choose(source, window):
    hot = (source[:, :, None] == jnp.arange((2 * FAR + 1) * SLOTS)).astype(jnp.float32)
    south_edge, north_edge, sides = window[:, 0], window[:, 1], window[:, 2]
    south = pick(hot[:, 2], north_edge)
    north = pick(hot[:, 3], south_edge)
    mirrored = pick(hot[:, 4], north_edge)[:, :, IB - 1 :: -1]
    sign = jnp.where((jnp.arange(110) >= 80) & (jnp.arange(110) < 100), -1.0, 1.0)
    mirrored = mirrored * sign[:, None]
    north = north + jnp.pad(mirrored, ((0, 0), (0, 0), (0, LANES - IB)))
    west = pick(hot[:, 0], sides[:, :, EAST_LANE:])
    east = pick(hot[:, 1], sides[:, :, :EAST_LANE])
    out = jnp.stack([south, north, jnp.concatenate([west, east], axis=2)], axis=1)
    return jnp.pad(out, ((0, 0), (0, 0), (0, ROWS - 110), (0, 0)))


def coordinates(index, total):
    index = lax.rem(index + total, total)
    return (index // 4, lax.rem(index, 4))


def greet(offsets, me, total):
    barrier = pltpu.get_barrier_semaphore()
    for offset in offsets:
        pl.semaphore_signal(barrier, inc=1, device_id=coordinates(me + offset, total), device_id_type=MESH)
    pl.semaphore_wait(barrier, len(offsets))


def far_kernel(total, pack_ref, out_ref, send_sem, recv_sem, own_sem):
    me = lax.axis_index("blk") * 4 + lax.axis_index("sub")
    steps = [e for e in range(-FAR, FAR + 1) if e != 0]
    own = pltpu.make_async_copy(pack_ref, out_ref.at[FAR], own_sem)
    own.start()
    greet([GROUP * e for e in steps], me, total)
    copies = []
    for e in steps:
        copy = pltpu.make_async_remote_copy(
            src_ref=pack_ref,
            dst_ref=out_ref.at[FAR - e],
            send_sem=send_sem.at[FAR - e],
            recv_sem=recv_sem.at[FAR - e],
            device_id=coordinates(me + GROUP * e, total),
            device_id_type=MESH,
        )
        copy.start()
        copies.append(copy)
    own.wait()
    for copy in copies:
        copy.wait()


def near_kernel(total, message_ref, out_ref, send_sem, recv_sem, own_sem):
    me = lax.axis_index("blk") * 4 + lax.axis_index("sub")
    half = GROUP // 2
    own = pltpu.make_async_copy(message_ref.at[half], out_ref.at[half], own_sem)
    own.start()
    greet([c for c in range(-half, half + 1) if c != 0], me, total)
    copies = []
    for c in range(-half, half):
        if c == 0:
            continue
        copy = pltpu.make_async_remote_copy(
            src_ref=message_ref.at[c + half],
            dst_ref=out_ref.at[c + half],
            send_sem=send_sem.at[c + half],
            recv_sem=recv_sem.at[c + half],
            device_id=coordinates(me + c, total),
            device_id_type=MESH,
        )
        copy.start()
        copies.append(copy)
    own.wait()
    for copy in copies:
        copy.wait()


def exchange(kernel, data, count, ident, total):
    return pl.pallas_call(
        lambda *refs: kernel(total, *refs),
        out_shape=jax.ShapeDtypeStruct((count,) + data.shape[-3:], jnp.float32),
        in_specs=[pl.BlockSpec(memory_space=pl.ANY)],
        out_specs=pl.BlockSpec(memory_space=pl.ANY),
        scratch_shapes=[
            pltpu.SemaphoreType.DMA((count,)),
            pltpu.SemaphoreType.DMA((count,)),
            pltpu.SemaphoreType.DMA,
        ],
        compiler_params=pltpu.CompilerParams(collective_id=ident, has_side_effects=True),
    )(data)


def finish(tracers, velocity, kappa, kmt, halos, live):
    def rows_of(index, start, chans, lanes):
        piece = halos[index, start : start + SLOTS * chans, lanes]
        return piece.reshape(SLOTS, chans, -1)

    def grid(field):
        return field.reshape(SLOTS, -1, JB, IB)

    row = slice(0, IB)
    west = slice(0, JB)
    east = slice(EAST_LANE, EAST_LANE + JB)
    stack = jnp.stack

    def both(index, lanes, start, chans, order, axis):
        near = rows_of(index, start, chans, lanes)
        if order is None:
            return jnp.expand_dims(near, axis)
        far = rows_of(index, 40, chans, lanes)
        return stack([far, near] if order else [near, far], axis=axis)

    state, speed = grid(tracers), grid(velocity)
    depth = grid(kmt)
    ext_x = jnp.concatenate([both(2, west, 0, 4, True, 3), state, both(2, east, 0, 4, False, 3)], axis=3)
    ext_y = jnp.concatenate([both(0, row, 0, 4, True, 2), state, both(1, row, 0, 4, False, 2)], axis=2)
    u = jnp.concatenate([both(2, west, 80, 2, None, 3), speed[:, :2], both(2, east, 80, 2, None, 3)], axis=3)
    v = jnp.concatenate([both(0, row, 80, 2, None, 2), speed[:, 2:], both(1, row, 80, 2, None, 2)], axis=2)
    depth_x = jnp.concatenate([both(2, west, 100, 1, None, 3), depth, both(2, east, 100, 1, None, 3)], axis=3)
    depth_y = jnp.concatenate([both(0, row, 100, 1, None, 2), depth, both(1, row, 100, 1, None, 2)], axis=2)
    levels = jnp.arange(2, dtype=jnp.float32).reshape(1, 2, 1, 1)
    wet_x = jnp.clip(depth_x - levels, 0.0, 1.0)
    wet_y = jnp.clip(depth_y - levels, 0.0, 1.0)
    wet = jnp.clip(depth - levels, 0.0, 1.0)
    face_x = 0.5 * (u[..., :-1] + u[..., 1:]) * wet_x[..., :-1] * wet_x[..., 1:]
    face_y = 0.5 * (v[:, :, :-1] + v[:, :, 1:]) * wet_y[:, :, :-1] * wet_y[:, :, 1:]
    coupling = kappa.reshape(SLOTS, JB, IB) * wet[:, 0] * wet[:, 1]

    def flux(velocity_face, far_a, a, b, far_b):
        speed_face = velocity_face[:, None]
        centered = (7.0 * (a + b) - (far_a + far_b)) / 12.0
        upwind = (far_b - 3.0 * b + 3.0 * a - far_a) / 12.0
        return speed_face * centered + jnp.abs(speed_face) * upwind

    x = ext_x.reshape(SLOTS, 2, 2, JB, IB + 4)
    y = ext_y.reshape(SLOTS, 2, 2, JB + 4, IB)
    n = IB + 1
    flux_x = flux(face_x, x[..., :n], x[..., 1 : n + 1], x[..., 2 : n + 2], x[..., 3:])
    n = JB + 1
    flux_y = flux(face_y, y[:, :, :, :n], y[:, :, :, 1 : n + 1], y[:, :, :, 2 : n + 2], y[:, :, :, 3:])
    divergence = flux_x[..., 1:] - flux_x[..., :-1] + (flux_y[:, :, :, 1:] - flux_y[:, :, :, :-1])
    explicit = state.reshape(SLOTS, 2, 2, JB, IB) - COURANT * wet[:, None] * divergence
    c = coupling[:, None]
    first = explicit[:, :, 0] / (1.0 + c)
    ratio = c / (1.0 + c)
    lower = (explicit[:, :, 1] + c * first) / (1.0 + c - c * ratio)
    upper = first + ratio * lower
    result = stack([upper, lower], axis=2).reshape(SLOTS, 4, JB * IB)
    return jnp.where(live[:, None, None], result, 0.0)


def per_device(tracers, velocity, kappa, kmt, block_owner, neighbours, fold_partner):
    total = lax.axis_size("blk") * lax.axis_size("sub")
    me = lax.axis_index("blk") * 4 + lax.axis_index("sub")
    packs = edge_packs(tracers, velocity, kmt)
    window = exchange(far_kernel, packs, 2 * FAR + 1, 0, total)
    source, live = link_table(me, total, block_owner, neighbours, fold_partner)
    messages = choose(source, window)
    arrived = exchange(near_kernel, messages, GROUP, 1, total)
    halos = jnp.sum(arrived, axis=0)
    half = GROUP // 2 * SLOTS
    return finish(tracers, velocity, kappa, kmt, halos, live[half : half + SLOTS])


def solution(mesh):
    placed = (
        P(("blk", "sub"), None, None),
        P(("blk", "sub"), None, None),
        P(("blk", "sub"), None),
        P(("blk", "sub"), None),
        P(),
        P(),
        P(),
    )
    return jax.shard_map(
        per_device,
        mesh=mesh,
        in_specs=placed,
        out_specs=P(("blk", "sub"), None, None),
        check_vma=False,
    )
```

```python
import jax
import jax.numpy as jnp
from jax import lax
from jax.experimental import pallas as pl
from jax.experimental.pallas import tpu as pltpu
from jax.sharding import PartitionSpec as P

IB = 90
JB = 60
CELLS = IB * JB
SLOTS = 10
PAIRS = SLOTS // 2
DEVICES = 256
COURANT = 0.2
GROUP = 8
HALF = GROUP // 2
FAR = 3
LANES = 128
TILES = 43
FRAME = 47
SIDE = 64
PACK = SLOTS + 1
OWN_UP = FAR * PACK
OWN_DOWN = OWN_UP + PACK
EXTRA = OWN_DOWN + (FAR + 1) * PACK
EMPTY = EXTRA + 2 * PACK
WINDOW = EMPTY + 2
WANT = 2 * SLOTS + 2
FOLD_REACH = 14
MESH = pl.DeviceIdType.MESH
COLUMNS = ("south", "north", "earlier", "later", "west", "east", "send_later", "send_earlier", "next", "previous", "fold", "live", "up")
AT = {name: number for number, name in enumerate(COLUMNS)}


def position():
    return lax.axis_index("blk") * 4 + lax.axis_index("sub")


def lanes_at(tile):
    return pl.ds(tile * LANES, LANES)


def iotas():
    return (
        lax.broadcasted_iota(jnp.int32, (8, LANES), 0),
        lax.broadcasted_iota(jnp.int32, (8, LANES), 1),
    )


def take(packed, index):
    return jnp.take_along_axis(packed, index, axis=1, mode="promise_in_bounds")


def row(value, number):
    return jnp.broadcast_to(value[number : number + 1], (8, LANES))


def table_kernel(owner_ref, near_ref, fold_ref, out_ref):
    me = position()
    rows = GROUP * SLOTS
    blocks = owner_ref.shape[1]
    number = lax.broadcasted_iota(jnp.int32, (rows, 1), 0).astype(jnp.float32)
    which = jnp.floor((number + 0.5) * (1.0 / SLOTS))
    slot = number - which * SLOTS
    offset = which - HALF
    device = offset + jnp.float32(1) * me
    device = jnp.where(device < 0, device + DEVICES, device)
    device = jnp.where(device >= DEVICES, device - DEVICES, device)
    code = device * SLOTS + slot
    owner = owner_ref[...].astype(jnp.float32)
    hit = owner == code
    ids = lax.broadcasted_iota(jnp.int32, (1, blocks), 1).astype(jnp.float32)

    def total(mask, value):
        return jnp.sum(jnp.where(mask, value, 0.0), axis=1, keepdims=True)

    own_count = total((owner >= device * SLOTS) & (owner < device * SLOTS + SLOTS), 1.0)
    before_count = total((owner >= device * SLOTS - SLOTS) & (owner < device * SLOTS), 1.0)
    live = total(hit, 1.0)
    links = []
    for k in range(5):
        link = near_ref[k : k + 1, :] if k < 4 else fold_ref[...]
        block = total(hit, link.astype(jnp.float32) + 1.0) - 1.0
        links.append(total(block == ids, owner + 1.0) - 1.0)

    def where_is(other):
        source = jnp.floor((other + 0.5) * (1.0 / SLOTS))
        apart = source - device
        eight = apart + offset
        hop = jnp.floor((eight + 0.5) * (1.0 / GROUP))
        there = (other >= 0) & (hop * GROUP == eight)
        return there, source, other - source * SLOTS, apart, hop

    vote = jnp.where(links[3] >= 0, jnp.where(links[3] > code, 1.0, -1.0), 0.0)
    vote = vote - jnp.where(links[2] >= 0, jnp.where(links[2] > code, 1.0, -1.0), 0.0)
    up = jnp.sum(vote, axis=0, keepdims=True) >= 0

    def straight(other, own_if_up, own_if_down):
        there, _, place, apart, hop = where_is(other)
        index = jnp.where(
            apart < 0,
            (hop + FAR) * PACK,
            jnp.where(apart > 0, OWN_DOWN + hop * PACK, jnp.where(up, own_if_up, own_if_down)),
        )
        return jnp.where(there, index + place, float(EMPTY))

    south = straight(links[2], float(OWN_UP), float(OWN_DOWN))
    north = straight(links[3], float(OWN_DOWN), float(OWN_UP))
    there, _, place, apart, hop = where_is(links[4])
    folded_up = jnp.where(
        apart < 0, (hop + FAR) * PACK, jnp.where(hop > 0, EXTRA + (hop - 1) * PACK, float(OWN_UP))
    )
    folded_down = jnp.where(
        apart > 0, OWN_DOWN + hop * PACK, jnp.where(hop < 0, EXTRA + (-hop - 1) * PACK, float(OWN_DOWN))
    )
    folded = jnp.where(up, folded_up, folded_down) + place
    north = jnp.where(there, folded, north)
    sides = []
    columns = {"earlier": 0.0, "later": 0.0, "send_later": 0.0, "send_earlier": 0.0, "next": 0.0, "previous": 0.0}
    for side in range(2):
        other = links[side]
        there, source, place, apart, hop = where_is(other)
        linked = other >= 0
        after = linked & (slot == own_count - 1.0) & (other == device * SLOTS + SLOTS)
        before = linked & (slot == 0) & (apart == -1) & (place + 1.0 == before_count)
        earlier = linked & (apart < 0) & ~before
        later = linked & (apart > 0) & ~after
        mine = slot * 2.0 + (side + 1.0)
        columns["earlier"] += jnp.where(earlier & there, (hop + FAR) * PACK + SLOTS - EMPTY, 0.0)
        columns["later"] += jnp.where(later & there, OWN_DOWN + hop * PACK + SLOTS - EMPTY, 0.0)
        columns["send_later"] += jnp.where(later, mine, 0.0)
        columns["send_earlier"] += jnp.where(earlier, mine, 0.0)
        columns["next"] += jnp.where(after, mine, 0.0)
        columns["previous"] += jnp.where(before, mine, 0.0)
        index = jnp.where(linked & (apart == 0), place * 2.0 + (1.0 - side), 24.0)
        index = jnp.where(before, 20.0, jnp.where(after, 21.0, index))
        index = jnp.where(earlier, 22.0, jnp.where(later, 23.0, index))
        sides.append(index)
    columns.update(
        south=south, north=north, west=sides[0], east=sides[1], live=live,
        fold=jnp.where(links[4] >= 0, 1.0, 0.0), up=jnp.where(up, 1.0, 0.0),
    )
    lane = lax.broadcasted_iota(jnp.int32, (rows, LANES), 1)
    result = jnp.zeros((rows, LANES), jnp.float32)
    for name, at in AT.items():
        result = jnp.where(lane == at, columns[name], result)
    out_ref[...] = result.astype(jnp.int32)


def link_table(block_owner, neighbours, fold_partner):
    return pl.pallas_call(
        table_kernel,
        out_shape=jax.ShapeDtypeStruct((GROUP * SLOTS, LANES), jnp.int32),
        compiler_params=pltpu.CompilerParams(vmem_limit_bytes=20 << 20),
        name="table",
    )(block_owner[None], neighbours.T, fold_partner[None])


def own_row(table_ref, slot, name):
    return table_ref[HALF * SLOTS + slot, AT[name]]


def load4(ref, half, t):
    if t < TILES - 1:
        return ref[half, :, lanes_at(t)]
    width = CELLS - t * LANES
    return jnp.pad(ref[half, :, pl.ds(t * LANES, width)], ((0, 0), (0, LANES - width)))


def load_rows(ref, t):
    if t < TILES - 1:
        return ref[:, lanes_at(t)]
    width = CELLS - t * LANES
    return jnp.pad(ref[:, pl.ds(t * LANES, width)], ((0, 0), (0, LANES - width)))


def line(tiles, start, lane):
    first = start // LANES
    r = start % LANES
    if r == 0:
        return tiles(first)
    amount = LANES - r
    return jnp.where(lane < amount, pltpu.roll(tiles(first), amount, 1), pltpu.roll(tiles(first + 1), amount, 1))


ROW_STARTS = (0, IB, (JB - 1) * IB, (JB - 2) * IB)


def pack_kernel(table_ref, tracers_ref, velocity_ref, kmt_ref, up_ref, down_ref, next_ref, sides_ref, depth_rows):
    pair = pl.program_id(0)
    sub, lane = iotas()
    column = lane % SIDE
    base_near = column * IB + jnp.where(lane >= SIDE, IB - 1, 0)
    base_far = column * IB + jnp.where(lane >= SIDE, IB - 2, 1)
    near_tile, near_at = base_near // LANES, base_near % LANES
    far_tile, far_at = base_far // LANES, base_far % LANES

    @pl.when(pair == 0)
    def _():
        lane10 = lane[0:1]
        near = jnp.zeros((16, LANES), jnp.float32)
        index16 = jnp.concatenate([near_at, near_at], axis=0)
        tile16 = jnp.concatenate([near_tile, near_tile], axis=0)

        def padded(t):
            return jnp.pad(load_rows(kmt_ref, t), ((0, 6), (0, 0)))

        for t in range(TILES):
            near = jnp.where(tile16 == t, take(padded(t), index16), near)
        south = padded(0)
        north = line(padded, (JB - 1) * IB, lane10)
        for q in range(SLOTS):
            depth_rows[0, q] = row(south, q)
            depth_rows[1, q] = row(north, q)
            depth_rows[2, q] = row(near, q)

    flag = own_row(table_ref, 0, "up") > 0
    aux_at = lane
    for s in range(8):
        move = {6: 28, 7: 14}.get(s, 90 if s % 2 == 0 else 52)
        aux_at = jnp.where((sub == s) & (lane >= IB), lane - move, aux_at)
    lane4 = lane[0:4]
    for half in range(2):
        q = 2 * pair + half

        def tracer(t):
            return load4(tracers_ref, half, t)

        def speed(t):
            return load4(velocity_ref, half, t)

        packets = []
        for kind, (near, far) in enumerate(((0, 1), (JB - 1, JB - 2))):
            body = jnp.concatenate([line(tracer, near * IB, lane4), line(tracer, far * IB, lane4)], axis=0)
            v = line(speed, near * IB, lane4)
            v0, v1 = row(v, 2), row(v, 3)
            joint = jnp.where(lane >= 76, v0, pltpu.roll(v1, LANES - 14, 1))
            aux = jnp.where(sub == 6, joint, depth_rows[kind, q])
            aux = jnp.where(sub < 2, v0, jnp.where(sub < 4, v1, aux))
            packets.append(jnp.where(lane < IB, body, take(aux, aux_at)))
        up_ref[q] = jnp.where(flag, packets[1], packets[0])
        down_ref[q] = jnp.where(flag, packets[0], packets[1])

    near = far = drift = jnp.zeros((8, LANES), jnp.float32)
    for t in range(TILES):
        x = jnp.concatenate([load4(tracers_ref, 0, t), load4(tracers_ref, 1, t)], axis=0)
        v = jnp.concatenate([load4(velocity_ref, 0, t), load4(velocity_ref, 1, t)], axis=0)
        near = jnp.where(near_tile == t, take(x, near_at), near)
        far = jnp.where(far_tile == t, take(x, far_at), far)
        drift = jnp.where(near_tile == t, take(v, near_at), drift)
    for half in range(2):
        q = 2 * pair + half
        if half == 0:
            body = jnp.where(sub < 4, near, pltpu.roll(far, 4, 0))
            aux = drift
        else:
            body = jnp.where(sub < 4, pltpu.roll(near, 4, 0), far)
            aux = pltpu.roll(drift, 4, 0)
        aux = jnp.where(sub == 2, depth_rows[2, q], aux)
        sides_ref[2 * q] = jnp.where(lane < SIDE, body, pltpu.roll(aux, SIDE, 1))
        sides_ref[2 * q + 1] = jnp.where(lane < SIDE, pltpu.roll(body, SIDE, 1), aux)

    @pl.when(pair == PAIRS - 1)
    def _():
        sides_ref[2 * SLOTS] = jnp.zeros((8, LANES), jnp.float32)

        def chosen(name):
            value = own_row(table_ref, 0, name)
            for q in range(1, SLOTS):
                value = value + own_row(table_ref, q, name)
            return sides_ref[jnp.where(value > 0, value - 1, 2 * SLOTS)]

        up_ref[SLOTS] = chosen("send_later")
        down_ref[SLOTS] = chosen("send_earlier")
        next_ref[0] = chosen("next")
        next_ref[1] = chosen("previous")


def packet_shape(*lead):
    return jax.ShapeDtypeStruct(lead + (8, LANES), jnp.float32)


def edge_packs(table, tracers, velocity, kmt):
    field = pl.BlockSpec((2, 4, CELLS), lambda p: (p, 0, 0))

    def whole(count):
        return pl.BlockSpec((count, 8, LANES), lambda p: (0, 0, 0))

    return pl.pallas_call(
        pack_kernel,
        grid=(PAIRS,),
        out_shape=[packet_shape(PACK), packet_shape(PACK), packet_shape(2), packet_shape(2 * SLOTS + 1)],
        in_specs=[
            pl.BlockSpec(memory_space=pltpu.SMEM),
            field,
            field,
            pl.BlockSpec((SLOTS, CELLS), lambda p: (0, 0)),
        ],
        out_specs=[whole(PACK), whole(PACK), whole(2), whole(2 * SLOTS + 1)],
        scratch_shapes=[pltpu.VMEM((3, SLOTS, 8, LANES), jnp.float32)],
        compiler_params=pltpu.CompilerParams(vmem_limit_bytes=20 << 20),
        name="pack",
    )(table, tracers, velocity, kmt)


def choose_kernel(table_ref, window_ref, out_ref):
    for c in range(GROUP):
        earlier = later = EMPTY
        for q in range(SLOTS):
            r = c * SLOTS + q
            out_ref[c, q] = window_ref[table_ref[r, AT["south"]]]
            out_ref[c, SLOTS + q] = window_ref[table_ref[r, AT["north"]]]
            earlier = earlier + table_ref[r, AT["earlier"]]
            later = later + table_ref[r, AT["later"]]
        out_ref[c, 2 * SLOTS] = window_ref[earlier]
        out_ref[c, 2 * SLOTS + 1] = window_ref[later]


def choose(table, window):
    vmem = pl.BlockSpec(memory_space=pltpu.VMEM)
    return pl.pallas_call(
        choose_kernel,
        out_shape=packet_shape(GROUP, WANT),
        in_specs=[pl.BlockSpec(memory_space=pltpu.SMEM), vmem],
        out_specs=vmem,
        compiler_params=pltpu.CompilerParams(vmem_limit_bytes=20 << 20),
        name="choose",
    )(table, window)


def coordinates(index):
    index = lax.rem(index + DEVICES, DEVICES)
    return (index // 4, lax.rem(index, 4))


def greet(offsets, me):
    barrier = pltpu.get_barrier_semaphore()
    for offset in offsets:
        pl.semaphore_signal(barrier, inc=1, device_id=coordinates(me + offset), device_id_type=MESH)
    pl.semaphore_wait(barrier, len(offsets))


FAR_SENDS = (
    [("up", GROUP * k, (FAR - k) * PACK) for k in range(1, FAR + 1)]
    + [("down", -GROUP * k, OWN_DOWN + k * PACK) for k in range(1, FAR + 1)]
    + [("next", 1, 0), ("next", -1, 1)]
)


def far_kernel(up_ref, down_ref, next_ref, window_ref, beside_ref, send_sem, recv_sem, extra_send, extra_recv):
    me = position()
    greet([offset for _, offset, _ in FAR_SENDS], me)
    copies = []
    for number, (kind, offset, place) in enumerate(FAR_SENDS):
        if kind == "next":
            source, target = next_ref.at[place], beside_ref.at[place]
        else:
            source = up_ref if kind == "up" else down_ref
            target = window_ref.at[pl.ds(place, PACK)]
        copy = pltpu.make_async_remote_copy(
            src_ref=source,
            dst_ref=target,
            send_sem=send_sem.at[number],
            recv_sem=recv_sem.at[number],
            device_id=coordinates(me + offset),
            device_id_type=MESH,
        )
        copy.start()
        copies.append(copy)

    def fold_copy(k, downwards):
        return pltpu.make_async_remote_copy(
            src_ref=up_ref if downwards else down_ref,
            dst_ref=window_ref.at[pl.ds(EXTRA + (k - 1) * PACK, PACK)],
            send_sem=extra_send.at[k - 1],
            recv_sem=extra_recv.at[k - 1],
            device_id=coordinates(me - GROUP * k if downwards else me + GROUP * k),
            device_id_type=MESH,
        )

    high, low = DEVICES - FOLD_REACH, FOLD_REACH
    for k in (1, 2):
        @pl.when(me >= high)
        def _():
            fold_copy(k, True).start()

        @pl.when(me < low)
        def _():
            fold_copy(k, False).start()

    window_ref[pl.ds(OWN_UP, PACK)] = up_ref[...]
    window_ref[pl.ds(OWN_DOWN, PACK)] = down_ref[...]
    window_ref[pl.ds(EMPTY, 2)] = jnp.zeros((2, 8, LANES), jnp.float32)
    for copy in copies:
        copy.wait()
    for k in (1, 2):
        @pl.when(me >= high)
        def _():
            fold_copy(k, True).wait_send()

        @pl.when(me < low)
        def _():
            fold_copy(k, False).wait_send()

        @pl.when((me + GROUP * k >= high) & (me + GROUP * k < DEVICES))
        def _():
            fold_copy(k, True).wait_recv()

        @pl.when((me - GROUP * k >= 0) & (me - GROUP * k < low))
        def _():
            fold_copy(k, False).wait_recv()


def far_exchange(up, down, beside):
    vmem = pl.BlockSpec(memory_space=pltpu.VMEM)
    return pl.pallas_call(
        far_kernel,
        out_shape=[packet_shape(WINDOW), packet_shape(2)],
        in_specs=[vmem] * 3,
        out_specs=[vmem] * 2,
        scratch_shapes=[
            pltpu.SemaphoreType.DMA((len(FAR_SENDS),)),
            pltpu.SemaphoreType.DMA((len(FAR_SENDS),)),
            pltpu.SemaphoreType.DMA((2,)),
            pltpu.SemaphoreType.DMA((2,)),
        ],
        compiler_params=pltpu.CompilerParams(
            collective_id=0, has_side_effects=True, vmem_limit_bytes=20 << 20
        ),
        name="far",
    )(up, down, beside)


def near_kernel(message_ref, out_ref, send_sem, recv_sem):
    me = position()
    greet([c for c in range(-HALF, HALF + 1) if c != 0], me)
    copies = []
    for c in range(-HALF, HALF):
        if c == 0:
            continue
        copy = pltpu.make_async_remote_copy(
            src_ref=message_ref.at[c + HALF],
            dst_ref=out_ref.at[c + HALF],
            send_sem=send_sem.at[c + HALF],
            recv_sem=recv_sem.at[c + HALF],
            device_id=coordinates(me + c),
            device_id_type=MESH,
        )
        copy.start()
        copies.append(copy)
    out_ref[HALF] = message_ref[HALF]
    for copy in copies:
        copy.wait()


def near_exchange(messages):
    vmem = pl.BlockSpec(memory_space=pltpu.VMEM)
    return pl.pallas_call(
        near_kernel,
        out_shape=packet_shape(GROUP, WANT),
        in_specs=[vmem],
        out_specs=vmem,
        scratch_shapes=[pltpu.SemaphoreType.DMA((GROUP,)), pltpu.SemaphoreType.DMA((GROUP,))],
        compiler_params=pltpu.CompilerParams(
            collective_id=1, has_side_effects=True, vmem_limit_bytes=20 << 20
        ),
        name="near",
    )(messages)


def finish_kernel(table_ref, tracers_ref, velocity_ref, kappa_ref, kmt_ref, arrived_ref, sides_ref, beside_ref, out_ref,
                  halo, around, place, spot, xs, us, vs, all_ds, all_ks):
    pair = pl.program_id(0)
    sub, lane = iotas()
    upper = sub < 4

    def spread(ref, p, t):
        width = min(LANES, CELLS - t * LANES)
        value = ref[2 * p : 2 * p + 2, pl.ds(t * LANES, width)]
        if width < LANES:
            value = jnp.pad(value, ((0, 0), (0, LANES - width)))
        return jnp.where(
            sub < 4, jnp.broadcast_to(value[0:1], (8, LANES)), jnp.broadcast_to(value[1:2], (8, LANES))
        )

    @pl.when(pair == 0)
    def _():
        for number in range(WANT):
            total = arrived_ref[0, number]
            for source in range(1, GROUP):
                total = total + arrived_ref[source, number]
            halo[number] = total
        for number in range(2 * SLOTS):
            around[number] = sides_ref[number]
        around[2 * SLOTS] = beside_ref[0]
        around[2 * SLOTS + 1] = beside_ref[1]
        around[2 * SLOTS + 2] = halo[2 * SLOTS]
        around[2 * SLOTS + 3] = halo[2 * SLOTS + 1]
        around[2 * SLOTS + 4] = jnp.zeros((8, LANES), jnp.float32)
        for t in range(TILES):
            flat = lane + t * LANES
            j = ((flat.astype(jnp.float32) + 0.5) * (1.0 / IB)).astype(jnp.int32)
            i = flat - j * IB
            place[:, lanes_at(t)] = i
            spot[:, lanes_at(t)] = j + jnp.where(i >= IB // 2, SIDE, 0)
            for p in range(PAIRS):
                all_ds[p, :, lanes_at(t + 2)] = spread(kmt_ref, p, t)
                all_ks[p, :, lanes_at(t)] = spread(kappa_ref, p, t)

    ds, ks = all_ds.at[pair], all_ks.at[pair]
    lower_half = sub % 4 < 2
    for t in range(TILES):
        xs[:, lanes_at(t + 2)] = jnp.concatenate([load4(tracers_ref, 0, t), load4(tracers_ref, 1, t)], axis=0)
        speed = jnp.concatenate([load4(velocity_ref, 0, t), load4(velocity_ref, 1, t)], axis=0)
        us[:, lanes_at(t + 2)] = jnp.where(lower_half, speed, pltpu.roll(speed, 2, 0))
        vs[:, lanes_at(t + 2)] = jnp.where(lower_half, pltpu.roll(speed, 6, 0), speed)

    def frame(ref, south_near, south_far, north_near, north_far):
        if south_far is not None:
            ref[:, lanes_at(0)] = pltpu.roll(south_far, 76, 1)
            ref[:, lanes_at(1)] = jnp.where(lane < 38, pltpu.roll(south_far, 76, 1), pltpu.roll(south_near, 38, 1))
            far = pltpu.roll(north_far, 114, 1)
            ref[:, lanes_at(45)] = far
        else:
            ref[:, lanes_at(1)] = pltpu.roll(south_near, 38, 1)
            far = pltpu.roll(north_near, 24, 1)
        tail = ref[:, lanes_at(44)]
        ref[:, lanes_at(44)] = jnp.where(lane < 24, tail, jnp.where(lane < 114, pltpu.roll(north_near, 24, 1), far))

    odd = sub % 2 == 1

    def paired(first, second):
        return jnp.where(upper, first, second)

    def across(first, second):
        near = jnp.where(upper, first, pltpu.roll(second, 4, 0))
        return near, jnp.where(upper, pltpu.roll(first, 4, 0), second)

    def unpack(packet):
        a, b = pltpu.roll(packet, 38, 1), pltpu.roll(packet, 76, 1)
        c, d = pltpu.roll(packet, 100, 1), pltpu.roll(packet, 114, 1)

        def joined(first, second, third):
            return jnp.where(lane < 38, first, jnp.where(lane < 76, second, third))

        speed = jnp.where(odd, joined(row(a, 2), row(b, 3), row(d, 6)), joined(row(a, 0), row(b, 1), row(c, 6)))
        return speed, joined(row(a, 4), row(b, 5), row(d, 7))

    def rows_from(first, second):
        near, far = across(first, second)
        (speed_a, depth_a), (speed_b, depth_b) = unpack(first), unpack(second)
        return near, far, paired(speed_a, speed_b), paired(depth_a, depth_b)

    slots = (2 * pair, 2 * pair + 1)
    south = rows_from(halo[slots[0]], halo[slots[1]])
    north = rows_from(halo[SLOTS + slots[0]], halo[SLOTS + slots[1]])
    folded = paired(*(own_row(table_ref, q, "fold") for q in slots)) > 0
    back = jnp.where(lane < IB, IB - 1 - lane, lane)
    north = [
        jnp.where(folded, sign * take(value, back), value) for value, sign in zip(north, (1.0, 1.0, -1.0, 1.0))
    ]
    frame(xs, south[0], south[1], north[0], north[1])
    frame(vs, south[2], None, north[2], None)
    frame(ds, south[3], None, north[3], None)
    bodies, speeds, depths = [], [], []
    for q in slots:
        west, east = (around[own_row(table_ref, q, name)] for name in ("west", "east"))
        bodies.append(jnp.where(lane < SIDE, west, pltpu.roll(east, SIDE, 1)))
        aux = jnp.where(lane < SIDE, pltpu.roll(west, SIDE, 1), east)
        speeds.append(jnp.where(odd, row(aux, 1), row(aux, 0)))
        depths.append(row(aux, 2))
    side_near, side_far = across(*bodies)
    side_speed, side_depth = paired(*speeds), paired(*depths)
    level = (sub % 2).astype(jnp.float32)
    keep = paired(*(own_row(table_ref, q, "live") for q in slots)) > 0
    turned = {}

    def tile_of(ref, tile):
        key = (id(ref), tile, 0)
        if key not in turned:
            turned[key] = ref[:, lanes_at(tile)]
        return turned[key]

    def turn(ref, tile, r):
        key = (id(ref), tile, r)
        if key not in turned:
            turned[key] = pltpu.roll(tile_of(ref, tile), LANES - r, 1)
        return turned[key]

    def shift(ref, t, s):
        tile = t + 2 + s // LANES
        r = s % LANES
        return jnp.where(lane < LANES - r, turn(ref, tile, r), turn(ref, tile + 1, r))

    def flux(w, far_a, a, b, far_b):
        return jnp.maximum(w, 0.0) * (5.0 * a + 2.0 * b - far_a) + jnp.minimum(w, 0.0) * (2.0 * a + 5.0 * b - far_b)

    def wetness(d):
        return jnp.clip(d - level, 0.0, 1.0)

    def swap(z):
        return jnp.where(odd, pltpu.roll(z, 1, 0), pltpu.roll(z, 7, 0))

    for t in range(TILES):
        for key in [k for k in turned if k[1] < t]:
            del turned[key]
        i, index = place[:, lanes_at(t)], spot[:, lanes_at(t)]
        first, last = i == 0, i == IB - 1
        near, far = take(side_near, index), take(side_far, index)
        x = tile_of(xs, t + 2)
        west = jnp.where(first, near, shift(xs, t, -1))
        west_far = jnp.where(first, far, jnp.where(i == 1, near, shift(xs, t, -2)))
        east = jnp.where(last, near, shift(xs, t, 1))
        east_far = jnp.where(last, far, jnp.where(i == IB - 2, near, shift(xs, t, 2)))
        u = tile_of(us, t + 2)
        side_u = take(side_speed, index)
        u_west = jnp.where(first, side_u, shift(us, t, -1))
        u_east = jnp.where(last, side_u, shift(us, t, 1))
        wet = wetness(tile_of(ds, t + 2))
        side_d = take(side_depth, index)
        wet_west = wetness(jnp.where(first, side_d, shift(ds, t, -1)))
        wet_east = wetness(jnp.where(last, side_d, shift(ds, t, 1)))
        wet_south = wetness(shift(ds, t, -IB))
        wet_north = wetness(shift(ds, t, IB))
        v = tile_of(vs, t + 2)
        x_south, x_south_far = shift(xs, t, -IB), shift(xs, t, -2 * IB)
        x_north, x_north_far = shift(xs, t, IB), shift(xs, t, 2 * IB)
        flux_east = flux((u + u_east) * (wet * wet_east), west, x, east, east_far)
        flux_west = flux((u_west + u) * (wet_west * wet), west_far, west, x, east)
        flux_north = flux((v + shift(vs, t, IB)) * (wet * wet_north), x_south, x, x_north, x_north_far)
        flux_south = flux((shift(vs, t, -IB) + v) * (wet_south * wet), x_south_far, x_south, x, x_north)
        divergence = flux_east - flux_west + (flux_north - flux_south)
        explicit = x - (wet * (COURANT / 12.0)) * divergence
        coupling = ks[:, lanes_at(t)] * wet * swap(wet)
        share = coupling / (1.0 + 2.0 * coupling)
        result = explicit + share * (swap(explicit) - explicit)
        result = jnp.where(keep, result, 0.0)
        width = min(LANES, CELLS - t * LANES)
        out_ref[0, :, pl.ds(t * LANES, width)] = result[0:4, :width]
        out_ref[1, :, pl.ds(t * LANES, width)] = result[4:8, :width]


def finish(table, tracers, velocity, kappa, kmt, arrived, sides, beside):
    field = pl.BlockSpec((2, 4, CELLS), lambda p: (p, 0, 0))
    column = pl.BlockSpec((SLOTS, CELLS), lambda p: (0, 0))

    def whole(*lead):
        return pl.BlockSpec(lead + (8, LANES), lambda p: (0,) * (len(lead) + 2))

    wide = pltpu.VMEM((8, FRAME * LANES), jnp.float32)
    return pl.pallas_call(
        finish_kernel,
        grid=(PAIRS,),
        out_shape=jax.ShapeDtypeStruct((SLOTS, 4, CELLS), jnp.float32),
        in_specs=[
            pl.BlockSpec(memory_space=pltpu.SMEM),
            field,
            field,
            column,
            column,
            whole(GROUP, WANT),
            whole(2 * SLOTS + 1),
            whole(2),
        ],
        out_specs=field,
        scratch_shapes=[
            pltpu.VMEM((WANT, 8, LANES), jnp.float32),
            pltpu.VMEM((2 * SLOTS + 5, 8, LANES), jnp.float32),
            pltpu.VMEM((8, TILES * LANES), jnp.int32),
            pltpu.VMEM((8, TILES * LANES), jnp.int32),
            wide,
            wide,
            wide,
            pltpu.VMEM((PAIRS, 8, FRAME * LANES), jnp.float32),
            pltpu.VMEM((PAIRS, 8, TILES * LANES), jnp.float32),
        ],
        compiler_params=pltpu.CompilerParams(vmem_limit_bytes=40 << 20),
        name="advance",
    )(table, tracers, velocity, kappa, kmt, arrived, sides, beside)


def per_device(tracers, velocity, kappa, kmt, block_owner, neighbours, fold_partner):
    table = link_table(block_owner, neighbours, fold_partner)
    up, down, beside, sides = edge_packs(table, tracers, velocity, kmt)
    window, beside = far_exchange(up, down, beside)
    arrived = near_exchange(choose(table, window))
    return finish(table, tracers, velocity, kappa, kmt, arrived, sides, beside)


def solution(mesh):
    placed = (
        P(("blk", "sub"), None, None),
        P(("blk", "sub"), None, None),
        P(("blk", "sub"), None),
        P(("blk", "sub"), None),
        P(),
        P(),
        P(),
    )
    return jax.shard_map(
        per_device,
        mesh=mesh,
        in_specs=placed,
        out_specs=P(("blk", "sub"), None, None),
        check_vma=False,
    )
```

```python
import jax
import jax.numpy as jnp
from jax import lax
from jax.experimental import pallas as pl
from jax.experimental.pallas import tpu as pltpu
from jax.sharding import PartitionSpec as P

IB = 90
JB = 60
CELLS = IB * JB
SLOTS = 10
PAIRS = SLOTS // 2
DEVICES = 256
COURANT = 0.2
STRIDE = 4
HOPS = 7
LANES = 128
TILES = 43
FRAME = 47
SIDE = 64
PACK = SLOTS + 1
OWN_DOWN = HOPS * PACK
EXTRA = OWN_DOWN + STRIDE * PACK
EXTRAS = 3
EMPTY = EXTRA + EXTRAS * PACK
WINDOW = EMPTY + 1
WANT = 2 * SLOTS + 2
TARGETS = STRIDE + HOPS
TABLE_ROWS = 112
EARLY = 2
BIG = 63 << 20
FOLD_REACH = 14
MESH = pl.DeviceIdType.MESH
COLUMNS = ("behind", "ahead", "extra", "earlier", "later", "west", "east", "send_later", "send_earlier", "next", "previous", "fold", "live", "up")
AT = {name: number for number, name in enumerate(COLUMNS)}


def position():
    return lax.axis_index("blk") * 4 + lax.axis_index("sub")


def lanes_at(tile):
    return pl.ds(tile * LANES, LANES)


def iotas():
    return (
        lax.broadcasted_iota(jnp.int32, (8, LANES), 0),
        lax.broadcasted_iota(jnp.int32, (8, LANES), 1),
    )


def take(packed, index):
    return jnp.take_along_axis(packed, index, axis=1, mode="promise_in_bounds")


def row(value, number):
    return jnp.broadcast_to(value[number : number + 1], (8, LANES))


def table_of(owner_ref, near_ref, fold_ref):
    me = position()
    rows = TABLE_ROWS
    strips = owner_ref.shape[0]
    number = lax.broadcasted_iota(jnp.int32, (rows, 1), 0).astype(jnp.float32)
    which = jnp.floor((number + 0.5) * (1.0 / SLOTS))
    slot = number - which * SLOTS
    onward = which < STRIDE
    hops = jnp.where(onward, which, which - STRIDE)
    device = jnp.where(onward, hops, -STRIDE * hops) + jnp.float32(1) * me
    device = jnp.where(device < 0, device + DEVICES, device)
    device = jnp.where(device >= DEVICES, device - DEVICES, device)
    code = device * SLOTS + slot
    wide = lax.broadcasted_iota(jnp.int32, (1, LANES), 1).astype(jnp.float32)

    def total(pieces):
        acc = jnp.zeros((rows, LANES), jnp.float32)
        for mask, value in pieces:
            acc = acc + jnp.where(mask, value, 0.0)
        return jnp.sum(acc, axis=1, keepdims=True)

    owners = [owner_ref[t : t + 1, :].astype(jnp.float32) for t in range(strips)]
    hits = [owner == code for owner in owners]
    first = device * SLOTS
    own_count = total([((owner >= first) & (owner < first + SLOTS), 1.0) for owner in owners])
    before_count = total([((owner >= first - SLOTS) & (owner < first), 1.0) for owner in owners])
    live = total([(hit, 1.0) for hit in hits])
    links = []
    for k in range(5):
        if k < 4:
            link = [near_ref[k : k + 1, lanes_at(t)].astype(jnp.float32) for t in range(strips)]
        else:
            link = [fold_ref[t : t + 1, :].astype(jnp.float32) for t in range(strips)]
        block = total([(hit, piece + 1.0) for hit, piece in zip(hits, link)]) - 1.0
        links.append(total([(block == wide + t * LANES, owner + 1.0) for t, owner in enumerate(owners)]) - 1.0)

    def where_is(other):
        source = jnp.floor((other + 0.5) * (1.0 / SLOTS))
        apart = source - device
        distance = jnp.abs(apart)
        far = jnp.floor((distance + 0.5) * (1.0 / STRIDE))
        rest = distance - far * STRIDE
        from_behind = (other >= 0) & (apart <= 0) & onward & (rest == hops)
        from_ahead = (other >= 0) & (apart >= 0) & ~onward & (far == hops)
        return source, other - source * SLOTS, apart, far, rest, from_behind, from_ahead

    vote = jnp.where(links[3] >= 0, jnp.where(links[3] > code, 1.0, -1.0), 0.0)
    vote = vote - jnp.where(links[2] >= 0, jnp.where(links[2] > code, 1.0, -1.0), 0.0)
    up = jnp.sum(vote, axis=0, keepdims=True) >= 0
    empty = float(EMPTY)
    _, place, _, far, _, from_behind, _ = where_is(jnp.where(up, links[2], links[3]))
    behind = jnp.where(from_behind, far * PACK + place, empty)
    _, place, _, _, rest, _, from_ahead = where_is(jnp.where(up, links[3], links[2]))
    ahead = jnp.where(from_ahead, OWN_DOWN + rest * PACK + place, empty)
    _, place, apart, far, rest, from_behind, from_ahead = where_is(links[4])
    against = jnp.where(rest > 0, EXTRA + (rest - 1.0) * PACK, 0.0) + place
    ahead = jnp.where(up & from_ahead, against, ahead)
    against = jnp.where(far > 0, EXTRA + (far - 1.0) * PACK, float(OWN_DOWN)) + place
    behind = jnp.where(~up & from_behind, against, behind)
    extra = jnp.where(up & from_behind & (apart < 0), far * PACK + place, empty)
    extra = jnp.where(~up & from_ahead & (apart > 0), OWN_DOWN + rest * PACK + place, extra)
    sides = []
    columns = {"earlier": 0.0, "later": 0.0, "send_later": 0.0, "send_earlier": 0.0, "next": 0.0, "previous": 0.0}
    for side in range(2):
        other = links[side]
        source, place, apart, far, rest, from_behind, from_ahead = where_is(other)
        linked = other >= 0
        after = linked & (slot == own_count - 1.0) & (other == device * SLOTS + SLOTS)
        before = linked & (slot == 0) & (apart == -1) & (place + 1.0 == before_count)
        earlier = linked & (apart < 0) & ~before
        later = linked & (apart > 0) & ~after
        mine = slot * 2.0 + (side + 1.0)
        columns["earlier"] += jnp.where(earlier & from_behind, far * PACK + SLOTS - EMPTY, 0.0)
        columns["later"] += jnp.where(later & from_ahead, OWN_DOWN + rest * PACK + SLOTS - EMPTY, 0.0)
        columns["send_later"] += jnp.where(later, mine, 0.0)
        columns["send_earlier"] += jnp.where(earlier, mine, 0.0)
        columns["next"] += jnp.where(after, mine, 0.0)
        columns["previous"] += jnp.where(before, mine, 0.0)
        index = jnp.where(linked & (apart == 0), place * 2.0 + (1.0 - side), 24.0)
        index = jnp.where(before, 20.0, jnp.where(after, 21.0, index))
        index = jnp.where(earlier, 22.0, jnp.where(later, 23.0, index))
        sides.append(index)
    columns.update(
        behind=behind, ahead=ahead, extra=extra, west=sides[0], east=sides[1], live=live,
        fold=jnp.where(links[4] >= 0, 1.0, 0.0), up=jnp.where(up, 1.0, 0.0),
    )
    lane = lax.broadcasted_iota(jnp.int32, (rows, LANES), 1)
    result = jnp.zeros((rows, LANES), jnp.float32)
    for name, at in AT.items():
        result = jnp.where(lane == at, columns[name], result)
    own = number < SLOTS
    chosen = {
        name: jnp.sum(jnp.where(own, columns[name], 0.0), axis=0, keepdims=True)
        for name in ("send_later", "send_earlier", "next", "previous")
    }
    return result.astype(jnp.int32), up, chosen


def own_row(table_ref, slot, name):
    return table_ref[slot, AT[name]]


def load4(ref, half, t):
    if t < TILES - 1:
        return ref[half, :, lanes_at(t)]
    width = CELLS - t * LANES
    return jnp.pad(ref[half, :, pl.ds(t * LANES, width)], ((0, 0), (0, LANES - width)))


def load_rows(ref, t):
    if t < TILES - 1:
        return ref[:, lanes_at(t)]
    width = CELLS - t * LANES
    return jnp.pad(ref[:, pl.ds(t * LANES, width)], ((0, 0), (0, LANES - width)))


def line(tiles, start, lane):
    first = start // LANES
    r = start % LANES
    if r == 0:
        return tiles(first)
    amount = LANES - r
    return jnp.where(lane < amount, pltpu.roll(tiles(first), amount, 1), pltpu.roll(tiles(first + 1), amount, 1))


ROW_STARTS = (0, IB, (JB - 1) * IB, (JB - 2) * IB)


def front_kernel(owner_hbm, near_hbm, fold_hbm, tracers_hbm, velocity_hbm, kmt_hbm, table_ref, up_ref, down_ref, next_ref,
                 sides_ref, tracers_all, velocity_all, kmt_ref, depth_rows, sems,
                 owner_ref, near_ref, fold_ref, list_sems):
    lists = [
        pltpu.make_async_copy(source, target, list_sems.at[number])
        for number, (source, target) in enumerate(
            ((owner_hbm, owner_ref), (near_hbm, near_ref), (fold_hbm, fold_ref))
        )
    ]
    for copy in lists:
        copy.start()

    def fetch(pair):
        part = pl.ds(2 * pair, 2)
        return (
            pltpu.make_async_copy(tracers_hbm.at[part], tracers_all.at[part], sems.at[0, pair]),
            pltpu.make_async_copy(velocity_hbm.at[part], velocity_all.at[part], sems.at[1, pair]),
        )

    kmt_copy = pltpu.make_async_copy(kmt_hbm, kmt_ref, sems.at[0, PAIRS])
    kmt_copy.start()
    for pair in range(PAIRS):
        for copy in fetch(pair):
            copy.start()
    for copy in lists:
        copy.wait()
    table, up, chosen = table_of(owner_ref, near_ref, fold_ref)
    table_ref[...] = table
    sub, lane = iotas()
    flag = jnp.broadcast_to(up, (8, LANES))
    column = lane % SIDE
    base_near = column * IB + jnp.where(lane >= SIDE, IB - 1, 0)
    base_far = column * IB + jnp.where(lane >= SIDE, IB - 2, 1)
    near_tile, near_at = base_near // LANES, base_near % LANES
    far_tile, far_at = base_far // LANES, base_far % LANES
    kmt_copy.wait()
    near = jnp.zeros((16, LANES), jnp.float32)
    index16 = jnp.concatenate([near_at, near_at], axis=0)
    tile16 = jnp.concatenate([near_tile, near_tile], axis=0)

    def padded(t):
        return jnp.pad(load_rows(kmt_ref, t), ((0, 6), (0, 0)))

    for t in range(TILES):
        near = jnp.where(tile16 == t, take(padded(t), index16), near)
    south = padded(0)
    north = line(padded, (JB - 1) * IB, lane[0:1])
    for q in range(SLOTS):
        depth_rows[0, q] = row(south, q)
        depth_rows[1, q] = row(north, q)
        depth_rows[2, q] = row(near, q)
    aux_at = lane
    for s in range(8):
        move = {6: 28, 7: 14}.get(s, 90 if s % 2 == 0 else 52)
        aux_at = jnp.where((sub == s) & (lane >= IB), lane - move, aux_at)
    lane4 = lane[0:4]

    def one_pair(pair, carry):
        for copy in fetch(pair):
            copy.wait()
        tracers_ref, velocity_ref = tracers_all.at[pl.ds(2 * pair, 2)], velocity_all.at[pl.ds(2 * pair, 2)]
        for half in range(2):
            q = 2 * pair + half

            def tracer(t):
                return load4(tracers_ref, half, t)

            def speed(t):
                return load4(velocity_ref, half, t)

            packets = []
            for kind, (near, far) in enumerate(((0, 1), (JB - 1, JB - 2))):
                body = jnp.concatenate([line(tracer, near * IB, lane4), line(tracer, far * IB, lane4)], axis=0)
                v = line(speed, near * IB, lane4)
                v0, v1 = row(v, 2), row(v, 3)
                joint = jnp.where(lane >= 76, v0, pltpu.roll(v1, LANES - 14, 1))
                aux = jnp.where(sub == 6, joint, depth_rows[kind, q])
                aux = jnp.where(sub < 2, v0, jnp.where(sub < 4, v1, aux))
                packets.append(jnp.where(lane < IB, body, take(aux, aux_at)))
            up_ref[q] = jnp.where(flag, packets[1], packets[0])
            down_ref[q] = jnp.where(flag, packets[0], packets[1])
        near = far = drift = jnp.zeros((8, LANES), jnp.float32)
        for t in range(TILES):
            x = jnp.concatenate([load4(tracers_ref, 0, t), load4(tracers_ref, 1, t)], axis=0)
            v = jnp.concatenate([load4(velocity_ref, 0, t), load4(velocity_ref, 1, t)], axis=0)
            near = jnp.where(near_tile == t, take(x, near_at), near)
            far = jnp.where(far_tile == t, take(x, far_at), far)
            drift = jnp.where(near_tile == t, take(v, near_at), drift)
        for half in range(2):
            q = 2 * pair + half
            if half == 0:
                body = jnp.where(sub < 4, near, pltpu.roll(far, 4, 0))
                aux = drift
            else:
                body = jnp.where(sub < 4, pltpu.roll(near, 4, 0), far)
                aux = pltpu.roll(drift, 4, 0)
            aux = jnp.where(sub == 2, depth_rows[2, q], aux)
            sides_ref[2 * q] = jnp.where(lane < SIDE, body, pltpu.roll(aux, SIDE, 1))
            sides_ref[2 * q + 1] = jnp.where(lane < SIDE, pltpu.roll(body, SIDE, 1), aux)
        return carry

    lax.fori_loop(0, PAIRS, one_pair, 0)
    outputs = {"send_later": (up_ref, SLOTS), "send_earlier": (down_ref, SLOTS), "next": (next_ref, 0), "previous": (next_ref, 1)}
    for name, (ref, at) in outputs.items():
        which = jnp.broadcast_to(chosen[name], (8, LANES))
        packet = jnp.zeros((8, LANES), jnp.float32)
        for number in range(2 * SLOTS):
            packet = jnp.where(which == number + 1.0, sides_ref[number], packet)
        ref[at] = packet


def packet_shape(*lead):
    return jax.ShapeDtypeStruct(lead + (8, LANES), jnp.float32)


def front(block_owner, neighbours, fold_partner, tracers, velocity, kmt):
    vmem = pl.BlockSpec(memory_space=pltpu.VMEM)
    anywhere = pl.BlockSpec(memory_space=pltpu.HBM)
    return pl.pallas_call(
        front_kernel,
        out_shape=[
            jax.ShapeDtypeStruct((TABLE_ROWS, LANES), jnp.int32),
            packet_shape(PACK),
            packet_shape(PACK),
            packet_shape(2),
            packet_shape(2 * SLOTS),
        ],
        in_specs=[anywhere] * 6,
        out_specs=[vmem] * 5,
        scratch_shapes=[
            pltpu.VMEM((SLOTS, 4, CELLS), jnp.float32),
            pltpu.VMEM((SLOTS, 4, CELLS), jnp.float32),
            pltpu.VMEM((SLOTS, CELLS), jnp.float32),
            pltpu.VMEM((3, SLOTS, 8, LANES), jnp.float32),
            pltpu.SemaphoreType.DMA((2, PAIRS + 1)),
            pltpu.VMEM((SLOTS, LANES), jnp.int32),
            pltpu.VMEM((4, SLOTS * LANES), jnp.int32),
            pltpu.VMEM((SLOTS, LANES), jnp.int32),
            pltpu.SemaphoreType.DMA((3,)),
        ],
        compiler_params=pltpu.CompilerParams(vmem_limit_bytes=BIG),
        name="front",
    )(block_owner.reshape(-1, LANES), neighbours.T, fold_partner.reshape(-1, LANES), tracers, velocity, kmt)


def coordinates(index):
    index = lax.rem(index + DEVICES, DEVICES)
    return (index // 4, lax.rem(index, 4))


PARTNERS = [sign * step for step in [1, 2, 3] + [STRIDE * a for a in range(1, HOPS)] for sign in (1, -1)]
HIGH, LOW = DEVICES - FOLD_REACH, FOLD_REACH


def exchange_kernel(table_ref, up_ref, down_ref, next_ref, tracers_hbm, velocity_hbm, kappa_hbm, kmt_hbm, halo_ref, beside_ref,
                    partial_ref, edges_ref, rows_ref, spot_ref, kind_ref, window, message, extra_message, arrived,
                    extra_arrived, send_sem, recv_sem, extra_send, extra_recv, later_send, later_recv, last_send, last_recv,
                    tracers_all, velocity_all, kappa_ref, kmt_ref, xs, us, vs, all_ds, all_ks, ws, gs, place_ref, load_sem):
    me = position()
    loads = [
        pltpu.make_async_copy(source, target, load_sem.at[number])
        for number, (source, target) in enumerate(
            ((kmt_hbm, kmt_ref), (kappa_hbm, kappa_ref), (tracers_hbm, tracers_all), (velocity_hbm, velocity_all))
        )
    ]
    for copy in loads:
        copy.start()
    barrier = pltpu.get_barrier_semaphore()
    for offset in PARTNERS:
        pl.semaphore_signal(barrier, inc=1, device_id=coordinates(me + offset), device_id_type=MESH)
    pl.semaphore_wait(barrier, len(PARTNERS))

    def remote(source, target, sends, recvs, number, offset):
        return pltpu.make_async_remote_copy(
            src_ref=source,
            dst_ref=target,
            send_sem=sends.at[number],
            recv_sem=recvs.at[number],
            device_id=coordinates(me + offset),
            device_id_type=MESH,
        )

    plan = []
    for a in range(HOPS - 1, 0, -1):
        plan.append((up_ref, window.at[pl.ds(a * PACK, PACK)], STRIDE * a))
        if a < STRIDE:
            plan.append((down_ref, window.at[pl.ds(OWN_DOWN + a * PACK, PACK)], -a))
    plan.append((next_ref.at[0], beside_ref.at[0], 1))
    plan.append((next_ref.at[1], beside_ref.at[1], -1))
    copies = [
        remote(source, target, send_sem, recv_sem, number, offset)
        for number, (source, target, offset) in enumerate(plan)
    ]
    for copy in copies:
        copy.start()

    def fold_copy(k, downwards):
        target = window.at[pl.ds(EXTRA + (k - 1) * PACK, PACK)]
        if downwards:
            return remote(up_ref, target, extra_send, extra_recv, k - 1, -k)
        return remote(down_ref, target, extra_send, extra_recv, k - 1, STRIDE * k)

    for k in range(1, EXTRAS + 1):
        @pl.when(me >= HIGH)
        def _():
            fold_copy(k, True).start()

        @pl.when(me < LOW)
        def _():
            fold_copy(k, False).start()

        from_high = (me + k >= HIGH) & (me + k < DEVICES)
        from_low = (me - STRIDE * k >= 0) & (me - STRIDE * k < LOW)

        @pl.when(jnp.logical_not(from_high | from_low))
        def _():
            window[pl.ds(EXTRA + (k - 1) * PACK, PACK)] = jnp.zeros((PACK, 8, LANES), jnp.float32)

    window[pl.ds(0, PACK)] = up_ref[...]
    window[pl.ds(OWN_DOWN, PACK)] = down_ref[...]
    window[EMPTY] = jnp.zeros((8, LANES), jnp.float32)
    loads[0].wait()
    loads[1].wait()
    prepare(kappa_ref, kmt_ref, xs, us, vs, all_ds, all_ks, place_ref, spot_ref, kind_ref)
    loads[2].wait()
    loads[3].wait()

    def one_pair(pair, carry):
        part = pl.ds(2 * pair, 2)
        interior(
            tracers_all.at[part], velocity_all.at[part], xs, us, vs, all_ds.at[pair], all_ks.at[pair], ws, gs,
            place_ref, partial_ref.at[pair], edges_ref.at[pair], rows_ref.at[pair],
        )
        return carry

    lax.fori_loop(0, EARLY, one_pair, 0)
    for copy in copies:
        copy.wait()
    for k in range(1, EXTRAS + 1):
        @pl.when(me >= HIGH)
        def _():
            fold_copy(k, True).wait_send()

        @pl.when(me < LOW)
        def _():
            fold_copy(k, False).wait_send()

        @pl.when((me + k >= HIGH) & (me + k < DEVICES))
        def _():
            fold_copy(k, True).wait_recv()

        @pl.when((me - STRIDE * k >= 0) & (me - STRIDE * k < LOW))
        def _():
            fold_copy(k, False).wait_recv()

    def fill(number, halo_name, wrap_name):
        wrap = EMPTY
        for q in range(SLOTS):
            r = number * SLOTS + q
            message[number, q] = window[table_ref[r, AT[halo_name]]]
            wrap = wrap + table_ref[r, AT[wrap_name]]
        message[number, SLOTS] = window[wrap]

    later = []
    for number in [STRIDE + a for a in range(HOPS - 1, 0, -1)] + [1, 2, 3]:
        onward = number < STRIDE
        fill(number, *(("behind", "earlier") if onward else ("ahead", "later")))
        offset = number if onward else -STRIDE * (number - STRIDE)
        copy = remote(message.at[number], arrived.at[number], later_send, later_recv, number, offset)
        copy.start()
        later.append(copy)

    def last_copy(k, onward):
        offset = k if onward else -STRIDE * k
        return remote(extra_message.at[k], extra_arrived.at[k], last_send, last_recv, k, offset)

    def to_high(k):
        return (me + k >= HIGH) & (me + k < DEVICES)

    def to_low(k):
        return (me - STRIDE * k >= 0) & (me - STRIDE * k < LOW)

    for k in range(STRIDE):
        for goes, number in ((to_high(k), k), (to_low(k), STRIDE + k)):
            @pl.when(goes)
            def _():
                for q in range(SLOTS):
                    extra_message[k, q] = window[table_ref[number * SLOTS + q, AT["extra"]]]
                if k > 0:
                    last_copy(k, number < STRIDE).start()

    fill(0, "behind", "earlier")
    fill(STRIDE, "ahead", "later")
    lax.fori_loop(EARLY, PAIRS, one_pair, 0)
    for copy in later:
        copy.wait()
    flag = own_row(table_ref, 0, "up") > 0
    for q in range(PACK):
        behind = message[0, q]
        for number in range(1, STRIDE):
            behind = behind + arrived[number, q]
        ahead = message[STRIDE, q]
        for number in range(STRIDE + 1, TARGETS):
            ahead = ahead + arrived[number, q]
        if q < SLOTS:
            halo_ref[q] = jnp.where(flag, behind, ahead)
            halo_ref[SLOTS + q] = jnp.where(flag, ahead, behind)
        else:
            halo_ref[2 * SLOTS] = behind
            halo_ref[2 * SLOTS + 1] = ahead
    for k in range(1, STRIDE):
        for goes, onward in ((to_high(k), True), (to_low(k), False)):
            @pl.when(goes)
            def _():
                last_copy(k, onward).wait_send()

        for comes, onward in ((me >= HIGH, True), (me < LOW, False)):
            @pl.when(comes)
            def _():
                last_copy(k, onward).wait_recv()

    @pl.when((me >= HIGH) | (me < LOW))
    def _():
        for q in range(SLOTS):
            value = extra_message[0, q]
            for k in range(1, STRIDE):
                value = value + extra_arrived[k, q]
            halo_ref[SLOTS + q] = halo_ref[SLOTS + q] + value


def exchange(table, up, down, beside, tracers, velocity, kappa, kmt):
    vmem = pl.BlockSpec(memory_space=pltpu.VMEM)
    anywhere = pl.BlockSpec(memory_space=pltpu.HBM)

    def packets(*lead):
        return pltpu.VMEM(lead + (8, LANES), jnp.float32)

    def tiles(*lead):
        return pltpu.VMEM(lead[:-1] + (8, lead[-1] * LANES), jnp.float32)

    def sems(count):
        return [pltpu.SemaphoreType.DMA((count,))] * 2

    cells = jax.ShapeDtypeStruct((8, TILES * LANES), jnp.int32)
    return pl.pallas_call(
        exchange_kernel,
        out_shape=[
            packet_shape(WANT),
            packet_shape(2),
            jax.ShapeDtypeStruct((PAIRS, 8, TILES * LANES), jnp.float32),
            packet_shape(PAIRS, 8),
            packet_shape(PAIRS, 16),
            cells,
            cells,
        ],
        in_specs=[pl.BlockSpec(memory_space=pltpu.SMEM)] + [vmem] * 3 + [anywhere] * 4,
        out_specs=[vmem] * 7,
        scratch_shapes=[
            packets(WINDOW),
            packets(TARGETS, PACK),
            packets(STRIDE, SLOTS),
            packets(TARGETS, PACK),
            packets(STRIDE, SLOTS),
            *sems(HOPS - 1 + EXTRAS + 2),
            *sems(EXTRAS),
            *sems(TARGETS),
            *sems(STRIDE),
            pltpu.VMEM((SLOTS, 4, CELLS), jnp.float32),
            pltpu.VMEM((SLOTS, 4, CELLS), jnp.float32),
            pltpu.VMEM((SLOTS, CELLS), jnp.float32),
            pltpu.VMEM((SLOTS, CELLS), jnp.float32),
            tiles(FRAME),
            tiles(FRAME),
            tiles(FRAME),
            tiles(PAIRS, FRAME),
            tiles(PAIRS, TILES),
            tiles(TILES),
            tiles(TILES),
            pltpu.VMEM((8, TILES * LANES), jnp.int32),
            pltpu.SemaphoreType.DMA((4,)),
        ],
        compiler_params=pltpu.CompilerParams(collective_id=0, has_side_effects=True, vmem_limit_bytes=BIG),
        name="exchange",
    )(table, up, down, beside, tracers, velocity, kappa, kmt)


def flux(w, far_a, a, b, far_b):
    return jnp.maximum(w, 0.0) * (5.0 * a + 2.0 * b - far_a) + jnp.minimum(w, 0.0) * (2.0 * a + 5.0 * b - far_b)


def wetness(d):
    sub, _ = iotas()
    return jnp.clip(d - (sub % 2).astype(jnp.float32), 0.0, 1.0)


def swap(z):
    sub, _ = iotas()
    return jnp.where(sub % 2 == 1, pltpu.roll(z, 1, 0), pltpu.roll(z, 7, 0))


def prepare(kappa_ref, kmt_ref, xs, us, vs, all_ds, all_ks, place_ref, spot_ref, kind_ref):
    sub, lane = iotas()
    zero = jnp.zeros((8, LANES), jnp.float32)
    for t in (0, 1, 45, 46):
        for ref in (xs, us, vs):
            ref[:, lanes_at(t)] = zero
        for p in range(PAIRS):
            all_ds[p, :, lanes_at(t)] = zero

    def one_tile(t, rows_kappa, rows_kmt):
        flat = lane + t * LANES
        j = ((flat.astype(jnp.float32) + 0.5) * (1.0 / IB)).astype(jnp.int32)
        i = flat - j * IB
        place_ref[:, lanes_at(t)] = i
        spot_ref[:, lanes_at(t)] = j + jnp.where(i >= IB // 2, SIDE, 0)
        kind_ref[:, lanes_at(t)] = jnp.where(
            (i == 0) | (i == IB - 1), 1, jnp.where((i == 1) | (i == IB - 2), 2, 0)
        )
        for p in range(PAIRS):
            for rows, ref, at in ((rows_kmt, all_ds, t + 2), (rows_kappa, all_ks, t)):
                ref[p, :, lanes_at(at)] = jnp.where(sub < 4, row(rows, 2 * p), row(rows, 2 * p + 1))

    for t in range(TILES):
        one_tile(t, load_rows(kappa_ref, t), load_rows(kmt_ref, t))


def interior(tracers_ref, velocity_ref, xs, us, vs, ds, ks, ws, gs, place_ref, partial_ref, edges_ref, rows_ref):
    sub, lane = iotas()
    lower_half = sub % 4 < 2
    column = lane % SIDE
    base_near = column * IB + jnp.where(lane >= SIDE, IB - 1, 0)
    base_far = column * IB + jnp.where(lane >= SIDE, IB - 2, 1)
    bases = (base_near // LANES, base_near % LANES), (base_far // LANES, base_far % LANES)
    for t in range(TILES):
        xs[:, lanes_at(t + 2)] = jnp.concatenate([load4(tracers_ref, 0, t), load4(tracers_ref, 1, t)], axis=0)
        speed = jnp.concatenate([load4(velocity_ref, 0, t), load4(velocity_ref, 1, t)], axis=0)
        us[:, lanes_at(t + 2)] = jnp.where(lower_half, speed, pltpu.roll(speed, 2, 0))
        vs[:, lanes_at(t + 2)] = jnp.where(lower_half, pltpu.roll(speed, 6, 0), speed)
    turned = {}

    def tile_of(name, ref, tile):
        if (name, tile, 0) not in turned:
            turned[name, tile, 0] = ref[:, lanes_at(tile)]
        return turned[name, tile, 0]

    def turn(name, ref, tile, r):
        if (name, tile, r) not in turned:
            turned[name, tile, r] = pltpu.roll(tile_of(name, ref, tile), LANES - r, 1)
        return turned[name, tile, r]

    def shift(name, ref, t, s):
        tile = t + 2 + s // LANES
        r = s % LANES
        return jnp.where(lane < LANES - r, turn(name, ref, tile, r), turn(name, ref, tile + 1, r))

    edges = [jnp.zeros((8, LANES), jnp.float32)] * 8
    for t in range(TILES):
        for key in [k for k in turned if k[1] < t]:
            del turned[key]
        i = place_ref[:, lanes_at(t)]
        x, u, v = (tile_of(name, ref, t + 2) for name, ref in (("x", xs), ("u", us), ("v", vs)))
        wet = wetness(tile_of("d", ds, t + 2))
        west = jnp.where(i == 0, 0.0, shift("x", xs, t, -1))
        west_far = jnp.where(i <= 1, 0.0, shift("x", xs, t, -2))
        east = jnp.where(i == IB - 1, 0.0, shift("x", xs, t, 1))
        east_far = jnp.where(i >= IB - 2, 0.0, shift("x", xs, t, 2))
        wet_west = jnp.where(i == 0, 0.0, wetness(shift("d", ds, t, -1)))
        wet_east = jnp.where(i == IB - 1, 0.0, wetness(shift("d", ds, t, 1)))
        wet_south = wetness(shift("d", ds, t, -IB))
        wet_north = wetness(shift("d", ds, t, IB))
        south, south_far = shift("x", xs, t, -IB), shift("x", xs, t, -2 * IB)
        north, north_far = shift("x", xs, t, IB), shift("x", xs, t, 2 * IB)
        flux_east = flux((u + shift("u", us, t, 1)) * (wet * wet_east), west, x, east, east_far)
        flux_west = flux((shift("u", us, t, -1) + u) * (wet_west * wet), west_far, west, x, east)
        flux_north = flux((v + shift("v", vs, t, IB)) * (wet * wet_north), south, x, north, north_far)
        flux_south = flux((shift("v", vs, t, -IB) + v) * (wet_south * wet), south_far, south, x, north)
        divergence = flux_east - flux_west + (flux_north - flux_south)
        explicit = x - (wet * (COURANT / 12.0)) * divergence
        coupling = ks[:, lanes_at(t)] * wet * swap(wet)
        share = coupling / (1.0 + 2.0 * coupling)
        partial_ref[:, lanes_at(t)] = explicit + share * (swap(explicit) - explicit)
        ws[:, lanes_at(t)] = wet
        gs[:, lanes_at(t)] = share
        for k, (tile, at) in enumerate(bases):
            here = tile == t
            for n, value in enumerate((x, u, wet, share)):
                edges[2 * n + k] = jnp.where(here, take(value, at), edges[2 * n + k])
    for n in range(8):
        edges_ref[n] = edges[n]
    for k, number in enumerate((0, 1, JB - 1, JB - 2)):
        for n, (ref, offset) in enumerate(((xs, 2), (vs, 2), (ws, 0), (gs, 0))):
            rows_ref[4 * k + n] = line(lambda t: ref[:, lanes_at(t + offset)], number * IB, lane)


def finish_kernel(table_ref, halo, sides_ref, beside_ref, partial_ref, edges_ref, rows_ref, spot_ref, kind_ref, out_hbm,
                  around, out_ref, sems):
    for number in range(2 * SLOTS):
        around[number] = sides_ref[number]
    around[2 * SLOTS] = beside_ref[0]
    around[2 * SLOTS + 1] = beside_ref[1]
    around[2 * SLOTS + 2] = halo[2 * SLOTS]
    around[2 * SLOTS + 3] = halo[2 * SLOTS + 1]
    around[2 * SLOTS + 4] = jnp.zeros((8, LANES), jnp.float32)

    def store(pair):
        part = pl.ds(2 * pair, 2)
        return pltpu.make_async_copy(out_ref.at[part], out_hbm.at[part], sems.at[pair])

    def one_pair(pair, carry):
        finish_pair(
            pair, table_ref, halo, around, partial_ref.at[pair], edges_ref.at[pair], rows_ref.at[pair], spot_ref, kind_ref,
            out_ref.at[pl.ds(2 * pair, 2)],
        )
        store(pair).start()
        return carry

    lax.fori_loop(0, PAIRS, one_pair, 0)
    for pair in range(PAIRS):
        store(pair).wait()


def finish_pair(pair, table_ref, halo, around, partial_ref, edges_ref, rows_ref, spot_ref, kind_ref, out_ref):
    sub, lane = iotas()
    upper = sub < 4
    odd = sub % 2 == 1

    def paired(first, second):
        return jnp.where(upper, first, second)

    def across(first, second):
        near = jnp.where(upper, first, pltpu.roll(second, 4, 0))
        return near, jnp.where(upper, pltpu.roll(first, 4, 0), second)

    def unpack(packet):
        a, b = pltpu.roll(packet, 38, 1), pltpu.roll(packet, 76, 1)
        c, d = pltpu.roll(packet, 100, 1), pltpu.roll(packet, 114, 1)

        def joined(first, second, third):
            return jnp.where(lane < 38, first, jnp.where(lane < 76, second, third))

        speed = jnp.where(odd, joined(row(a, 2), row(b, 3), row(d, 6)), joined(row(a, 0), row(b, 1), row(c, 6)))
        return speed, joined(row(a, 4), row(b, 5), row(d, 7))

    def rows_from(first, second):
        near, far = across(first, second)
        (speed_a, depth_a), (speed_b, depth_b) = unpack(first), unpack(second)
        return near, far, paired(speed_a, speed_b), paired(depth_a, depth_b)

    slots = (2 * pair, 2 * pair + 1)
    south = rows_from(halo[slots[0]], halo[slots[1]])
    north = rows_from(halo[SLOTS + slots[0]], halo[SLOTS + slots[1]])
    folded = paired(*(own_row(table_ref, q, "fold") for q in slots)) > 0
    back = jnp.where(lane < IB, IB - 1 - lane, lane)
    north = [
        jnp.where(folded, sign * take(value, back), value) for value, sign in zip(north, (1.0, 1.0, -1.0, 1.0))
    ]
    bodies, speeds, depths = [], [], []
    for q in slots:
        west, east = (around[own_row(table_ref, q, name)] for name in ("west", "east"))
        bodies.append(jnp.where(lane < SIDE, west, pltpu.roll(east, SIDE, 1)))
        aux = jnp.where(lane < SIDE, pltpu.roll(west, SIDE, 1), east)
        speeds.append(jnp.where(odd, row(aux, 1), row(aux, 0)))
        depths.append(row(aux, 2))
    side_near, side_far = across(*bodies)
    side_speed, side_depth = paired(*speeds), paired(*depths)
    keep = paired(*(own_row(table_ref, q, "live") for q in slots)) > 0

    def boundary(sign, halo_near, halo_far, halo_speed, halo_depth, own):
        (x_near, x_far), (speed_near, speed_far), (wet_near, wet_far), (share_near, share_far) = own
        outer = sign * (halo_speed + speed_near) * (wetness(halo_depth) * wet_near)
        inner = sign * (speed_near + speed_far) * (wet_near * wet_far)
        lost = jnp.minimum(inner, 0.0) * halo_near
        near = -(COURANT / 12.0) * wet_near * (flux(outer, x_far, x_near, halo_near, halo_far) + lost)
        far = (COURANT / 12.0) * wet_far * lost
        return near + share_near * (swap(near) - near), far + share_far * (swap(far) - far)

    edges = [edges_ref[n] for n in range(8)]
    rows = [rows_ref[n] for n in range(16)]
    side_sign = jnp.where(lane < SIDE, -1.0, 1.0)
    side = boundary(side_sign, side_near, side_far, side_speed, side_depth, [edges[2 * n : 2 * n + 2] for n in range(4)])
    add_south = boundary(-1.0, *south, list(zip(rows[0:4], rows[4:8])))
    add_north = boundary(1.0, *north, list(zip(rows[8:12], rows[12:16])))
    pieces = {}
    for start, value in zip((0, IB, (JB - 1) * IB, (JB - 2) * IB), (*add_south, *add_north)):
        first, at = start // LANES, start % LANES
        moved = pltpu.roll(value, at, 1) if at else value
        pieces.setdefault(first, []).append((moved, (lane >= at) & (lane < at + IB)))
        if at + IB > LANES:
            pieces.setdefault(first + 1, []).append((moved, lane < at + IB - LANES))
    for t in range(TILES):
        kind, index = kind_ref[:, lanes_at(t)], spot_ref[:, lanes_at(t)]
        value = partial_ref[:, lanes_at(t)]
        value = value + jnp.where(kind == 1, take(side[0], index), jnp.where(kind == 2, take(side[1], index), 0.0))
        for moved, mask in pieces.get(t, []):
            value = value + jnp.where(mask, moved, 0.0)
        value = jnp.where(keep, value, 0.0)
        width = min(LANES, CELLS - t * LANES)
        out_ref[0, :, pl.ds(t * LANES, width)] = value[0:4, :width]
        out_ref[1, :, pl.ds(t * LANES, width)] = value[4:8, :width]


def finish(table, halo, sides, beside, partial, edges, rows, spot, kind):
    vmem = pl.BlockSpec(memory_space=pltpu.VMEM)
    return pl.pallas_call(
        finish_kernel,
        out_shape=jax.ShapeDtypeStruct((SLOTS, 4, CELLS), jnp.float32),
        in_specs=[pl.BlockSpec(memory_space=pltpu.SMEM)] + [vmem] * 8,
        out_specs=pl.BlockSpec(memory_space=pltpu.HBM),
        scratch_shapes=[
            pltpu.VMEM((2 * SLOTS + 5, 8, LANES), jnp.float32),
            pltpu.VMEM((SLOTS, 4, CELLS), jnp.float32),
            pltpu.SemaphoreType.DMA((PAIRS,)),
        ],
        compiler_params=pltpu.CompilerParams(vmem_limit_bytes=BIG),
        name="final",
    )(table, halo, sides, beside, partial, edges, rows, spot, kind)


def per_device(tracers, velocity, kappa, kmt, block_owner, neighbours, fold_partner):
    table, up, down, beside, sides = front(block_owner, neighbours, fold_partner, tracers, velocity, kmt)
    halo, beside, *work = exchange(table, up, down, beside, tracers, velocity, kappa, kmt)
    return finish(table, halo, sides, beside, *work)


def solution(mesh):
    placed = (
        P(("blk", "sub"), None, None),
        P(("blk", "sub"), None, None),
        P(("blk", "sub"), None),
        P(("blk", "sub"), None),
        P(),
        P(),
        P(),
    )
    return jax.shard_map(
        per_device,
        mesh=mesh,
        in_specs=placed,
        out_specs=P(("blk", "sub"), None, None),
        check_vma=False,
    )
```

```python
import jax
import jax.numpy as jnp
from jax import lax
from jax.experimental import pallas as pl
from jax.experimental.pallas import tpu as pltpu
from jax.sharding import PartitionSpec as P

IB = 90
JB = 60
CELLS = IB * JB
SLOTS = 10
PAIRS = SLOTS // 2
DEVICES = 256
COURANT = 0.2
STRIDE = 4
HOPS = 7
LANES = 128
TILES = 43
FRAME = 47
SIDE = 64
PACK = SLOTS + 1
OWN_DOWN = HOPS * PACK
EXTRA = OWN_DOWN + STRIDE * PACK
EXTRAS = 3
EMPTY = EXTRA + EXTRAS * PACK
WINDOW = EMPTY + 1
WANT = 2 * SLOTS + 2
TARGETS = STRIDE + HOPS
TABLE_ROWS = 112
EARLY = 2
EDGES = 24
BIG = 63 << 20
FOLD_REACH = 14
MESH = pl.DeviceIdType.MESH
COLUMNS = ("behind", "ahead", "extra", "earlier", "later", "west", "east", "send_later", "send_earlier", "next", "previous", "fold", "live", "up")
AT = {name: number for number, name in enumerate(COLUMNS)}


def position():
    return lax.axis_index("blk") * 4 + lax.axis_index("sub")


def lanes_at(tile):
    return pl.ds(tile * LANES, LANES)


def iotas():
    return (
        lax.broadcasted_iota(jnp.int32, (8, LANES), 0),
        lax.broadcasted_iota(jnp.int32, (8, LANES), 1),
    )


def take(packed, index):
    return jnp.take_along_axis(packed, index, axis=1, mode="promise_in_bounds")


def row(value, number):
    return jnp.broadcast_to(value[number : number + 1], (8, LANES))


def table_of(owner_ref, near_ref, fold_ref):
    me = position()
    rows = TABLE_ROWS
    strips = owner_ref.shape[0]
    number = lax.broadcasted_iota(jnp.int32, (rows, 1), 0).astype(jnp.float32)
    which = jnp.floor((number + 0.5) * (1.0 / SLOTS))
    slot = number - which * SLOTS
    onward = which < STRIDE
    hops = jnp.where(onward, which, which - STRIDE)
    device = jnp.where(onward, hops, -STRIDE * hops) + jnp.float32(1) * me
    device = jnp.where(device < 0, device + DEVICES, device)
    device = jnp.where(device >= DEVICES, device - DEVICES, device)
    code = device * SLOTS + slot
    wide = lax.broadcasted_iota(jnp.int32, (1, LANES), 1).astype(jnp.float32)

    def total(pieces):
        acc = jnp.zeros((rows, LANES), jnp.float32)
        for mask, value in pieces:
            acc = acc + jnp.where(mask, value, 0.0)
        return jnp.sum(acc, axis=1, keepdims=True)

    owners = [owner_ref[t : t + 1, :].astype(jnp.float32) for t in range(strips)]
    hits = [owner == code for owner in owners]
    first = device * SLOTS
    own_count = total([((owner >= first) & (owner < first + SLOTS), 1.0) for owner in owners])
    before_count = total([((owner >= first - SLOTS) & (owner < first), 1.0) for owner in owners])
    live = total([(hit, 1.0) for hit in hits])
    links = []
    for k in range(5):
        if k < 4:
            link = [near_ref[k : k + 1, lanes_at(t)].astype(jnp.float32) for t in range(strips)]
        else:
            link = [fold_ref[t : t + 1, :].astype(jnp.float32) for t in range(strips)]
        block = total([(hit, piece + 1.0) for hit, piece in zip(hits, link)]) - 1.0
        links.append(total([(block == wide + t * LANES, owner + 1.0) for t, owner in enumerate(owners)]) - 1.0)

    def where_is(other):
        source = jnp.floor((other + 0.5) * (1.0 / SLOTS))
        apart = source - device
        distance = jnp.abs(apart)
        far = jnp.floor((distance + 0.5) * (1.0 / STRIDE))
        rest = distance - far * STRIDE
        from_behind = (other >= 0) & (apart <= 0) & onward & (rest == hops)
        from_ahead = (other >= 0) & (apart >= 0) & ~onward & (far == hops)
        return source, other - source * SLOTS, apart, far, rest, from_behind, from_ahead

    vote = jnp.where(links[3] >= 0, jnp.where(links[3] > code, 1.0, -1.0), 0.0)
    vote = vote - jnp.where(links[2] >= 0, jnp.where(links[2] > code, 1.0, -1.0), 0.0)
    up = jnp.sum(vote, axis=0, keepdims=True) >= 0
    empty = float(EMPTY)
    _, place, _, far, _, from_behind, _ = where_is(jnp.where(up, links[2], links[3]))
    behind = jnp.where(from_behind, far * PACK + place, empty)
    _, place, _, _, rest, _, from_ahead = where_is(jnp.where(up, links[3], links[2]))
    ahead = jnp.where(from_ahead, OWN_DOWN + rest * PACK + place, empty)
    _, place, apart, far, rest, from_behind, from_ahead = where_is(links[4])
    against = jnp.where(rest > 0, EXTRA + (rest - 1.0) * PACK, 0.0) + place
    ahead = jnp.where(up & from_ahead, against, ahead)
    against = jnp.where(far > 0, EXTRA + (far - 1.0) * PACK, float(OWN_DOWN)) + place
    behind = jnp.where(~up & from_behind, against, behind)
    extra = jnp.where(up & from_behind & (apart < 0), far * PACK + place, empty)
    extra = jnp.where(~up & from_ahead & (apart > 0), OWN_DOWN + rest * PACK + place, extra)
    sides = []
    columns = {"earlier": 0.0, "later": 0.0, "send_later": 0.0, "send_earlier": 0.0, "next": 0.0, "previous": 0.0}
    for side in range(2):
        other = links[side]
        source, place, apart, far, rest, from_behind, from_ahead = where_is(other)
        linked = other >= 0
        after = linked & (slot == own_count - 1.0) & (other == device * SLOTS + SLOTS)
        before = linked & (slot == 0) & (apart == -1) & (place + 1.0 == before_count)
        earlier = linked & (apart < 0) & ~before
        later = linked & (apart > 0) & ~after
        mine = slot * 2.0 + (side + 1.0)
        columns["earlier"] += jnp.where(earlier & from_behind, far * PACK + SLOTS - EMPTY, 0.0)
        columns["later"] += jnp.where(later & from_ahead, OWN_DOWN + rest * PACK + SLOTS - EMPTY, 0.0)
        columns["send_later"] += jnp.where(later, mine, 0.0)
        columns["send_earlier"] += jnp.where(earlier, mine, 0.0)
        columns["next"] += jnp.where(after, mine, 0.0)
        columns["previous"] += jnp.where(before, mine, 0.0)
        index = jnp.where(linked & (apart == 0), place * 2.0 + (1.0 - side), 24.0)
        index = jnp.where(before, 20.0, jnp.where(after, 21.0, index))
        index = jnp.where(earlier, 22.0, jnp.where(later, 23.0, index))
        sides.append(jnp.clip(index, 0.0, 24.0))
    columns.update(
        behind=behind, ahead=ahead, extra=extra, west=sides[0], east=sides[1], live=live,
        fold=jnp.where(links[4] >= 0, 1.0, 0.0), up=jnp.where(up, 1.0, 0.0),
    )
    for name in ("behind", "ahead", "extra"):
        columns[name] = jnp.clip(columns[name], 0.0, empty)
    lane = lax.broadcasted_iota(jnp.int32, (rows, LANES), 1)
    result = jnp.zeros((rows, LANES), jnp.float32)
    for name, at in AT.items():
        result = jnp.where(lane == at, columns[name], result)
    own = number < SLOTS
    chosen = {
        name: jnp.sum(jnp.where(own, columns[name], 0.0), axis=0, keepdims=True)
        for name in ("send_later", "send_earlier", "next", "previous")
    }
    return result.astype(jnp.int32), up, chosen


def own_row(table_ref, slot, name):
    return table_ref[slot, AT[name]]


def load4(ref, half, t):
    if t < TILES - 1:
        return ref[half, :, lanes_at(t)]
    width = CELLS - t * LANES
    return jnp.pad(ref[half, :, pl.ds(t * LANES, width)], ((0, 0), (0, LANES - width)))


def load_rows(ref, t):
    if t < TILES - 1:
        return ref[:, lanes_at(t)]
    width = CELLS - t * LANES
    return jnp.pad(ref[:, pl.ds(t * LANES, width)], ((0, 0), (0, LANES - width)))


def line(tiles, start, lane):
    first = start // LANES
    r = start % LANES
    if r == 0:
        return tiles(first)
    amount = LANES - r
    return jnp.where(lane < amount, pltpu.roll(tiles(first), amount, 1), pltpu.roll(tiles(first + 1), amount, 1))


ROW_STARTS = (0, IB, (JB - 1) * IB, (JB - 2) * IB)


def pack_edges(fetch, loads, up, chosen, tracers_all, velocity_all, kmt_ref, up_ref, down_ref, next_ref, sides_ref, depth_rows):
    sub, lane = iotas()
    flag = jnp.broadcast_to(up, (8, LANES))
    column = lane % SIDE
    base_near = column * IB + jnp.where(lane >= SIDE, IB - 1, 0)
    base_far = column * IB + jnp.where(lane >= SIDE, IB - 2, 1)
    near_tile, near_at = base_near // LANES, base_near % LANES
    far_tile, far_at = base_far // LANES, base_far % LANES
    loads["kmt"].wait()
    near = jnp.zeros((16, LANES), jnp.float32)
    index16 = jnp.concatenate([near_at, near_at], axis=0)
    tile16 = jnp.concatenate([near_tile, near_tile], axis=0)

    def padded(t):
        return jnp.pad(load_rows(kmt_ref, t), ((0, 6), (0, 0)))

    for t in range(TILES):
        near = jnp.where(tile16 == t, take(padded(t), index16), near)
    south = padded(0)
    north = line(padded, (JB - 1) * IB, lane[0:1])
    for q in range(SLOTS):
        depth_rows[0, q] = row(south, q)
        depth_rows[1, q] = row(north, q)
        depth_rows[2, q] = row(near, q)
    aux_at = lane
    for s in range(8):
        move = {6: 28, 7: 14}.get(s, 90 if s % 2 == 0 else 52)
        aux_at = jnp.where((sub == s) & (lane >= IB), lane - move, aux_at)
    lane4 = lane[0:4]

    def one_pair(pair, carry):
        for copy in fetch(pair):
            copy.wait()
        tracers_ref, velocity_ref = tracers_all.at[pl.ds(2 * pair, 2)], velocity_all.at[pl.ds(2 * pair, 2)]
        for half in range(2):
            q = 2 * pair + half

            def tracer(t):
                return load4(tracers_ref, half, t)

            def speed(t):
                return load4(velocity_ref, half, t)

            packets = []
            for kind, (near, far) in enumerate(((0, 1), (JB - 1, JB - 2))):
                body = jnp.concatenate([line(tracer, near * IB, lane4), line(tracer, far * IB, lane4)], axis=0)
                v = line(speed, near * IB, lane4)
                v0, v1 = row(v, 2), row(v, 3)
                joint = jnp.where(lane >= 76, v0, pltpu.roll(v1, LANES - 14, 1))
                aux = jnp.where(sub == 6, joint, depth_rows[kind, q])
                aux = jnp.where(sub < 2, v0, jnp.where(sub < 4, v1, aux))
                packets.append(jnp.where(lane < IB, body, take(aux, aux_at)))
            up_ref[q] = jnp.where(flag, packets[1], packets[0])
            down_ref[q] = jnp.where(flag, packets[0], packets[1])
        near = far = drift = jnp.zeros((8, LANES), jnp.float32)
        for t in range(TILES):
            x = jnp.concatenate([load4(tracers_ref, 0, t), load4(tracers_ref, 1, t)], axis=0)
            v = jnp.concatenate([load4(velocity_ref, 0, t), load4(velocity_ref, 1, t)], axis=0)
            near = jnp.where(near_tile == t, take(x, near_at), near)
            far = jnp.where(far_tile == t, take(x, far_at), far)
            drift = jnp.where(near_tile == t, take(v, near_at), drift)
        for half in range(2):
            q = 2 * pair + half
            if half == 0:
                body = jnp.where(sub < 4, near, pltpu.roll(far, 4, 0))
                aux = drift
            else:
                body = jnp.where(sub < 4, pltpu.roll(near, 4, 0), far)
                aux = pltpu.roll(drift, 4, 0)
            aux = jnp.where(sub == 2, depth_rows[2, q], aux)
            sides_ref[2 * q] = jnp.where(lane < SIDE, body, pltpu.roll(aux, SIDE, 1))
            sides_ref[2 * q + 1] = jnp.where(lane < SIDE, pltpu.roll(body, SIDE, 1), aux)
        return carry

    lax.fori_loop(0, PAIRS, one_pair, 0)
    outputs = {"send_later": (up_ref, SLOTS), "send_earlier": (down_ref, SLOTS), "next": (next_ref, 0), "previous": (next_ref, 1)}
    for name, (ref, at) in outputs.items():
        which = jnp.broadcast_to(chosen[name], (8, LANES))
        packet = jnp.zeros((8, LANES), jnp.float32)
        for number in range(2 * SLOTS):
            packet = jnp.where(which == number + 1.0, sides_ref[number], packet)
        ref[at] = packet


def packet_shape(*lead):
    return jax.ShapeDtypeStruct(lead + (8, LANES), jnp.float32)


def coordinates(index):
    index = lax.rem(index + DEVICES, DEVICES)
    return (index // 4, lax.rem(index, 4))


PARTNERS = [sign * step for step in [1, 2, 3] + [STRIDE * a for a in range(1, HOPS)] for sign in (1, -1)]
HIGH, LOW = DEVICES - FOLD_REACH, FOLD_REACH


def exchange_kernel(owner_hbm, near_hbm, fold_hbm, tracers_hbm, velocity_hbm, kappa_hbm, kmt_hbm, table_out, halo_ref,
                    beside_ref, sides_ref, partial_hbm, edges_hbm, up_ref, down_ref, next_ref, window, message,
                    extra_message, arrived, extra_arrived, send_sem, recv_sem, extra_send, extra_recv, later_send, later_recv,
                    last_send, last_recv, owner_ref, near_ref, fold_ref, tracers_all, velocity_all, kappa_ref, kmt_ref,
                    depth_rows, table_ref, xs, us, vs, all_ds, all_ks, ws, gs, place_ref, partial_all, edges_all, load_sem,
                    pair_sem, out_sem):
    me = position()
    barrier = pltpu.get_barrier_semaphore()
    for offset in PARTNERS:
        pl.semaphore_signal(barrier, inc=1, device_id=coordinates(me + offset), device_id_type=MESH)
    sources = {
        "owner": (owner_hbm, owner_ref),
        "near": (near_hbm, near_ref),
        "fold": (fold_hbm, fold_ref),
        "kmt": (kmt_hbm, kmt_ref),
        "kappa": (kappa_hbm, kappa_ref),
    }
    loads = {
        name: pltpu.make_async_copy(source, target, load_sem.at[number])
        for number, (name, (source, target)) in enumerate(sources.items())
    }

    def fetch(pair):
        part = pl.ds(2 * pair, 2)
        return (
            pltpu.make_async_copy(tracers_hbm.at[part], tracers_all.at[part], pair_sem.at[0, pair]),
            pltpu.make_async_copy(velocity_hbm.at[part], velocity_all.at[part], pair_sem.at[1, pair]),
        )

    for name in ("owner", "near", "fold", "kmt"):
        loads[name].start()
    for pair in range(PAIRS):
        for copy in fetch(pair):
            copy.start()
    loads["kappa"].start()
    for name in ("owner", "near", "fold"):
        loads[name].wait()
    table, up, chosen = table_of(owner_ref, near_ref, fold_ref)
    table_out[...] = table
    table_copy = pltpu.make_async_copy(table_out, table_ref, load_sem.at[len(sources)])
    table_copy.start()
    pack_edges(
        fetch, loads, up, chosen, tracers_all, velocity_all, kmt_ref, up_ref, down_ref, next_ref, sides_ref, depth_rows
    )
    pl.semaphore_wait(barrier, len(PARTNERS))

    def remote(source, target, sends, recvs, number, offset):
        return pltpu.make_async_remote_copy(
            src_ref=source,
            dst_ref=target,
            send_sem=sends.at[number],
            recv_sem=recvs.at[number],
            device_id=coordinates(me + offset),
            device_id_type=MESH,
        )

    plan = []
    for a in range(HOPS - 1, 0, -1):
        plan.append((up_ref, window.at[pl.ds(a * PACK, PACK)], STRIDE * a))
        if a < STRIDE:
            plan.append((down_ref, window.at[pl.ds(OWN_DOWN + a * PACK, PACK)], -a))
    plan.append((next_ref.at[0], beside_ref.at[0], 1))
    plan.append((next_ref.at[1], beside_ref.at[1], -1))
    copies = [
        remote(source, target, send_sem, recv_sem, number, offset)
        for number, (source, target, offset) in enumerate(plan)
    ]
    for copy in copies:
        copy.start()

    def fold_copy(k, downwards):
        target = window.at[pl.ds(EXTRA + (k - 1) * PACK, PACK)]
        if downwards:
            return remote(up_ref, target, extra_send, extra_recv, k - 1, -k)
        return remote(down_ref, target, extra_send, extra_recv, k - 1, STRIDE * k)

    for k in range(1, EXTRAS + 1):
        @pl.when(me >= HIGH)
        def _():
            fold_copy(k, True).start()

        @pl.when(me < LOW)
        def _():
            fold_copy(k, False).start()

        from_high = (me + k >= HIGH) & (me + k < DEVICES)
        from_low = (me - STRIDE * k >= 0) & (me - STRIDE * k < LOW)

        @pl.when(jnp.logical_not(from_high | from_low))
        def _():
            window[pl.ds(EXTRA + (k - 1) * PACK, PACK)] = jnp.zeros((PACK, 8, LANES), jnp.float32)

    window[pl.ds(0, PACK)] = up_ref[...]
    window[pl.ds(OWN_DOWN, PACK)] = down_ref[...]
    window[EMPTY] = jnp.zeros((8, LANES), jnp.float32)
    loads["kappa"].wait()
    prepare(kappa_ref, kmt_ref, xs, us, vs, all_ds, all_ks, place_ref)

    def save(pair):
        return (
            pltpu.make_async_copy(partial_all.at[pair], partial_hbm.at[pair], out_sem.at[0, pair]),
            pltpu.make_async_copy(edges_all.at[pair], edges_hbm.at[pair], out_sem.at[1, pair]),
        )

    def one_pair(pair, carry):
        part = pl.ds(2 * pair, 2)
        interior(
            tracers_all.at[part], velocity_all.at[part], xs, us, vs, all_ds.at[pair], all_ks.at[pair], ws, gs,
            place_ref, partial_all.at[pair], edges_all.at[pair],
        )
        for copy in save(pair):
            copy.start()
        return carry

    table_copy.wait()
    lax.fori_loop(0, EARLY, one_pair, 0)
    for copy in copies:
        copy.wait()
    for k in range(1, EXTRAS + 1):
        @pl.when(me >= HIGH)
        def _():
            fold_copy(k, True).wait_send()

        @pl.when(me < LOW)
        def _():
            fold_copy(k, False).wait_send()

        @pl.when((me + k >= HIGH) & (me + k < DEVICES))
        def _():
            fold_copy(k, True).wait_recv()

        @pl.when((me - STRIDE * k >= 0) & (me - STRIDE * k < LOW))
        def _():
            fold_copy(k, False).wait_recv()

    def picked(index):
        return window[jnp.minimum(jnp.maximum(index, 0), EMPTY)]

    def fill(number, halo_name, wrap_name):
        wrap = EMPTY
        for q in range(SLOTS):
            r = number * SLOTS + q
            message[number, q] = picked(table_ref[r, AT[halo_name]])
            wrap = wrap + table_ref[r, AT[wrap_name]]
        message[number, SLOTS] = picked(wrap)

    later = []
    for number in [STRIDE + a for a in range(HOPS - 1, 0, -1)] + [1, 2, 3]:
        onward = number < STRIDE
        fill(number, *(("behind", "earlier") if onward else ("ahead", "later")))
        offset = number if onward else -STRIDE * (number - STRIDE)
        copy = remote(message.at[number], arrived.at[number], later_send, later_recv, number, offset)
        copy.start()
        later.append(copy)

    def last_copy(k, onward):
        offset = k if onward else -STRIDE * k
        return remote(extra_message.at[k], extra_arrived.at[k], last_send, last_recv, k, offset)

    def to_high(k):
        return (me + k >= HIGH) & (me + k < DEVICES)

    def to_low(k):
        return (me - STRIDE * k >= 0) & (me - STRIDE * k < LOW)

    for k in range(STRIDE):
        for goes, number in ((to_high(k), k), (to_low(k), STRIDE + k)):
            @pl.when(goes)
            def _():
                for q in range(SLOTS):
                    extra_message[k, q] = picked(table_ref[number * SLOTS + q, AT["extra"]])
                if k > 0:
                    last_copy(k, number < STRIDE).start()

    fill(0, "behind", "earlier")
    fill(STRIDE, "ahead", "later")
    lax.fori_loop(EARLY, PAIRS, one_pair, 0)
    for copy in later:
        copy.wait()
    flag = own_row(table_ref, 0, "up") > 0
    for q in range(PACK):
        behind = message[0, q]
        for number in range(1, STRIDE):
            behind = behind + arrived[number, q]
        ahead = message[STRIDE, q]
        for number in range(STRIDE + 1, TARGETS):
            ahead = ahead + arrived[number, q]
        if q < SLOTS:
            halo_ref[q] = jnp.where(flag, behind, ahead)
            halo_ref[SLOTS + q] = jnp.where(flag, ahead, behind)
        else:
            halo_ref[2 * SLOTS] = behind
            halo_ref[2 * SLOTS + 1] = ahead
    for pair in range(PAIRS):
        for copy in save(pair):
            copy.wait()
    for k in range(1, STRIDE):
        for goes, onward in ((to_high(k), True), (to_low(k), False)):
            @pl.when(goes)
            def _():
                last_copy(k, onward).wait_send()

        for comes, onward in ((me >= HIGH, True), (me < LOW, False)):
            @pl.when(comes)
            def _():
                last_copy(k, onward).wait_recv()

    @pl.when((me >= HIGH) | (me < LOW))
    def _():
        for q in range(SLOTS):
            value = extra_message[0, q]
            for k in range(1, STRIDE):
                value = value + extra_arrived[k, q]
            halo_ref[SLOTS + q] = halo_ref[SLOTS + q] + value


def exchange(block_owner, neighbours, fold_partner, tracers, velocity, kappa, kmt):
    vmem = pl.BlockSpec(memory_space=pltpu.VMEM)
    anywhere = pl.BlockSpec(memory_space=pltpu.HBM)

    def packets(*lead):
        return pltpu.VMEM(lead + (8, LANES), jnp.float32)

    def tiles(*lead):
        return pltpu.VMEM(lead[:-1] + (8, lead[-1] * LANES), jnp.float32)

    def sems(count):
        return [pltpu.SemaphoreType.DMA((count,))] * 2

    return pl.pallas_call(
        exchange_kernel,
        out_shape=[
            jax.ShapeDtypeStruct((TABLE_ROWS, LANES), jnp.int32),
            packet_shape(WANT),
            packet_shape(2),
            packet_shape(2 * SLOTS),
            jax.ShapeDtypeStruct((PAIRS, 8, TILES * LANES), jnp.float32),
            packet_shape(PAIRS, EDGES),
        ],
        in_specs=[anywhere] * 7,
        out_specs=[vmem] * 4 + [anywhere] * 2,
        scratch_shapes=[
            packets(PACK),
            packets(PACK),
            packets(2),
            packets(WINDOW),
            packets(TARGETS, PACK),
            packets(STRIDE, SLOTS),
            packets(TARGETS, PACK),
            packets(STRIDE, SLOTS),
            *sems(HOPS - 1 + EXTRAS + 2),
            *sems(EXTRAS),
            *sems(TARGETS),
            *sems(STRIDE),
            pltpu.VMEM((SLOTS, LANES), jnp.int32),
            pltpu.VMEM((4, SLOTS * LANES), jnp.int32),
            pltpu.VMEM((SLOTS, LANES), jnp.int32),
            pltpu.VMEM((SLOTS, 4, CELLS), jnp.float32),
            pltpu.VMEM((SLOTS, 4, CELLS), jnp.float32),
            pltpu.VMEM((SLOTS, CELLS), jnp.float32),
            pltpu.VMEM((SLOTS, CELLS), jnp.float32),
            packets(3, SLOTS),
            pltpu.SMEM((TABLE_ROWS, LANES), jnp.int32),
            tiles(FRAME),
            tiles(FRAME),
            tiles(FRAME),
            tiles(PAIRS, FRAME),
            tiles(PAIRS, TILES),
            tiles(TILES),
            tiles(TILES),
            pltpu.VMEM((8, TILES * LANES), jnp.int32),
            tiles(PAIRS, TILES),
            packets(PAIRS, EDGES),
            pltpu.SemaphoreType.DMA((6,)),
            pltpu.SemaphoreType.DMA((2, PAIRS)),
            pltpu.SemaphoreType.DMA((2, PAIRS)),
        ],
        compiler_params=pltpu.CompilerParams(collective_id=0, has_side_effects=True, vmem_limit_bytes=BIG),
        name="exchange",
    )(block_owner.reshape(-1, LANES), neighbours.T, fold_partner.reshape(-1, LANES), tracers, velocity, kappa, kmt)


def flux(w, far_a, a, b, far_b):
    return jnp.maximum(w, 0.0) * (5.0 * a + 2.0 * b - far_a) + jnp.minimum(w, 0.0) * (2.0 * a + 5.0 * b - far_b)


def wetness(d):
    sub, _ = iotas()
    return jnp.clip(d - (sub % 2).astype(jnp.float32), 0.0, 1.0)


def swap(z):
    sub, _ = iotas()
    return jnp.where(sub % 2 == 1, pltpu.roll(z, 1, 0), pltpu.roll(z, 7, 0))


def place_of(t, lane):
    flat = lane + t * LANES
    j = ((flat.astype(jnp.float32) + 0.5) * (1.0 / IB)).astype(jnp.int32)
    return j, flat - j * IB


def prepare(kappa_ref, kmt_ref, xs, us, vs, all_ds, all_ks, place_ref):
    sub, lane = iotas()
    zero = jnp.zeros((8, LANES), jnp.float32)
    for t in (0, 1, 45, 46):
        for ref in (xs, us, vs):
            ref[:, lanes_at(t)] = zero
        for p in range(PAIRS):
            all_ds[p, :, lanes_at(t)] = zero

    def one_tile(t, rows_kappa, rows_kmt):
        place_ref[:, lanes_at(t)] = place_of(t, lane)[1]
        for p in range(PAIRS):
            for rows, ref, at in ((rows_kmt, all_ds, t + 2), (rows_kappa, all_ks, t)):
                ref[p, :, lanes_at(at)] = jnp.where(sub < 4, row(rows, 2 * p), row(rows, 2 * p + 1))

    for t in range(TILES):
        one_tile(t, load_rows(kappa_ref, t), load_rows(kmt_ref, t))


def interior(tracers_ref, velocity_ref, xs, us, vs, ds, ks, ws, gs, place_ref, partial_ref, edges_ref):
    sub, lane = iotas()
    lower_half = sub % 4 < 2
    column = lane % SIDE
    base_near = column * IB + jnp.where(lane >= SIDE, IB - 1, 0)
    base_far = column * IB + jnp.where(lane >= SIDE, IB - 2, 1)
    bases = (base_near // LANES, base_near % LANES), (base_far // LANES, base_far % LANES)
    for t in range(TILES):
        xs[:, lanes_at(t + 2)] = jnp.concatenate([load4(tracers_ref, 0, t), load4(tracers_ref, 1, t)], axis=0)
        speed = jnp.concatenate([load4(velocity_ref, 0, t), load4(velocity_ref, 1, t)], axis=0)
        us[:, lanes_at(t + 2)] = jnp.where(lower_half, speed, pltpu.roll(speed, 2, 0))
        vs[:, lanes_at(t + 2)] = jnp.where(lower_half, pltpu.roll(speed, 6, 0), speed)
    turned = {}

    def tile_of(name, ref, tile):
        if (name, tile, 0) not in turned:
            turned[name, tile, 0] = ref[:, lanes_at(tile)]
        return turned[name, tile, 0]

    def turn(name, ref, tile, r):
        if (name, tile, r) not in turned:
            turned[name, tile, r] = pltpu.roll(tile_of(name, ref, tile), LANES - r, 1)
        return turned[name, tile, r]

    def shift(name, ref, t, s):
        tile = t + 2 + s // LANES
        r = s % LANES
        return jnp.where(lane < LANES - r, turn(name, ref, tile, r), turn(name, ref, tile + 1, r))

    edges = [jnp.zeros((8, LANES), jnp.float32)] * 8
    for t in range(TILES):
        for key in [k for k in turned if k[1] < t]:
            del turned[key]
        i = place_ref[:, lanes_at(t)]
        x, u, v = (tile_of(name, ref, t + 2) for name, ref in (("x", xs), ("u", us), ("v", vs)))
        wet = wetness(tile_of("d", ds, t + 2))
        west = jnp.where(i == 0, 0.0, shift("x", xs, t, -1))
        west_far = jnp.where(i <= 1, 0.0, shift("x", xs, t, -2))
        east = jnp.where(i == IB - 1, 0.0, shift("x", xs, t, 1))
        east_far = jnp.where(i >= IB - 2, 0.0, shift("x", xs, t, 2))
        wet_west = jnp.where(i == 0, 0.0, wetness(shift("d", ds, t, -1)))
        wet_east = jnp.where(i == IB - 1, 0.0, wetness(shift("d", ds, t, 1)))
        wet_south = wetness(shift("d", ds, t, -IB))
        wet_north = wetness(shift("d", ds, t, IB))
        south, south_far = shift("x", xs, t, -IB), shift("x", xs, t, -2 * IB)
        north, north_far = shift("x", xs, t, IB), shift("x", xs, t, 2 * IB)
        flux_east = flux((u + shift("u", us, t, 1)) * (wet * wet_east), west, x, east, east_far)
        flux_west = flux((shift("u", us, t, -1) + u) * (wet_west * wet), west_far, west, x, east)
        flux_north = flux((v + shift("v", vs, t, IB)) * (wet * wet_north), south, x, north, north_far)
        flux_south = flux((shift("v", vs, t, -IB) + v) * (wet_south * wet), south_far, south, x, north)
        divergence = flux_east - flux_west + (flux_north - flux_south)
        explicit = x - (wet * (COURANT / 12.0)) * divergence
        coupling = ks[:, lanes_at(t)] * wet * swap(wet)
        share = coupling / (1.0 + 2.0 * coupling)
        partial_ref[:, lanes_at(t)] = explicit + share * (swap(explicit) - explicit)
        ws[:, lanes_at(t)] = wet
        gs[:, lanes_at(t)] = share
        for k, (tile, at) in enumerate(bases):
            here = tile == t
            for n, value in enumerate((x, u, wet, share)):
                edges[2 * n + k] = jnp.where(here, take(value, at), edges[2 * n + k])
    for n in range(8):
        edges_ref[n] = edges[n]
    for k, number in enumerate((0, 1, JB - 1, JB - 2)):
        for n, (ref, offset) in enumerate(((xs, 2), (vs, 2), (ws, 0), (gs, 0))):
            edges_ref[8 + 4 * k + n] = line(lambda t: ref[:, lanes_at(t + offset)], number * IB, lane)


def finish_kernel(table_ref, halo, sides_ref, beside_ref, partial_hbm, edges_hbm, out_hbm, around, partial_all, edges_all,
                  spot_ref, kind_ref, out_ref, load_sem, sems):
    def load(pair):
        return (
            pltpu.make_async_copy(partial_hbm.at[pair], partial_all.at[pair], load_sem.at[0, pair]),
            pltpu.make_async_copy(edges_hbm.at[pair], edges_all.at[pair], load_sem.at[1, pair]),
        )

    for pair in range(PAIRS):
        for copy in load(pair):
            copy.start()
    sub, lane = iotas()
    for t in range(TILES):
        j, i = place_of(t, lane)
        spot_ref[:, lanes_at(t)] = j + jnp.where(i >= IB // 2, SIDE, 0)
        kind_ref[:, lanes_at(t)] = jnp.where(
            (i == 0) | (i == IB - 1), 1, jnp.where((i == 1) | (i == IB - 2), 2, 0)
        )
    for number in range(2 * SLOTS):
        around[number] = sides_ref[number]
    around[2 * SLOTS] = beside_ref[0]
    around[2 * SLOTS + 1] = beside_ref[1]
    around[2 * SLOTS + 2] = halo[2 * SLOTS]
    around[2 * SLOTS + 3] = halo[2 * SLOTS + 1]
    around[2 * SLOTS + 4] = jnp.zeros((8, LANES), jnp.float32)

    def store(pair):
        part = pl.ds(2 * pair, 2)
        return pltpu.make_async_copy(out_ref.at[part], out_hbm.at[part], sems.at[pair])

    def one_pair(pair, carry):
        for copy in load(pair):
            copy.wait()
        finish_pair(
            pair, table_ref, halo, around, partial_all.at[pair], edges_all.at[pair], spot_ref, kind_ref,
            out_ref.at[pl.ds(2 * pair, 2)],
        )
        store(pair).start()
        return carry

    lax.fori_loop(0, PAIRS, one_pair, 0)
    for pair in range(PAIRS):
        store(pair).wait()


def finish_pair(pair, table_ref, halo, around, partial_ref, edges_ref, spot_ref, kind_ref, out_ref):
    sub, lane = iotas()
    upper = sub < 4
    odd = sub % 2 == 1

    def paired(first, second):
        return jnp.where(upper, first, second)

    def across(first, second):
        near = jnp.where(upper, first, pltpu.roll(second, 4, 0))
        return near, jnp.where(upper, pltpu.roll(first, 4, 0), second)

    def unpack(packet):
        a, b = pltpu.roll(packet, 38, 1), pltpu.roll(packet, 76, 1)
        c, d = pltpu.roll(packet, 100, 1), pltpu.roll(packet, 114, 1)

        def joined(first, second, third):
            return jnp.where(lane < 38, first, jnp.where(lane < 76, second, third))

        speed = jnp.where(odd, joined(row(a, 2), row(b, 3), row(d, 6)), joined(row(a, 0), row(b, 1), row(c, 6)))
        return speed, joined(row(a, 4), row(b, 5), row(d, 7))

    def rows_from(first, second):
        near, far = across(first, second)
        (speed_a, depth_a), (speed_b, depth_b) = unpack(first), unpack(second)
        return near, far, paired(speed_a, speed_b), paired(depth_a, depth_b)

    slots = (2 * pair, 2 * pair + 1)
    south = rows_from(halo[slots[0]], halo[slots[1]])
    north = rows_from(halo[SLOTS + slots[0]], halo[SLOTS + slots[1]])
    folded = paired(*(own_row(table_ref, q, "fold") for q in slots)) > 0
    back = jnp.where(lane < IB, IB - 1 - lane, lane)
    north = [
        jnp.where(folded, sign * take(value, back), value) for value, sign in zip(north, (1.0, 1.0, -1.0, 1.0))
    ]
    bodies, speeds, depths = [], [], []
    for q in slots:
        west, east = (around[own_row(table_ref, q, name)] for name in ("west", "east"))
        bodies.append(jnp.where(lane < SIDE, west, pltpu.roll(east, SIDE, 1)))
        aux = jnp.where(lane < SIDE, pltpu.roll(west, SIDE, 1), east)
        speeds.append(jnp.where(odd, row(aux, 1), row(aux, 0)))
        depths.append(row(aux, 2))
    side_near, side_far = across(*bodies)
    side_speed, side_depth = paired(*speeds), paired(*depths)
    keep = paired(*(own_row(table_ref, q, "live") for q in slots)) > 0

    def boundary(sign, halo_near, halo_far, halo_speed, halo_depth, own):
        (x_near, x_far), (speed_near, speed_far), (wet_near, wet_far), (share_near, share_far) = own
        outer = sign * (halo_speed + speed_near) * (wetness(halo_depth) * wet_near)
        inner = sign * (speed_near + speed_far) * (wet_near * wet_far)
        lost = jnp.minimum(inner, 0.0) * halo_near
        near = -(COURANT / 12.0) * wet_near * (flux(outer, x_far, x_near, halo_near, halo_far) + lost)
        far = (COURANT / 12.0) * wet_far * lost
        return near + share_near * (swap(near) - near), far + share_far * (swap(far) - far)

    edges = [edges_ref[n] for n in range(8)]
    rows = [edges_ref[8 + n] for n in range(16)]
    side_sign = jnp.where(lane < SIDE, -1.0, 1.0)
    side = boundary(side_sign, side_near, side_far, side_speed, side_depth, [edges[2 * n : 2 * n + 2] for n in range(4)])
    add_south = boundary(-1.0, *south, list(zip(rows[0:4], rows[4:8])))
    add_north = boundary(1.0, *north, list(zip(rows[8:12], rows[12:16])))
    pieces = {}
    for start, value in zip((0, IB, (JB - 1) * IB, (JB - 2) * IB), (*add_south, *add_north)):
        first, at = start // LANES, start % LANES
        moved = pltpu.roll(value, at, 1) if at else value
        pieces.setdefault(first, []).append((moved, (lane >= at) & (lane < at + IB)))
        if at + IB > LANES:
            pieces.setdefault(first + 1, []).append((moved, lane < at + IB - LANES))
    for t in range(TILES):
        kind, index = kind_ref[:, lanes_at(t)], spot_ref[:, lanes_at(t)]
        value = partial_ref[:, lanes_at(t)]
        value = value + jnp.where(kind == 1, take(side[0], index), jnp.where(kind == 2, take(side[1], index), 0.0))
        for moved, mask in pieces.get(t, []):
            value = value + jnp.where(mask, moved, 0.0)
        value = jnp.where(keep, value, 0.0)
        width = min(LANES, CELLS - t * LANES)
        out_ref[0, :, pl.ds(t * LANES, width)] = value[0:4, :width]
        out_ref[1, :, pl.ds(t * LANES, width)] = value[4:8, :width]


def finish(table, halo, beside, sides, partial, edges):
    vmem = pl.BlockSpec(memory_space=pltpu.VMEM)
    anywhere = pl.BlockSpec(memory_space=pltpu.HBM)
    return pl.pallas_call(
        finish_kernel,
        out_shape=jax.ShapeDtypeStruct((SLOTS, 4, CELLS), jnp.float32),
        in_specs=[pl.BlockSpec(memory_space=pltpu.SMEM)] + [vmem] * 3 + [anywhere] * 2,
        out_specs=anywhere,
        scratch_shapes=[
            pltpu.VMEM((2 * SLOTS + 5, 8, LANES), jnp.float32),
            pltpu.VMEM((PAIRS, 8, TILES * LANES), jnp.float32),
            pltpu.VMEM((PAIRS, EDGES, 8, LANES), jnp.float32),
            pltpu.VMEM((8, TILES * LANES), jnp.int32),
            pltpu.VMEM((8, TILES * LANES), jnp.int32),
            pltpu.VMEM((SLOTS, 4, CELLS), jnp.float32),
            pltpu.SemaphoreType.DMA((2, PAIRS)),
            pltpu.SemaphoreType.DMA((PAIRS,)),
        ],
        compiler_params=pltpu.CompilerParams(vmem_limit_bytes=BIG),
        name="final",
    )(table, halo, sides, beside, partial, edges)


def per_device(tracers, velocity, kappa, kmt, block_owner, neighbours, fold_partner):
    return finish(*exchange(block_owner, neighbours, fold_partner, tracers, velocity, kappa, kmt))


def solution(mesh):
    placed = (
        P(("blk", "sub"), None, None),
        P(("blk", "sub"), None, None),
        P(("blk", "sub"), None),
        P(("blk", "sub"), None),
        P(),
        P(),
        P(),
    )
    return jax.shard_map(
        per_device,
        mesh=mesh,
        in_specs=placed,
        out_specs=P(("blk", "sub"), None, None),
        check_vma=False,
    )
```

```python
import jax
import jax.numpy as jnp
from jax import lax
from jax.experimental import pallas as pl
from jax.experimental.pallas import tpu as pltpu
from jax.sharding import PartitionSpec as P

IB = 90
JB = 60
CELLS = IB * JB
SLOTS = 10
PAIRS = SLOTS // 2
DEVICES = 256
COURANT = 0.2
STRIDE = 4
HOPS = 7
LANES = 128
TILES = 43
FRAME = 47
SIDE = 64
PACK = SLOTS + 1
EXTRAS = 3
OWN_DOWN = HOPS * PACK
LOW_EXTRA = OWN_DOWN + PACK
OWN_UP = STRIDE * PACK
HIGH_EXTRA = OWN_UP + PACK
EMPTY = LOW_EXTRA + EXTRAS * PACK
WINDOW = EMPTY + 1
WANT = 2 * SLOTS + 2
TARGETS = STRIDE + HOPS
TABLE_ROWS = 112
EARLY = (0, 1, 3)
EDGES = 24
BIG = 63 << 20
FOLD_REACH = 14
MESH = pl.DeviceIdType.MESH
COLUMNS = ("behind", "ahead", "extra", "earlier", "later", "west", "east", "send_later", "send_earlier", "next", "previous", "fold", "live", "up")
AT = {name: number for number, name in enumerate(COLUMNS)}


def position():
    return lax.axis_index("blk") * 4 + lax.axis_index("sub")


def lanes_at(tile):
    return pl.ds(tile * LANES, LANES)


def iotas():
    return (
        lax.broadcasted_iota(jnp.int32, (8, LANES), 0),
        lax.broadcasted_iota(jnp.int32, (8, LANES), 1),
    )


def take(packed, index):
    return jnp.take_along_axis(packed, index, axis=1, mode="promise_in_bounds")


def row(value, number):
    return jnp.broadcast_to(value[number : number + 1], (8, LANES))


def table_of(owner_ref, near_ref, fold_ref, rows):
    me = position()
    strips = owner_ref.shape[0]
    number = lax.broadcasted_iota(jnp.int32, (rows, 1), 0).astype(jnp.float32)
    which = jnp.floor((number + 0.5) * (1.0 / SLOTS))
    slot = number - which * SLOTS
    onward = which < STRIDE
    hops = jnp.where(onward, which, which - STRIDE)
    device = jnp.where(onward, hops, -STRIDE * hops) + jnp.float32(1) * me
    device = jnp.where(device < 0, device + DEVICES, device)
    device = jnp.where(device >= DEVICES, device - DEVICES, device)
    code = device * SLOTS + slot
    wide = lax.broadcasted_iota(jnp.int32, (1, LANES), 1).astype(jnp.float32)

    def total(pieces):
        acc = jnp.zeros((rows, LANES), jnp.float32)
        for mask, value in pieces:
            acc = acc + jnp.where(mask, value, 0.0)
        return jnp.sum(acc, axis=1, keepdims=True)

    owners = [owner_ref[t : t + 1, :].astype(jnp.float32) for t in range(strips)]
    hits = [owner == code for owner in owners]
    first = device * SLOTS
    own_count = total([((owner >= first) & (owner < first + SLOTS), 1.0) for owner in owners])
    before_count = total([((owner >= first - SLOTS) & (owner < first), 1.0) for owner in owners])
    live = total([(hit, 1.0) for hit in hits])
    links = []
    for k in range(5):
        if k < 4:
            link = [near_ref[k : k + 1, lanes_at(t)].astype(jnp.float32) for t in range(strips)]
        else:
            link = [fold_ref[t : t + 1, :].astype(jnp.float32) for t in range(strips)]
        block = total([(hit, piece + 1.0) for hit, piece in zip(hits, link)]) - 1.0
        links.append(total([(block == wide + t * LANES, owner + 1.0) for t, owner in enumerate(owners)]) - 1.0)

    def where_is(other):
        source = jnp.floor((other + 0.5) * (1.0 / SLOTS))
        apart = source - device
        distance = jnp.abs(apart)
        far = jnp.floor((distance + 0.5) * (1.0 / STRIDE))
        rest = distance - far * STRIDE
        from_behind = (other >= 0) & (apart <= 0) & onward & (rest == hops)
        from_ahead = (other >= 0) & (apart >= 0) & ~onward & (far == hops)
        return source, other - source * SLOTS, apart, far, rest, from_behind, from_ahead

    vote = jnp.where(links[3] >= 0, jnp.where(links[3] > code, 1.0, -1.0), 0.0)
    vote = vote - jnp.where(links[2] >= 0, jnp.where(links[2] > code, 1.0, -1.0), 0.0)
    lean = count = jnp.zeros((1, LANES), jnp.float32)
    for t, owner in enumerate(owners):
        top = fold_ref[t : t + 1, :] >= 0
        lean = lean + jnp.where(top, owner - 0.5 * DEVICES * SLOTS, 0.0)
        count = count + jnp.where(top, 1.0, 0.0)
    lean, count = (jnp.sum(value, axis=1, keepdims=True) for value in (lean, count))
    vote = jnp.sum(vote, axis=0, keepdims=True)
    up = jnp.where(count > 0, lean, vote) >= 0
    empty = float(EMPTY)
    _, place, _, far, _, from_behind, _ = where_is(jnp.where(up, links[2], links[3]))
    behind = jnp.where(from_behind, far * PACK + place, empty)
    _, place, _, _, rest, _, from_ahead = where_is(jnp.where(up, links[3], links[2]))
    ahead = jnp.where(from_ahead, rest * PACK + place, empty)
    _, place, apart, far, rest, from_behind, from_ahead = where_is(links[4])
    against = jnp.where(rest > 0, HIGH_EXTRA + (rest - 1.0) * PACK, float(OWN_UP)) + place
    ahead = jnp.where(up & from_ahead, against, ahead)
    against = jnp.where(far > 0, LOW_EXTRA + (far - 1.0) * PACK, float(OWN_DOWN)) + place
    behind = jnp.where(~up & from_behind, against, behind)
    extra = jnp.where(up & from_behind & (apart < 0), far * PACK + place, empty)
    extra = jnp.where(~up & from_ahead & (apart > 0), rest * PACK + place, extra)
    sides = []
    columns = {"earlier": 0.0, "later": 0.0, "send_later": 0.0, "send_earlier": 0.0, "next": 0.0, "previous": 0.0}
    for side in range(2):
        other = links[side]
        source, place, apart, far, rest, from_behind, from_ahead = where_is(other)
        linked = other >= 0
        after = linked & (slot == own_count - 1.0) & (other == device * SLOTS + SLOTS)
        before = linked & (slot == 0) & (apart == -1) & (place + 1.0 == before_count)
        earlier = linked & (apart < 0) & ~before
        later = linked & (apart > 0) & ~after
        mine = slot * 2.0 + (side + 1.0)
        columns["earlier"] += jnp.where(earlier & from_behind, far * PACK + SLOTS - EMPTY, 0.0)
        columns["later"] += jnp.where(later & from_ahead, rest * PACK + SLOTS - EMPTY, 0.0)
        columns["send_later"] += jnp.where(later, mine, 0.0)
        columns["send_earlier"] += jnp.where(earlier, mine, 0.0)
        columns["next"] += jnp.where(after, mine, 0.0)
        columns["previous"] += jnp.where(before, mine, 0.0)
        index = jnp.where(linked & (apart == 0), place * 2.0 + (1.0 - side), 24.0)
        index = jnp.where(before, 20.0, jnp.where(after, 21.0, index))
        index = jnp.where(earlier, 22.0, jnp.where(later, 23.0, index))
        sides.append(jnp.clip(index, 0.0, 24.0))
    columns.update(
        behind=behind, ahead=ahead, extra=extra, west=sides[0], east=sides[1], live=live,
        fold=jnp.where(links[4] >= 0, 1.0, 0.0), up=jnp.where(up, 1.0, 0.0),
    )
    for name in ("behind", "ahead", "extra"):
        columns[name] = jnp.clip(columns[name], 0.0, empty)
    lane = lax.broadcasted_iota(jnp.int32, (rows, LANES), 1)
    result = jnp.zeros((rows, LANES), jnp.float32)
    for name, at in AT.items():
        result = jnp.where(lane == at, columns[name], result)
    own = number < SLOTS
    chosen = {
        name: jnp.sum(jnp.where(own, columns[name], 0.0), axis=0, keepdims=True)
        for name in ("send_later", "send_earlier", "next", "previous")
    }
    return result.astype(jnp.int32), up, chosen


def own_row(table_ref, slot, name):
    return table_ref[slot, AT[name]]


def load4(ref, half, t):
    if t < TILES - 1:
        return ref[half, :, lanes_at(t)]
    width = CELLS - t * LANES
    return jnp.pad(ref[half, :, pl.ds(t * LANES, width)], ((0, 0), (0, LANES - width)))


def load_rows(ref, t):
    if t < TILES - 1:
        return ref[:, lanes_at(t)]
    width = CELLS - t * LANES
    return jnp.pad(ref[:, pl.ds(t * LANES, width)], ((0, 0), (0, LANES - width)))


def line(tiles, start, lane):
    first = start // LANES
    r = start % LANES
    if r == 0:
        return tiles(first)
    amount = LANES - r
    return jnp.where(lane < amount, pltpu.roll(tiles(first), amount, 1), pltpu.roll(tiles(first + 1), amount, 1))


ROW_STARTS = (0, IB, (JB - 1) * IB, (JB - 2) * IB)


def pack_edges(fetch, loads, up, chosen, tracers_all, velocity_all, kmt_ref, up_ref, down_ref, next_ref, sides_ref, depth_rows):
    sub, lane = iotas()
    flag = jnp.broadcast_to(up, (8, LANES))
    column = lane % SIDE
    base_near = column * IB + jnp.where(lane >= SIDE, IB - 1, 0)
    base_far = column * IB + jnp.where(lane >= SIDE, IB - 2, 1)
    near_tile, near_at = base_near // LANES, base_near % LANES
    far_tile, far_at = base_far // LANES, base_far % LANES
    loads["kmt"].wait()
    near = jnp.zeros((16, LANES), jnp.float32)
    index16 = jnp.concatenate([near_at, near_at], axis=0)
    tile16 = jnp.concatenate([near_tile, near_tile], axis=0)

    def padded(t):
        return jnp.pad(load_rows(kmt_ref, t), ((0, 6), (0, 0)))

    for t in range(TILES):
        near = jnp.where(tile16 == t, take(padded(t), index16), near)
    south = padded(0)
    north = line(padded, (JB - 1) * IB, lane[0:1])
    for q in range(SLOTS):
        depth_rows[0, q] = row(south, q)
        depth_rows[1, q] = row(north, q)
        depth_rows[2, q] = row(near, q)
    aux_at = lane
    for s in range(8):
        move = {6: 28, 7: 14}.get(s, 90 if s % 2 == 0 else 52)
        aux_at = jnp.where((sub == s) & (lane >= IB), lane - move, aux_at)
    lane4 = lane[0:4]

    def one_pair(pair, carry):
        for copy in fetch(pair):
            copy.wait()
        tracers_ref, velocity_ref = tracers_all.at[pl.ds(2 * pair, 2)], velocity_all.at[pl.ds(2 * pair, 2)]
        for half in range(2):
            q = 2 * pair + half

            def tracer(t):
                return load4(tracers_ref, half, t)

            def speed(t):
                return load4(velocity_ref, half, t)

            packets = []
            for kind, (near, far) in enumerate(((0, 1), (JB - 1, JB - 2))):
                body = jnp.concatenate([line(tracer, near * IB, lane4), line(tracer, far * IB, lane4)], axis=0)
                v = line(speed, near * IB, lane4)
                v0, v1 = row(v, 2), row(v, 3)
                joint = jnp.where(lane >= 76, v0, pltpu.roll(v1, LANES - 14, 1))
                aux = jnp.where(sub == 6, joint, depth_rows[kind, q])
                aux = jnp.where(sub < 2, v0, jnp.where(sub < 4, v1, aux))
                packets.append(jnp.where(lane < IB, body, take(aux, aux_at)))
            up_ref[q] = jnp.where(flag, packets[1], packets[0])
            down_ref[q] = jnp.where(flag, packets[0], packets[1])
        near = far = drift = jnp.zeros((8, LANES), jnp.float32)
        for t in range(TILES):
            x = jnp.concatenate([load4(tracers_ref, 0, t), load4(tracers_ref, 1, t)], axis=0)
            v = jnp.concatenate([load4(velocity_ref, 0, t), load4(velocity_ref, 1, t)], axis=0)
            near = jnp.where(near_tile == t, take(x, near_at), near)
            far = jnp.where(far_tile == t, take(x, far_at), far)
            drift = jnp.where(near_tile == t, take(v, near_at), drift)
        for half in range(2):
            q = 2 * pair + half
            if half == 0:
                body = jnp.where(sub < 4, near, pltpu.roll(far, 4, 0))
                aux = drift
            else:
                body = jnp.where(sub < 4, pltpu.roll(near, 4, 0), far)
                aux = pltpu.roll(drift, 4, 0)
            aux = jnp.where(sub == 2, depth_rows[2, q], aux)
            sides_ref[2 * q] = jnp.where(lane < SIDE, body, pltpu.roll(aux, SIDE, 1))
            sides_ref[2 * q + 1] = jnp.where(lane < SIDE, pltpu.roll(body, SIDE, 1), aux)
        return carry

    lax.fori_loop(0, PAIRS, one_pair, 0)
    outputs = {"send_later": (up_ref, SLOTS), "send_earlier": (down_ref, SLOTS), "next": (next_ref, 0), "previous": (next_ref, 1)}
    for name, (ref, at) in outputs.items():
        which = jnp.broadcast_to(chosen[name], (8, LANES))
        packet = jnp.zeros((8, LANES), jnp.float32)
        for number in range(2 * SLOTS):
            packet = jnp.where(which == number + 1.0, sides_ref[number], packet)
        ref[at] = packet


def packet_shape(*lead):
    return jax.ShapeDtypeStruct(lead + (8, LANES), jnp.float32)


def coordinates(index):
    index = lax.rem(index + DEVICES, DEVICES)
    return (index // 4, lax.rem(index, 4))


PARTNERS = [sign * step for step in [1, 2, 3] + [STRIDE * a for a in range(1, HOPS)] for sign in (1, -1)]
HIGH, LOW = DEVICES - FOLD_REACH, FOLD_REACH


def exchange_kernel(owner_hbm, near_hbm, fold_hbm, tracers_hbm, velocity_hbm, kappa_hbm, kmt_hbm, out_hbm, table_out, halo_ref,
                    beside_ref, sides_ref, around, spot_ref, kind_ref, out_ref, up_ref, down_ref, next_ref, window, window_ahead, message,
                    extra_message, arrived, extra_arrived, send_sem, recv_sem, extra_send, extra_recv, low_send, low_recv, later_send, later_recv,
                    last_send, last_recv, owner_ref, near_ref, fold_ref, tracers_all, velocity_all, kappa_ref, kmt_ref,
                    depth_rows, table_ref, xs, us, vs, all_ds, all_ks, ws, gs, place_ref, partial_all, edges_all, load_sem,
                    pair_sem, out_sem):
    me = position()
    barrier = pltpu.get_barrier_semaphore()
    for offset in PARTNERS:
        pl.semaphore_signal(barrier, inc=1, device_id=coordinates(me + offset), device_id_type=MESH)
    sources = {
        "owner": (owner_hbm, owner_ref),
        "near": (near_hbm, near_ref),
        "fold": (fold_hbm, fold_ref),
        "kmt": (kmt_hbm, kmt_ref),
        "kappa": (kappa_hbm, kappa_ref),
    }
    loads = {
        name: pltpu.make_async_copy(source, target, load_sem.at[number])
        for number, (name, (source, target)) in enumerate(sources.items())
    }

    def fetch(pair):
        part = pl.ds(2 * pair, 2)
        return (
            pltpu.make_async_copy(tracers_hbm.at[part], tracers_all.at[part], pair_sem.at[0, pair]),
            pltpu.make_async_copy(velocity_hbm.at[part], velocity_all.at[part], pair_sem.at[1, pair]),
        )

    for name in ("owner", "near", "fold", "kmt"):
        loads[name].start()
    for pair in range(PAIRS):
        for copy in fetch(pair):
            copy.start()
    loads["kappa"].start()
    for name in ("owner", "near", "fold"):
        loads[name].wait()
    _, up, chosen = table_of(owner_ref, near_ref, fold_ref, 16)
    pack_edges(
        fetch, loads, up, chosen, tracers_all, velocity_all, kmt_ref, up_ref, down_ref, next_ref, sides_ref, depth_rows
    )
    pl.semaphore_wait(barrier, len(PARTNERS))

    def remote(source, target, sends, recvs, number, offset):
        return pltpu.make_async_remote_copy(
            src_ref=source,
            dst_ref=target,
            send_sem=sends.at[number],
            recv_sem=recvs.at[number],
            device_id=coordinates(me + offset),
            device_id_type=MESH,
        )

    plan = []
    for a in range(HOPS - 1, 0, -1):
        plan.append((up_ref, window.at[pl.ds(a * PACK, PACK)], STRIDE * a))
    plan.append((next_ref.at[0], beside_ref.at[0], 1))
    plan.append((next_ref.at[1], beside_ref.at[1], -1))
    first_down = len(plan)
    for a in (2, 1, 3):
        plan.append((down_ref, window_ahead.at[pl.ds(a * PACK, PACK)], -a))
    copies = [
        remote(source, target, send_sem, recv_sem, number, offset)
        for number, (source, target, offset) in enumerate(plan)
    ]
    for number in list(range(first_down, len(plan))) + list(range(first_down)):
        copies[number].start()

    def high_copy(k):
        target = window_ahead.at[pl.ds(HIGH_EXTRA + (k - 1) * PACK, PACK)]
        return remote(up_ref, target, extra_send, extra_recv, k - 1, -k)

    def low_copy(k):
        target = window.at[pl.ds(LOW_EXTRA + (k - 1) * PACK, PACK)]
        return remote(down_ref, target, low_send, low_recv, k - 1, STRIDE * k)

    def from_high(k):
        return (me + k >= HIGH) & (me + k < DEVICES)

    def from_low(k):
        return (me - STRIDE * k >= 0) & (me - STRIDE * k < LOW)

    nothing = jnp.zeros((PACK, 8, LANES), jnp.float32)
    for k in range(1, EXTRAS + 1):
        @pl.when(me >= HIGH)
        def _():
            high_copy(k).start()

        @pl.when(me < LOW)
        def _():
            low_copy(k).start()

        @pl.when(jnp.logical_not(from_high(k)))
        def _():
            window_ahead[pl.ds(HIGH_EXTRA + (k - 1) * PACK, PACK)] = nothing

        @pl.when(jnp.logical_not(from_low(k)))
        def _():
            window[pl.ds(LOW_EXTRA + (k - 1) * PACK, PACK)] = nothing

    window[pl.ds(0, PACK)] = up_ref[...]
    window[pl.ds(OWN_DOWN, PACK)] = down_ref[...]
    window[EMPTY] = jnp.zeros((8, LANES), jnp.float32)
    window_ahead[pl.ds(0, PACK)] = down_ref[...]
    window_ahead[pl.ds(OWN_UP, PACK)] = up_ref[...]
    for number in range(HIGH_EXTRA + EXTRAS * PACK, WINDOW):
        window_ahead[number] = jnp.zeros((8, LANES), jnp.float32)
    table, _, _ = table_of(owner_ref, near_ref, fold_ref, TABLE_ROWS)
    table_out[...] = table
    table_copy = pltpu.make_async_copy(table_out, table_ref, load_sem.at[len(sources)])
    table_copy.start()
    loads["kappa"].wait()
    prepare(kappa_ref, kmt_ref, xs, us, vs, all_ds, all_ks, place_ref, spot_ref, kind_ref)

    def one_pair(pair, carry):
        part = pl.ds(2 * pair, 2)
        interior(
            tracers_all.at[part], velocity_all.at[part], xs, us, vs, all_ds.at[pair], all_ks.at[pair], ws, gs,
            place_ref, partial_all.at[pair], edges_all.at[pair],
        )
        return carry

    def fill(number, halo_name, wrap_name):
        ref = window if number < STRIDE else window_ahead

        def picked(index):
            return ref[jnp.minimum(jnp.maximum(index, 0), EMPTY)]

        wrap = EMPTY
        for q in range(SLOTS):
            r = number * SLOTS + q
            message[number, q] = picked(table_ref[r, AT[halo_name]])
            wrap = wrap + table_ref[r, AT[wrap_name]]
        message[number, SLOTS] = picked(wrap)

    later = []

    def forward(numbers):
        for number in numbers:
            onward = number < STRIDE
            fill(number, *(("behind", "earlier") if onward else ("ahead", "later")))
            offset = number if onward else -STRIDE * (number - STRIDE)
            copy = remote(message.at[number], arrived.at[number], later_send, later_recv, number, offset)
            copy.start()
            later.append(copy)

    lax.fori_loop(EARLY[0], EARLY[1], one_pair, 0)
    table_copy.wait()
    for copy in copies[first_down:]:
        copy.wait_recv()
    for k in range(1, EXTRAS + 1):
        @pl.when(from_high(k))
        def _():
            high_copy(k).wait_recv()

    forward([STRIDE + a for a in range(HOPS - 1, 0, -1)])
    lax.fori_loop(EARLY[1], EARLY[2], one_pair, 0)
    for copy in copies[:first_down]:
        copy.wait_recv()
    for k in range(1, EXTRAS + 1):
        @pl.when(from_low(k))
        def _():
            low_copy(k).wait_recv()

    forward([2, 1, 3])

    def last_copy(k, onward):
        offset = k if onward else -STRIDE * k
        return remote(extra_message.at[k], extra_arrived.at[k], last_send, last_recv, k, offset)

    def extra_picked(ref, row_number):
        return ref[jnp.minimum(jnp.maximum(table_ref[row_number, AT["extra"]], 0), EMPTY)]

    for k in range(STRIDE):
        for goes, number, ref in ((from_high(k), k, window), (from_low(k), STRIDE + k, window_ahead)):
            @pl.when(goes)
            def _():
                for q in range(SLOTS):
                    extra_message[k, q] = extra_picked(ref, number * SLOTS + q)
                if k > 0:
                    last_copy(k, number < STRIDE).start()

    fill(0, "behind", "earlier")
    fill(STRIDE, "ahead", "later")
    lax.fori_loop(EARLY[2], PAIRS, one_pair, 0)
    for copy in later:
        copy.wait()
    for copy in copies:
        copy.wait_send()
    for k in range(1, EXTRAS + 1):
        @pl.when(me >= HIGH)
        def _():
            high_copy(k).wait_send()

        @pl.when(me < LOW)
        def _():
            low_copy(k).wait_send()

    flag = own_row(table_ref, 0, "up") > 0
    for q in range(PACK):
        behind = message[0, q]
        for number in range(1, STRIDE):
            behind = behind + arrived[number, q]
        ahead = message[STRIDE, q]
        for number in range(STRIDE + 1, TARGETS):
            ahead = ahead + arrived[number, q]
        if q < SLOTS:
            halo_ref[q] = jnp.where(flag, behind, ahead)
            halo_ref[SLOTS + q] = jnp.where(flag, ahead, behind)
        else:
            halo_ref[2 * SLOTS] = behind
            halo_ref[2 * SLOTS + 1] = ahead
    for k in range(1, STRIDE):
        for goes, onward in ((from_high(k), True), (from_low(k), False)):
            @pl.when(goes)
            def _():
                last_copy(k, onward).wait_send()

        for comes, onward in ((me >= HIGH, True), (me < LOW, False)):
            @pl.when(comes)
            def _():
                last_copy(k, onward).wait_recv()

    @pl.when((me >= HIGH) | (me < LOW))
    def _():
        for q in range(SLOTS):
            value = extra_message[0, q]
            for k in range(1, STRIDE):
                value = value + extra_arrived[k, q]
            halo_ref[SLOTS + q] = halo_ref[SLOTS + q] + value

    finish_all(table_ref, halo_ref, sides_ref, beside_ref, partial_all, edges_all, out_hbm, around, spot_ref, kind_ref, out_ref,
               out_sem)


def exchange(block_owner, neighbours, fold_partner, tracers, velocity, kappa, kmt):
    anywhere = pl.BlockSpec(memory_space=pltpu.HBM)

    def packets(*lead):
        return pltpu.VMEM(lead + (8, LANES), jnp.float32)

    def tiles(*lead):
        return pltpu.VMEM(lead[:-1] + (8, lead[-1] * LANES), jnp.float32)

    def sems(count):
        return [pltpu.SemaphoreType.DMA((count,))] * 2

    return pl.pallas_call(
        exchange_kernel,
        out_shape=jax.ShapeDtypeStruct((SLOTS, 4, CELLS), jnp.float32),
        in_specs=[anywhere] * 7,
        out_specs=anywhere,
        scratch_shapes=[
            pltpu.VMEM((TABLE_ROWS, LANES), jnp.int32),
            packets(WANT),
            packets(2),
            packets(2 * SLOTS),
            packets(2 * SLOTS + 5),
            pltpu.VMEM((8, TILES * LANES), jnp.int32),
            pltpu.VMEM((8, TILES * LANES), jnp.int32),
            pltpu.VMEM((SLOTS, 4, CELLS), jnp.float32),
            packets(PACK),
            packets(PACK),
            packets(2),
            packets(WINDOW),
            packets(WINDOW),
            packets(TARGETS, PACK),
            packets(STRIDE, SLOTS),
            packets(TARGETS, PACK),
            packets(STRIDE, SLOTS),
            *sems(HOPS - 1 + EXTRAS + 2),
            *sems(EXTRAS),
            *sems(EXTRAS),
            *sems(TARGETS),
            *sems(STRIDE),
            pltpu.VMEM((SLOTS, LANES), jnp.int32),
            pltpu.VMEM((4, SLOTS * LANES), jnp.int32),
            pltpu.VMEM((SLOTS, LANES), jnp.int32),
            pltpu.VMEM((SLOTS, 4, CELLS), jnp.float32),
            pltpu.VMEM((SLOTS, 4, CELLS), jnp.float32),
            pltpu.VMEM((SLOTS, CELLS), jnp.float32),
            pltpu.VMEM((SLOTS, CELLS), jnp.float32),
            packets(3, SLOTS),
            pltpu.SMEM((TABLE_ROWS, LANES), jnp.int32),
            tiles(FRAME),
            tiles(FRAME),
            tiles(FRAME),
            tiles(PAIRS, FRAME),
            tiles(PAIRS, TILES),
            tiles(TILES),
            tiles(TILES),
            pltpu.VMEM((8, TILES * LANES), jnp.int32),
            tiles(PAIRS, TILES),
            packets(PAIRS, EDGES),
            pltpu.SemaphoreType.DMA((6,)),
            pltpu.SemaphoreType.DMA((2, PAIRS)),
            pltpu.SemaphoreType.DMA((PAIRS,)),
        ],
        compiler_params=pltpu.CompilerParams(collective_id=0, has_side_effects=True, vmem_limit_bytes=BIG),
        name="exchange",
    )(block_owner.reshape(-1, LANES), neighbours.T, fold_partner.reshape(-1, LANES), tracers, velocity, kappa, kmt)


def flux(w, far_a, a, b, far_b):
    return jnp.maximum(w, 0.0) * (5.0 * a + 2.0 * b - far_a) + jnp.minimum(w, 0.0) * (2.0 * a + 5.0 * b - far_b)


def wetness(d):
    sub, _ = iotas()
    return jnp.clip(d - (sub % 2).astype(jnp.float32), 0.0, 1.0)


def swap(z):
    sub, _ = iotas()
    return jnp.where(sub % 2 == 1, pltpu.roll(z, 1, 0), pltpu.roll(z, 7, 0))


def place_of(t, lane):
    flat = lane + t * LANES
    j = ((flat.astype(jnp.float32) + 0.5) * (1.0 / IB)).astype(jnp.int32)
    return j, flat - j * IB


def prepare(kappa_ref, kmt_ref, xs, us, vs, all_ds, all_ks, place_ref, spot_ref, kind_ref):
    sub, lane = iotas()
    zero = jnp.zeros((8, LANES), jnp.float32)
    for t in (0, 1, 45, 46):
        for ref in (xs, us, vs):
            ref[:, lanes_at(t)] = zero
        for p in range(PAIRS):
            all_ds[p, :, lanes_at(t)] = zero

    def one_tile(t, rows_kappa, rows_kmt):
        j, i = place_of(t, lane)
        place_ref[:, lanes_at(t)] = i
        spot_ref[:, lanes_at(t)] = j + jnp.where(i >= IB // 2, SIDE, 0)
        kind_ref[:, lanes_at(t)] = jnp.where(
            (i == 0) | (i == IB - 1), 1, jnp.where((i == 1) | (i == IB - 2), 2, 0)
        )
        for p in range(PAIRS):
            for rows, ref, at in ((rows_kmt, all_ds, t + 2), (rows_kappa, all_ks, t)):
                ref[p, :, lanes_at(at)] = jnp.where(sub < 4, row(rows, 2 * p), row(rows, 2 * p + 1))

    for t in range(TILES):
        one_tile(t, load_rows(kappa_ref, t), load_rows(kmt_ref, t))


def interior(tracers_ref, velocity_ref, xs, us, vs, ds, ks, ws, gs, place_ref, partial_ref, edges_ref):
    sub, lane = iotas()
    lower_half = sub % 4 < 2
    column = lane % SIDE
    base_near = column * IB + jnp.where(lane >= SIDE, IB - 1, 0)
    base_far = column * IB + jnp.where(lane >= SIDE, IB - 2, 1)
    bases = (base_near // LANES, base_near % LANES), (base_far // LANES, base_far % LANES)
    for t in range(TILES):
        xs[:, lanes_at(t + 2)] = jnp.concatenate([load4(tracers_ref, 0, t), load4(tracers_ref, 1, t)], axis=0)
        speed = jnp.concatenate([load4(velocity_ref, 0, t), load4(velocity_ref, 1, t)], axis=0)
        us[:, lanes_at(t + 2)] = jnp.where(lower_half, speed, pltpu.roll(speed, 2, 0))
        vs[:, lanes_at(t + 2)] = jnp.where(lower_half, pltpu.roll(speed, 6, 0), speed)
    turned = {}

    def tile_of(name, ref, tile):
        if (name, tile, 0) not in turned:
            turned[name, tile, 0] = ref[:, lanes_at(tile)]
        return turned[name, tile, 0]

    def turn(name, ref, tile, r):
        if (name, tile, r) not in turned:
            turned[name, tile, r] = pltpu.roll(tile_of(name, ref, tile), LANES - r, 1)
        return turned[name, tile, r]

    def shift(name, ref, t, s):
        tile = t + 2 + s // LANES
        r = s % LANES
        return jnp.where(lane < LANES - r, turn(name, ref, tile, r), turn(name, ref, tile + 1, r))

    edges = [jnp.zeros((8, LANES), jnp.float32)] * 8
    for t in range(TILES):
        for key in [k for k in turned if k[1] < t]:
            del turned[key]
        i = place_ref[:, lanes_at(t)]
        x, u, v = (tile_of(name, ref, t + 2) for name, ref in (("x", xs), ("u", us), ("v", vs)))
        wet = wetness(tile_of("d", ds, t + 2))
        west = jnp.where(i == 0, 0.0, shift("x", xs, t, -1))
        west_far = jnp.where(i <= 1, 0.0, shift("x", xs, t, -2))
        east = jnp.where(i == IB - 1, 0.0, shift("x", xs, t, 1))
        east_far = jnp.where(i >= IB - 2, 0.0, shift("x", xs, t, 2))
        wet_west = jnp.where(i == 0, 0.0, wetness(shift("d", ds, t, -1)))
        wet_east = jnp.where(i == IB - 1, 0.0, wetness(shift("d", ds, t, 1)))
        wet_south = wetness(shift("d", ds, t, -IB))
        wet_north = wetness(shift("d", ds, t, IB))
        south, south_far = shift("x", xs, t, -IB), shift("x", xs, t, -2 * IB)
        north, north_far = shift("x", xs, t, IB), shift("x", xs, t, 2 * IB)
        flux_east = flux((u + shift("u", us, t, 1)) * (wet * wet_east), west, x, east, east_far)
        flux_west = flux((shift("u", us, t, -1) + u) * (wet_west * wet), west_far, west, x, east)
        flux_north = flux((v + shift("v", vs, t, IB)) * (wet * wet_north), south, x, north, north_far)
        flux_south = flux((shift("v", vs, t, -IB) + v) * (wet_south * wet), south_far, south, x, north)
        divergence = flux_east - flux_west + (flux_north - flux_south)
        explicit = x - (wet * (COURANT / 12.0)) * divergence
        coupling = ks[:, lanes_at(t)] * wet * swap(wet)
        share = coupling / (1.0 + 2.0 * coupling)
        partial_ref[:, lanes_at(t)] = explicit + share * (swap(explicit) - explicit)
        ws[:, lanes_at(t)] = wet
        gs[:, lanes_at(t)] = share
        for k, (tile, at) in enumerate(bases):
            here = tile == t
            for n, value in enumerate((x, u, wet, share)):
                edges[2 * n + k] = jnp.where(here, take(value, at), edges[2 * n + k])
    for n in range(8):
        edges_ref[n] = edges[n]
    for k, number in enumerate((0, 1, JB - 1, JB - 2)):
        for n, (ref, offset) in enumerate(((xs, 2), (vs, 2), (ws, 0), (gs, 0))):
            edges_ref[8 + 4 * k + n] = line(lambda t: ref[:, lanes_at(t + offset)], number * IB, lane)


def finish_all(table_ref, halo, sides_ref, beside_ref, partial_all, edges_all, out_hbm, around, spot_ref, kind_ref, out_ref,
               sems):
    for number in range(2 * SLOTS):
        around[number] = sides_ref[number]
    around[2 * SLOTS] = beside_ref[0]
    around[2 * SLOTS + 1] = beside_ref[1]
    around[2 * SLOTS + 2] = halo[2 * SLOTS]
    around[2 * SLOTS + 3] = halo[2 * SLOTS + 1]
    around[2 * SLOTS + 4] = jnp.zeros((8, LANES), jnp.float32)

    def store(pair):
        part = pl.ds(2 * pair, 2)
        return pltpu.make_async_copy(out_ref.at[part], out_hbm.at[part], sems.at[pair])

    def one_pair(pair, carry):
        finish_pair(
            pair, table_ref, halo, around, partial_all.at[pair], edges_all.at[pair], spot_ref, kind_ref,
            out_ref.at[pl.ds(2 * pair, 2)],
        )
        store(pair).start()
        return carry

    lax.fori_loop(0, PAIRS, one_pair, 0)
    for pair in range(PAIRS):
        store(pair).wait()


def finish_pair(pair, table_ref, halo, around, partial_ref, edges_ref, spot_ref, kind_ref, out_ref):
    sub, lane = iotas()
    upper = sub < 4
    odd = sub % 2 == 1

    def paired(first, second):
        return jnp.where(upper, first, second)

    def across(first, second):
        near = jnp.where(upper, first, pltpu.roll(second, 4, 0))
        return near, jnp.where(upper, pltpu.roll(first, 4, 0), second)

    def unpack(packet):
        a, b = pltpu.roll(packet, 38, 1), pltpu.roll(packet, 76, 1)
        c, d = pltpu.roll(packet, 100, 1), pltpu.roll(packet, 114, 1)

        def joined(first, second, third):
            return jnp.where(lane < 38, first, jnp.where(lane < 76, second, third))

        speed = jnp.where(odd, joined(row(a, 2), row(b, 3), row(d, 6)), joined(row(a, 0), row(b, 1), row(c, 6)))
        return speed, joined(row(a, 4), row(b, 5), row(d, 7))

    def rows_from(first, second):
        near, far = across(first, second)
        (speed_a, depth_a), (speed_b, depth_b) = unpack(first), unpack(second)
        return near, far, paired(speed_a, speed_b), paired(depth_a, depth_b)

    slots = (2 * pair, 2 * pair + 1)
    south = rows_from(halo[slots[0]], halo[slots[1]])
    north = rows_from(halo[SLOTS + slots[0]], halo[SLOTS + slots[1]])
    folded = paired(*(own_row(table_ref, q, "fold") for q in slots)) > 0
    back = jnp.where(lane < IB, IB - 1 - lane, lane)
    north = [
        jnp.where(folded, sign * take(value, back), value) for value, sign in zip(north, (1.0, 1.0, -1.0, 1.0))
    ]
    bodies, speeds, depths = [], [], []
    for q in slots:
        west, east = (around[jnp.minimum(jnp.maximum(own_row(table_ref, q, name), 0), 2 * SLOTS + 4)] for name in ("west", "east"))
        bodies.append(jnp.where(lane < SIDE, west, pltpu.roll(east, SIDE, 1)))
        aux = jnp.where(lane < SIDE, pltpu.roll(west, SIDE, 1), east)
        speeds.append(jnp.where(odd, row(aux, 1), row(aux, 0)))
        depths.append(row(aux, 2))
    side_near, side_far = across(*bodies)
    side_speed, side_depth = paired(*speeds), paired(*depths)
    keep = paired(*(own_row(table_ref, q, "live") for q in slots)) > 0

    def boundary(sign, halo_near, halo_far, halo_speed, halo_depth, own):
        (x_near, x_far), (speed_near, speed_far), (wet_near, wet_far), (share_near, share_far) = own
        outer = sign * (halo_speed + speed_near) * (wetness(halo_depth) * wet_near)
        inner = sign * (speed_near + speed_far) * (wet_near * wet_far)
        lost = jnp.minimum(inner, 0.0) * halo_near
        near = -(COURANT / 12.0) * wet_near * (flux(outer, x_far, x_near, halo_near, halo_far) + lost)
        far = (COURANT / 12.0) * wet_far * lost
        return near + share_near * (swap(near) - near), far + share_far * (swap(far) - far)

    edges = [edges_ref[n] for n in range(8)]
    rows = [edges_ref[8 + n] for n in range(16)]
    side_sign = jnp.where(lane < SIDE, -1.0, 1.0)
    side = boundary(side_sign, side_near, side_far, side_speed, side_depth, [edges[2 * n : 2 * n + 2] for n in range(4)])
    add_south = boundary(-1.0, *south, list(zip(rows[0:4], rows[4:8])))
    add_north = boundary(1.0, *north, list(zip(rows[8:12], rows[12:16])))
    pieces = {}
    for start, value in zip((0, IB, (JB - 1) * IB, (JB - 2) * IB), (*add_south, *add_north)):
        first, at = start // LANES, start % LANES
        moved = pltpu.roll(value, at, 1) if at else value
        pieces.setdefault(first, []).append((moved, (lane >= at) & (lane < at + IB)))
        if at + IB > LANES:
            pieces.setdefault(first + 1, []).append((moved, lane < at + IB - LANES))
    for t in range(TILES):
        kind, index = kind_ref[:, lanes_at(t)], spot_ref[:, lanes_at(t)]
        value = partial_ref[:, lanes_at(t)]
        value = value + jnp.where(kind == 1, take(side[0], index), jnp.where(kind == 2, take(side[1], index), 0.0))
        for moved, mask in pieces.get(t, []):
            value = value + jnp.where(mask, moved, 0.0)
        value = jnp.where(keep, value, 0.0)
        width = min(LANES, CELLS - t * LANES)
        out_ref[0, :, pl.ds(t * LANES, width)] = value[0:4, :width]
        out_ref[1, :, pl.ds(t * LANES, width)] = value[4:8, :width]


def per_device(tracers, velocity, kappa, kmt, block_owner, neighbours, fold_partner):
    return exchange(block_owner, neighbours, fold_partner, tracers, velocity, kappa, kmt)


def solution(mesh):
    placed = (
        P(("blk", "sub"), None, None),
        P(("blk", "sub"), None, None),
        P(("blk", "sub"), None),
        P(("blk", "sub"), None),
        P(),
        P(),
        P(),
    )
    return jax.shard_map(
        per_device,
        mesh=mesh,
        in_specs=placed,
        out_specs=P(("blk", "sub"), None, None),
        check_vma=False,
    )
```

```python
import jax
import jax.numpy as jnp
from jax import lax
from jax.experimental import pallas as pl
from jax.experimental.pallas import tpu as pltpu
from jax.sharding import PartitionSpec as P

IB = 90
JB = 60
CELLS = IB * JB
SLOTS = 10
PAIRS = SLOTS // 2
DEVICES = 256
COURANT = 0.2
STRIDE = 4
HOPS = 7
LANES = 128
TILES = 43
FRAME = 47
SIDE = 64
PACK = SLOTS + 1
EXTRAS = 3
OWN_DOWN = HOPS * PACK
LOW_EXTRA = OWN_DOWN + PACK
OWN_UP = STRIDE * PACK
HIGH_EXTRA = OWN_UP + PACK
EMPTY = LOW_EXTRA + EXTRAS * PACK
WINDOW = EMPTY + 1
WANT = 2 * SLOTS + 2
TARGETS = STRIDE + HOPS
TABLE_ROWS = 112
EARLY = (0, 2, 4)
EDGES = 24
BIG = 63 << 20
FOLD_REACH = 14
MESH = pl.DeviceIdType.MESH
COLUMNS = ("behind", "ahead", "extra", "earlier", "later", "west", "east", "send_later", "send_earlier", "next", "previous", "fold", "live", "up")
AT = {name: number for number, name in enumerate(COLUMNS)}


def position():
    return lax.axis_index("blk") * 4 + lax.axis_index("sub")


def lanes_at(tile):
    return pl.ds(tile * LANES, LANES)


def iotas():
    return (
        lax.broadcasted_iota(jnp.int32, (8, LANES), 0),
        lax.broadcasted_iota(jnp.int32, (8, LANES), 1),
    )


def take(packed, index):
    return jnp.take_along_axis(packed, index, axis=1, mode="promise_in_bounds")


def row(value, number):
    return jnp.broadcast_to(value[number : number + 1], (8, LANES))


def table_of(owner_ref, near_ref, fold_ref, rows):
    me = position()
    strips = owner_ref.shape[0]
    number = lax.broadcasted_iota(jnp.int32, (rows, 1), 0).astype(jnp.float32)
    which = jnp.floor((number + 0.5) * (1.0 / SLOTS))
    slot = number - which * SLOTS
    onward = which < STRIDE
    hops = jnp.where(onward, which, which - STRIDE)
    device = jnp.where(onward, hops, -STRIDE * hops) + jnp.float32(1) * me
    device = jnp.where(device < 0, device + DEVICES, device)
    device = jnp.where(device >= DEVICES, device - DEVICES, device)
    code = device * SLOTS + slot
    wide = lax.broadcasted_iota(jnp.int32, (1, LANES), 1).astype(jnp.float32)

    def total(pieces):
        acc = jnp.zeros((rows, LANES), jnp.float32)
        for mask, value in pieces:
            acc = acc + jnp.where(mask, value, 0.0)
        return jnp.sum(acc, axis=1, keepdims=True)

    owners = [owner_ref[t : t + 1, :].astype(jnp.float32) for t in range(strips)]
    hits = [owner == code for owner in owners]
    first = device * SLOTS
    own_count = total([((owner >= first) & (owner < first + SLOTS), 1.0) for owner in owners])
    before_count = total([((owner >= first - SLOTS) & (owner < first), 1.0) for owner in owners])
    live = total([(hit, 1.0) for hit in hits])
    links = []
    for k in range(5):
        if k < 4:
            link = [near_ref[k : k + 1, lanes_at(t)].astype(jnp.float32) for t in range(strips)]
        else:
            link = [fold_ref[t : t + 1, :].astype(jnp.float32) for t in range(strips)]
        block = total([(hit, piece + 1.0) for hit, piece in zip(hits, link)]) - 1.0
        links.append(total([(block == wide + t * LANES, owner + 1.0) for t, owner in enumerate(owners)]) - 1.0)

    def where_is(other):
        source = jnp.floor((other + 0.5) * (1.0 / SLOTS))
        apart = source - device
        distance = jnp.abs(apart)
        far = jnp.floor((distance + 0.5) * (1.0 / STRIDE))
        rest = distance - far * STRIDE
        from_behind = (other >= 0) & (apart <= 0) & onward & (rest == hops)
        from_ahead = (other >= 0) & (apart >= 0) & ~onward & (far == hops)
        return source, other - source * SLOTS, apart, far, rest, from_behind, from_ahead

    vote = jnp.where(links[3] >= 0, jnp.where(links[3] > code, 1.0, -1.0), 0.0)
    vote = vote - jnp.where(links[2] >= 0, jnp.where(links[2] > code, 1.0, -1.0), 0.0)
    lean = count = jnp.zeros((1, LANES), jnp.float32)
    for t, owner in enumerate(owners):
        top = fold_ref[t : t + 1, :] >= 0
        lean = lean + jnp.where(top, owner - 0.5 * DEVICES * SLOTS, 0.0)
        count = count + jnp.where(top, 1.0, 0.0)
    lean, count = (jnp.sum(value, axis=1, keepdims=True) for value in (lean, count))
    vote = jnp.sum(vote, axis=0, keepdims=True)
    up = jnp.where(count > 0, lean, vote) >= 0
    empty = float(EMPTY)
    _, place, _, far, _, from_behind, _ = where_is(jnp.where(up, links[2], links[3]))
    behind = jnp.where(from_behind, far * PACK + place, empty)
    _, place, _, _, rest, _, from_ahead = where_is(jnp.where(up, links[3], links[2]))
    ahead = jnp.where(from_ahead, rest * PACK + place, empty)
    _, place, apart, far, rest, from_behind, from_ahead = where_is(links[4])
    against = jnp.where(rest > 0, HIGH_EXTRA + (rest - 1.0) * PACK, float(OWN_UP)) + place
    ahead = jnp.where(up & from_ahead, against, ahead)
    against = jnp.where(far > 0, LOW_EXTRA + (far - 1.0) * PACK, float(OWN_DOWN)) + place
    behind = jnp.where(~up & from_behind, against, behind)
    extra = jnp.where(up & from_behind & (apart < 0), far * PACK + place, empty)
    extra = jnp.where(~up & from_ahead & (apart > 0), rest * PACK + place, extra)
    sides = []
    columns = {"earlier": 0.0, "later": 0.0, "send_later": 0.0, "send_earlier": 0.0, "next": 0.0, "previous": 0.0}
    for side in range(2):
        other = links[side]
        source, place, apart, far, rest, from_behind, from_ahead = where_is(other)
        linked = other >= 0
        after = linked & (slot == own_count - 1.0) & (other == device * SLOTS + SLOTS)
        before = linked & (slot == 0) & (apart == -1) & (place + 1.0 == before_count)
        earlier = linked & (apart < 0) & ~before
        later = linked & (apart > 0) & ~after
        mine = slot * 2.0 + (side + 1.0)
        columns["earlier"] += jnp.where(earlier & from_behind, far * PACK + SLOTS - EMPTY, 0.0)
        columns["later"] += jnp.where(later & from_ahead, rest * PACK + SLOTS - EMPTY, 0.0)
        columns["send_later"] += jnp.where(later, mine, 0.0)
        columns["send_earlier"] += jnp.where(earlier, mine, 0.0)
        columns["next"] += jnp.where(after, mine, 0.0)
        columns["previous"] += jnp.where(before, mine, 0.0)
        index = jnp.where(linked & (apart == 0), place * 2.0 + (1.0 - side), 24.0)
        index = jnp.where(before, 20.0, jnp.where(after, 21.0, index))
        index = jnp.where(earlier, 22.0, jnp.where(later, 23.0, index))
        sides.append(jnp.clip(index, 0.0, 24.0))
    columns.update(
        behind=behind, ahead=ahead, extra=extra, west=sides[0], east=sides[1], live=live,
        fold=jnp.where(links[4] >= 0, 1.0, 0.0), up=jnp.where(up, 1.0, 0.0),
    )
    for name in ("behind", "ahead", "extra"):
        columns[name] = jnp.clip(columns[name], 0.0, empty)
    lane = lax.broadcasted_iota(jnp.int32, (rows, LANES), 1)
    result = jnp.zeros((rows, LANES), jnp.float32)
    for name, at in AT.items():
        result = jnp.where(lane == at, columns[name], result)
    own = number < SLOTS
    chosen = {
        name: jnp.sum(jnp.where(own, columns[name], 0.0), axis=0, keepdims=True)
        for name in ("send_later", "send_earlier", "next", "previous")
    }
    return result.astype(jnp.int32), up, chosen


def own_row(table_ref, slot, name):
    return table_ref[slot, AT[name]]


def load4(ref, half, t):
    if t < TILES - 1:
        return ref[half, :, lanes_at(t)]
    width = CELLS - t * LANES
    return jnp.pad(ref[half, :, pl.ds(t * LANES, width)], ((0, 0), (0, LANES - width)))


def load_rows(ref, t):
    if t < TILES - 1:
        return ref[:, lanes_at(t)]
    width = CELLS - t * LANES
    return jnp.pad(ref[:, pl.ds(t * LANES, width)], ((0, 0), (0, LANES - width)))


def line(tiles, start, lane):
    first = start // LANES
    r = start % LANES
    if r == 0:
        return tiles(first)
    amount = LANES - r
    return jnp.where(lane < amount, pltpu.roll(tiles(first), amount, 1), pltpu.roll(tiles(first + 1), amount, 1))


ROW_STARTS = (0, IB, (JB - 1) * IB, (JB - 2) * IB)


def pack_edges(fetch, loads, up, chosen, tracers_all, velocity_all, kmt_ref, up_ref, down_ref, next_ref, sides_ref, depth_rows, edges_all):
    sub, lane = iotas()
    flag = jnp.broadcast_to(up, (8, LANES))
    column = lane % SIDE
    base_near = column * IB + jnp.where(lane >= SIDE, IB - 1, 0)
    base_far = column * IB + jnp.where(lane >= SIDE, IB - 2, 1)
    near_tile, near_at = base_near // LANES, base_near % LANES
    far_tile, far_at = base_far // LANES, base_far % LANES
    loads["kmt"].wait()
    near = jnp.zeros((16, LANES), jnp.float32)
    index16 = jnp.concatenate([near_at, near_at], axis=0)
    tile16 = jnp.concatenate([near_tile, near_tile], axis=0)

    def padded(t):
        return jnp.pad(load_rows(kmt_ref, t), ((0, 6), (0, 0)))

    for t in range(TILES):
        near = jnp.where(tile16 == t, take(padded(t), index16), near)
    south = padded(0)
    north = line(padded, (JB - 1) * IB, lane[0:1])
    for q in range(SLOTS):
        depth_rows[0, q] = row(south, q)
        depth_rows[1, q] = row(north, q)
        depth_rows[2, q] = row(near, q)
    aux_at = lane
    for s in range(8):
        move = {6: 28, 7: 14}.get(s, 90 if s % 2 == 0 else 52)
        aux_at = jnp.where((sub == s) & (lane >= IB), lane - move, aux_at)
    lane4 = lane[0:4]

    def one_pair(pair, carry):
        for copy in fetch(pair):
            copy.wait()
        tracers_ref, velocity_ref = tracers_all.at[pl.ds(2 * pair, 2)], velocity_all.at[pl.ds(2 * pair, 2)]
        for half in range(2):
            q = 2 * pair + half

            def tracer(t):
                return load4(tracers_ref, half, t)

            def speed(t):
                return load4(velocity_ref, half, t)

            packets = []
            for kind, (near, far) in enumerate(((0, 1), (JB - 1, JB - 2))):
                body = jnp.concatenate([line(tracer, near * IB, lane4), line(tracer, far * IB, lane4)], axis=0)
                v = line(speed, near * IB, lane4)
                v0, v1 = row(v, 2), row(v, 3)
                joint = jnp.where(lane >= 76, v0, pltpu.roll(v1, LANES - 14, 1))
                aux = jnp.where(sub == 6, joint, depth_rows[kind, q])
                aux = jnp.where(sub < 2, v0, jnp.where(sub < 4, v1, aux))
                packets.append(jnp.where(lane < IB, body, take(aux, aux_at)))
            up_ref[q] = jnp.where(flag, packets[1], packets[0])
            down_ref[q] = jnp.where(flag, packets[0], packets[1])
        near = far = drift = jnp.zeros((8, LANES), jnp.float32)
        for t in range(TILES):
            x = jnp.concatenate([load4(tracers_ref, 0, t), load4(tracers_ref, 1, t)], axis=0)
            v = jnp.concatenate([load4(velocity_ref, 0, t), load4(velocity_ref, 1, t)], axis=0)
            near = jnp.where(near_tile == t, take(x, near_at), near)
            far = jnp.where(far_tile == t, take(x, far_at), far)
            drift = jnp.where(near_tile == t, take(v, near_at), drift)
        edges_all[pair, 0] = near
        edges_all[pair, 1] = far
        edges_all[pair, 2] = jnp.where(sub % 4 < 2, drift, pltpu.roll(drift, 2, 0))
        for half in range(2):
            q = 2 * pair + half
            if half == 0:
                body = jnp.where(sub < 4, near, pltpu.roll(far, 4, 0))
                aux = drift
            else:
                body = jnp.where(sub < 4, pltpu.roll(near, 4, 0), far)
                aux = pltpu.roll(drift, 4, 0)
            aux = jnp.where(sub == 2, depth_rows[2, q], aux)
            sides_ref[2 * q] = jnp.where(lane < SIDE, body, pltpu.roll(aux, SIDE, 1))
            sides_ref[2 * q + 1] = jnp.where(lane < SIDE, pltpu.roll(body, SIDE, 1), aux)
        return carry

    lax.fori_loop(0, PAIRS, one_pair, 0)
    outputs = {"send_later": (up_ref, SLOTS), "send_earlier": (down_ref, SLOTS), "next": (next_ref, 0), "previous": (next_ref, 1)}
    for name, (ref, at) in outputs.items():
        which = jnp.broadcast_to(chosen[name], (8, LANES))
        packet = jnp.zeros((8, LANES), jnp.float32)
        for number in range(2 * SLOTS):
            packet = jnp.where(which == number + 1.0, sides_ref[number], packet)
        ref[at] = packet


def packet_shape(*lead):
    return jax.ShapeDtypeStruct(lead + (8, LANES), jnp.float32)


def coordinates(index):
    index = lax.rem(index + DEVICES, DEVICES)
    return (index // 4, lax.rem(index, 4))


PARTNERS = [sign * step for step in [1, 2, 3] + [STRIDE * a for a in range(1, HOPS)] for sign in (1, -1)]
HIGH, LOW = DEVICES - FOLD_REACH, FOLD_REACH


def exchange_kernel(owner_hbm, near_hbm, fold_hbm, tracers_hbm, velocity_hbm, kappa_hbm, kmt_hbm, out_hbm, table_out, halo_ref,
                    beside_ref, sides_ref, around, spot_ref, kind_ref, out_ref, up_ref, down_ref, next_ref, window, window_ahead, message,
                    extra_message, arrived, extra_arrived, send_sem, recv_sem, extra_send, extra_recv, low_send, low_recv, later_send, later_recv,
                    last_send, last_recv, owner_ref, near_ref, fold_ref, tracers_all, velocity_all, kappa_ref, kmt_ref,
                    depth_rows, table_ref, xs, us, vs, all_ds, all_ks, gs, fe, fn, place_ref, partial_all, edges_all, load_sem,
                    pair_sem, out_sem):
    me = position()
    barrier = pltpu.get_barrier_semaphore()
    for offset in PARTNERS:
        pl.semaphore_signal(barrier, inc=1, device_id=coordinates(me + offset), device_id_type=MESH)
    sources = {
        "owner": (owner_hbm, owner_ref),
        "near": (near_hbm, near_ref),
        "fold": (fold_hbm, fold_ref),
        "kmt": (kmt_hbm, kmt_ref),
        "kappa": (kappa_hbm, kappa_ref),
    }
    loads = {
        name: pltpu.make_async_copy(source, target, load_sem.at[number])
        for number, (name, (source, target)) in enumerate(sources.items())
    }

    def fetch(pair):
        part = pl.ds(2 * pair, 2)
        return (
            pltpu.make_async_copy(tracers_hbm.at[part], tracers_all.at[part], pair_sem.at[0, pair]),
            pltpu.make_async_copy(velocity_hbm.at[part], velocity_all.at[part], pair_sem.at[1, pair]),
        )

    for name in ("owner", "near", "fold", "kmt"):
        loads[name].start()
    for pair in range(PAIRS):
        for copy in fetch(pair):
            copy.start()
    loads["kappa"].start()
    for name in ("owner", "near", "fold"):
        loads[name].wait()
    _, up, chosen = table_of(owner_ref, near_ref, fold_ref, 16)
    pack_edges(
        fetch, loads, up, chosen, tracers_all, velocity_all, kmt_ref, up_ref, down_ref, next_ref, sides_ref, depth_rows,
        edges_all,
    )
    pl.semaphore_wait(barrier, len(PARTNERS))

    def remote(source, target, sends, recvs, number, offset):
        return pltpu.make_async_remote_copy(
            src_ref=source,
            dst_ref=target,
            send_sem=sends.at[number],
            recv_sem=recvs.at[number],
            device_id=coordinates(me + offset),
            device_id_type=MESH,
        )

    plan = []
    for a in range(HOPS - 1, 0, -1):
        plan.append((up_ref, window.at[pl.ds(a * PACK, PACK)], STRIDE * a))
    plan.append((next_ref.at[0], beside_ref.at[0], 1))
    plan.append((next_ref.at[1], beside_ref.at[1], -1))
    first_down = len(plan)
    for a in (2, 1, 3):
        plan.append((down_ref, window_ahead.at[pl.ds(a * PACK, PACK)], -a))
    copies = [
        remote(source, target, send_sem, recv_sem, number, offset)
        for number, (source, target, offset) in enumerate(plan)
    ]
    for number in list(range(first_down, len(plan))) + list(range(first_down)):
        copies[number].start()

    def high_copy(k):
        target = window_ahead.at[pl.ds(HIGH_EXTRA + (k - 1) * PACK, PACK)]
        return remote(up_ref, target, extra_send, extra_recv, k - 1, -k)

    def low_copy(k):
        target = window.at[pl.ds(LOW_EXTRA + (k - 1) * PACK, PACK)]
        return remote(down_ref, target, low_send, low_recv, k - 1, STRIDE * k)

    def from_high(k):
        return (me + k >= HIGH) & (me + k < DEVICES)

    def from_low(k):
        return (me - STRIDE * k >= 0) & (me - STRIDE * k < LOW)

    nothing = jnp.zeros((PACK, 8, LANES), jnp.float32)
    for k in range(1, EXTRAS + 1):
        @pl.when(me >= HIGH)
        def _():
            high_copy(k).start()

        @pl.when(me < LOW)
        def _():
            low_copy(k).start()

        @pl.when(jnp.logical_not(from_high(k)))
        def _():
            window_ahead[pl.ds(HIGH_EXTRA + (k - 1) * PACK, PACK)] = nothing

        @pl.when(jnp.logical_not(from_low(k)))
        def _():
            window[pl.ds(LOW_EXTRA + (k - 1) * PACK, PACK)] = nothing

    window[pl.ds(0, PACK)] = up_ref[...]
    window[pl.ds(OWN_DOWN, PACK)] = down_ref[...]
    window[EMPTY] = jnp.zeros((8, LANES), jnp.float32)
    window_ahead[pl.ds(0, PACK)] = down_ref[...]
    window_ahead[pl.ds(OWN_UP, PACK)] = up_ref[...]
    for number in range(HIGH_EXTRA + EXTRAS * PACK, WINDOW):
        window_ahead[number] = jnp.zeros((8, LANES), jnp.float32)
    table, _, _ = table_of(owner_ref, near_ref, fold_ref, TABLE_ROWS)
    table_out[...] = table
    table_copy = pltpu.make_async_copy(table_out, table_ref, load_sem.at[len(sources)])
    table_copy.start()
    loads["kappa"].wait()
    prepare(kappa_ref, kmt_ref, xs, us, vs, all_ds, all_ks, fe, fn, place_ref, spot_ref, kind_ref)

    def one_pair(pair, carry):
        part = pl.ds(2 * pair, 2)
        interior(
            tracers_all.at[part], velocity_all.at[part], xs, us, vs, all_ds.at[pair], all_ks.at[pair], gs, fe, fn,
            place_ref, partial_all.at[pair], edges_all.at[pair],
        )
        return carry

    def fill(number, halo_name, wrap_name):
        ref = window if number < STRIDE else window_ahead

        def picked(index):
            return ref[jnp.minimum(jnp.maximum(index, 0), EMPTY)]

        wrap = EMPTY
        for q in range(SLOTS):
            r = number * SLOTS + q
            message[number, q] = picked(table_ref[r, AT[halo_name]])
            wrap = wrap + table_ref[r, AT[wrap_name]]
        message[number, SLOTS] = picked(wrap)

    later = []

    def forward(numbers):
        for number in numbers:
            onward = number < STRIDE
            fill(number, *(("behind", "earlier") if onward else ("ahead", "later")))
            offset = number if onward else -STRIDE * (number - STRIDE)
            copy = remote(message.at[number], arrived.at[number], later_send, later_recv, number, offset)
            copy.start()
            later.append(copy)

    lax.fori_loop(EARLY[0], EARLY[1], one_pair, 0)
    table_copy.wait()
    for copy in copies[first_down:]:
        copy.wait_recv()
    for k in range(1, EXTRAS + 1):
        @pl.when(from_high(k))
        def _():
            high_copy(k).wait_recv()

    forward([STRIDE + a for a in range(HOPS - 1, 0, -1)])
    lax.fori_loop(EARLY[1], EARLY[2], one_pair, 0)
    for copy in copies[:first_down]:
        copy.wait_recv()
    for k in range(1, EXTRAS + 1):
        @pl.when(from_low(k))
        def _():
            low_copy(k).wait_recv()

    forward([2, 1, 3])

    def last_copy(k, onward):
        offset = k if onward else -STRIDE * k
        return remote(extra_message.at[k], extra_arrived.at[k], last_send, last_recv, k, offset)

    def extra_picked(ref, row_number):
        return ref[jnp.minimum(jnp.maximum(table_ref[row_number, AT["extra"]], 0), EMPTY)]

    for k in range(STRIDE):
        for goes, number, ref in ((from_high(k), k, window), (from_low(k), STRIDE + k, window_ahead)):
            @pl.when(goes)
            def _():
                for q in range(SLOTS):
                    extra_message[k, q] = extra_picked(ref, number * SLOTS + q)
                if k > 0:
                    last_copy(k, number < STRIDE).start()

    fill(0, "behind", "earlier")
    fill(STRIDE, "ahead", "later")
    lax.fori_loop(EARLY[2], PAIRS, one_pair, 0)
    for copy in later:
        copy.wait()
    for copy in copies:
        copy.wait_send()
    for k in range(1, EXTRAS + 1):
        @pl.when(me >= HIGH)
        def _():
            high_copy(k).wait_send()

        @pl.when(me < LOW)
        def _():
            low_copy(k).wait_send()

    flag = own_row(table_ref, 0, "up") > 0
    for q in range(PACK):
        behind = message[0, q]
        for number in range(1, STRIDE):
            behind = behind + arrived[number, q]
        ahead = message[STRIDE, q]
        for number in range(STRIDE + 1, TARGETS):
            ahead = ahead + arrived[number, q]
        if q < SLOTS:
            halo_ref[q] = jnp.where(flag, behind, ahead)
            halo_ref[SLOTS + q] = jnp.where(flag, ahead, behind)
        else:
            halo_ref[2 * SLOTS] = behind
            halo_ref[2 * SLOTS + 1] = ahead
    for k in range(1, STRIDE):
        for goes, onward in ((from_high(k), True), (from_low(k), False)):
            @pl.when(goes)
            def _():
                last_copy(k, onward).wait_send()

        for comes, onward in ((me >= HIGH, True), (me < LOW, False)):
            @pl.when(comes)
            def _():
                last_copy(k, onward).wait_recv()

    @pl.when((me >= HIGH) | (me < LOW))
    def _():
        for q in range(SLOTS):
            value = extra_message[0, q]
            for k in range(1, STRIDE):
                value = value + extra_arrived[k, q]
            halo_ref[SLOTS + q] = halo_ref[SLOTS + q] + value

    finish_all(table_ref, halo_ref, sides_ref, beside_ref, partial_all, edges_all, out_hbm, around, spot_ref, kind_ref, out_ref,
               out_sem)


def exchange(block_owner, neighbours, fold_partner, tracers, velocity, kappa, kmt):
    anywhere = pl.BlockSpec(memory_space=pltpu.HBM)

    def packets(*lead):
        return pltpu.VMEM(lead + (8, LANES), jnp.float32)

    def tiles(*lead):
        return pltpu.VMEM(lead[:-1] + (8, lead[-1] * LANES), jnp.float32)

    def sems(count):
        return [pltpu.SemaphoreType.DMA((count,))] * 2

    return pl.pallas_call(
        exchange_kernel,
        out_shape=jax.ShapeDtypeStruct((SLOTS, 4, CELLS), jnp.float32),
        in_specs=[anywhere] * 7,
        out_specs=anywhere,
        scratch_shapes=[
            pltpu.VMEM((TABLE_ROWS, LANES), jnp.int32),
            packets(WANT),
            packets(2),
            packets(2 * SLOTS),
            packets(2 * SLOTS + 5),
            pltpu.VMEM((8, TILES * LANES), jnp.int32),
            pltpu.VMEM((8, TILES * LANES), jnp.int32),
            pltpu.VMEM((SLOTS, 4, CELLS), jnp.float32),
            packets(PACK),
            packets(PACK),
            packets(2),
            packets(WINDOW),
            packets(WINDOW),
            packets(TARGETS, PACK),
            packets(STRIDE, SLOTS),
            packets(TARGETS, PACK),
            packets(STRIDE, SLOTS),
            *sems(HOPS - 1 + EXTRAS + 2),
            *sems(EXTRAS),
            *sems(EXTRAS),
            *sems(TARGETS),
            *sems(STRIDE),
            pltpu.VMEM((SLOTS, LANES), jnp.int32),
            pltpu.VMEM((4, SLOTS * LANES), jnp.int32),
            pltpu.VMEM((SLOTS, LANES), jnp.int32),
            pltpu.VMEM((SLOTS, 4, CELLS), jnp.float32),
            pltpu.VMEM((SLOTS, 4, CELLS), jnp.float32),
            pltpu.VMEM((SLOTS, CELLS), jnp.float32),
            pltpu.VMEM((SLOTS, CELLS), jnp.float32),
            packets(3, SLOTS),
            pltpu.SMEM((TABLE_ROWS, LANES), jnp.int32),
            tiles(FRAME),
            tiles(FRAME),
            tiles(FRAME),
            tiles(PAIRS, FRAME),
            tiles(PAIRS, TILES),
            tiles(TILES),
            tiles(TILES + 1),
            tiles(TILES + 1),
            pltpu.VMEM((8, TILES * LANES), jnp.int32),
            tiles(PAIRS, TILES),
            packets(PAIRS, EDGES),
            pltpu.SemaphoreType.DMA((6,)),
            pltpu.SemaphoreType.DMA((2, PAIRS)),
            pltpu.SemaphoreType.DMA((PAIRS,)),
        ],
        compiler_params=pltpu.CompilerParams(collective_id=0, has_side_effects=True, vmem_limit_bytes=BIG),
        name="exchange",
    )(block_owner.reshape(-1, LANES), neighbours.T, fold_partner.reshape(-1, LANES), tracers, velocity, kappa, kmt)


def flux(w, far_a, a, b, far_b):
    return jnp.maximum(w, 0.0) * (5.0 * a + 2.0 * b - far_a) + jnp.minimum(w, 0.0) * (2.0 * a + 5.0 * b - far_b)


def wetness(d):
    sub, _ = iotas()
    return jnp.clip(d - (sub % 2).astype(jnp.float32), 0.0, 1.0)


def swap(z):
    sub, _ = iotas()
    return jnp.where(sub % 2 == 1, pltpu.roll(z, 1, 0), pltpu.roll(z, 7, 0))


def place_of(t, lane):
    flat = lane + t * LANES
    j = ((flat.astype(jnp.float32) + 0.5) * (1.0 / IB)).astype(jnp.int32)
    return j, flat - j * IB


def prepare(kappa_ref, kmt_ref, xs, us, vs, all_ds, all_ks, fe, fn, place_ref, spot_ref, kind_ref):
    sub, lane = iotas()
    zero = jnp.zeros((8, LANES), jnp.float32)
    fe[:, lanes_at(0)] = zero
    fn[:, lanes_at(0)] = zero
    for t in (0, 1, 45, 46):
        for ref in (xs, us, vs):
            ref[:, lanes_at(t)] = zero
        for p in range(PAIRS):
            all_ds[p, :, lanes_at(t)] = zero

    def one_tile(t, rows_kappa, rows_kmt):
        j, i = place_of(t, lane)
        place_ref[:, lanes_at(t)] = i
        spot_ref[:, lanes_at(t)] = j + jnp.where(i >= IB // 2, SIDE, 0)
        kind_ref[:, lanes_at(t)] = jnp.where(
            (i == 0) | (i == IB - 1), 1, jnp.where((i == 1) | (i == IB - 2), 2, 0)
        )
        for p in range(PAIRS):
            depth = jnp.where(sub < 4, row(rows_kmt, 2 * p), row(rows_kmt, 2 * p + 1))
            all_ds[p, :, lanes_at(t + 2)] = wetness(depth)
            all_ks[p, :, lanes_at(t)] = jnp.where(sub < 4, row(rows_kappa, 2 * p), row(rows_kappa, 2 * p + 1))

    for t in range(TILES):
        one_tile(t, load_rows(kappa_ref, t), load_rows(kmt_ref, t))


def interior(tracers_ref, velocity_ref, xs, us, vs, ds, ks, gs, fe, fn, place_ref, partial_ref, edges_ref):
    sub, lane = iotas()
    lower_half = sub % 4 < 2
    column = lane % SIDE
    base_near = column * IB + jnp.where(lane >= SIDE, IB - 1, 0)
    base_far = column * IB + jnp.where(lane >= SIDE, IB - 2, 1)
    bases = (base_near // LANES, base_near % LANES), (base_far // LANES, base_far % LANES)
    for t in range(TILES):
        xs[:, lanes_at(t + 2)] = jnp.concatenate([load4(tracers_ref, 0, t), load4(tracers_ref, 1, t)], axis=0)
        speed = jnp.concatenate([load4(velocity_ref, 0, t), load4(velocity_ref, 1, t)], axis=0)
        us[:, lanes_at(t + 2)] = jnp.where(lower_half, speed, pltpu.roll(speed, 2, 0))
        vs[:, lanes_at(t + 2)] = jnp.where(lower_half, pltpu.roll(speed, 6, 0), speed)
    turned = {}

    def tile_of(name, ref, tile):
        if (name, tile, 0) not in turned:
            turned[name, tile, 0] = ref[:, lanes_at(tile)]
        return turned[name, tile, 0]

    def turn(name, ref, tile, r):
        if (name, tile, r) not in turned:
            turned[name, tile, r] = pltpu.roll(tile_of(name, ref, tile), LANES - r, 1)
        return turned[name, tile, r]

    def shift(name, ref, t, s):
        tile = t + 2 + s // LANES
        r = s % LANES
        return jnp.where(lane < LANES - r, turn(name, ref, tile, r), turn(name, ref, tile + 1, r))

    zero = jnp.zeros((8, LANES), jnp.float32)
    edges = [zero] * 5
    for t in range(TILES):
        for key in [k for k in turned if k[1] < t]:
            del turned[key]
        i = place_ref[:, lanes_at(t)]
        x, u, v, wet = (
            tile_of(name, ref, t + 2) for name, ref in (("x", xs), ("u", us), ("v", vs), ("d", ds))
        )
        last = i == IB - 1
        west = jnp.where(i == 0, 0.0, shift("x", xs, t, -1))
        east = jnp.where(last, 0.0, shift("x", xs, t, 1))
        east_far = jnp.where(i >= IB - 2, 0.0, shift("x", xs, t, 2))
        wet_east = jnp.where(last, 0.0, shift("d", ds, t, 1))
        wet_north = shift("d", ds, t, IB)
        south, north, north_far = (shift("x", xs, t, s) for s in (-IB, IB, 2 * IB))
        flux_east = flux((u + shift("u", us, t, 1)) * (wet * wet_east), west, x, east, east_far)
        flux_north = flux((v + shift("v", vs, t, IB)) * (wet * wet_north), south, x, north, north_far)
        fe[:, lanes_at(t + 1)] = flux_east
        fn[:, lanes_at(t + 1)] = flux_north
    back = {}

    def turned_flux(name, ref, tile, amount):
        if (name, tile) not in back:
            back[name, tile] = pltpu.roll(ref[:, lanes_at(tile)], amount, 1)
        return back[name, tile]

    for t in range(TILES):
        i = place_ref[:, lanes_at(t)]
        x, u, wet = (ref[:, lanes_at(t + 2)] for ref in (xs, us, ds))
        flux_east, flux_north = fe[:, lanes_at(t + 1)], fn[:, lanes_at(t + 1)]
        flux_west = jnp.where(lane < 1, turned_flux("e", fe, t, 1), turned_flux("e", fe, t + 1, 1))
        flux_west = jnp.where(i == 0, 0.0, flux_west)
        flux_south = jnp.where(lane < IB, turned_flux("n", fn, t, IB), turned_flux("n", fn, t + 1, IB))
        divergence = flux_east - flux_west + (flux_north - flux_south)
        explicit = x - (wet * (COURANT / 12.0)) * divergence
        coupling = ks[:, lanes_at(t)] * wet * swap(wet)
        share = coupling / (1.0 + 2.0 * coupling)
        partial_ref[:, lanes_at(t)] = explicit + share * (swap(explicit) - explicit)
        gs[:, lanes_at(t)] = share
        values = ((1, u), (0, wet), (1, wet), (0, share), (1, share))
        for n, (k, value) in enumerate(values):
            tile, at = bases[k]
            edges[n] = jnp.where(tile == t, take(value, at), edges[n])
    for n in range(5):
        edges_ref[3 + n] = edges[n]
    for k, number in enumerate((0, 1, JB - 1, JB - 2)):
        for n, (ref, offset) in enumerate(((xs, 2), (vs, 2), (ds, 2), (gs, 0))):
            edges_ref[8 + 4 * k + n] = line(lambda t: ref[:, lanes_at(t + offset)], number * IB, lane)


def finish_all(table_ref, halo, sides_ref, beside_ref, partial_all, edges_all, out_hbm, around, spot_ref, kind_ref, out_ref,
               sems):
    for number in range(2 * SLOTS):
        around[number] = sides_ref[number]
    around[2 * SLOTS] = beside_ref[0]
    around[2 * SLOTS + 1] = beside_ref[1]
    around[2 * SLOTS + 2] = halo[2 * SLOTS]
    around[2 * SLOTS + 3] = halo[2 * SLOTS + 1]
    around[2 * SLOTS + 4] = jnp.zeros((8, LANES), jnp.float32)

    def store(pair):
        part = pl.ds(2 * pair, 2)
        return pltpu.make_async_copy(out_ref.at[part], out_hbm.at[part], sems.at[pair])

    def one_pair(pair, carry):
        finish_pair(
            pair, table_ref, halo, around, partial_all.at[pair], edges_all.at[pair], spot_ref, kind_ref,
            out_ref.at[pl.ds(2 * pair, 2)],
        )
        store(pair).start()
        return carry

    lax.fori_loop(0, PAIRS, one_pair, 0)
    for pair in range(PAIRS):
        store(pair).wait()


def finish_pair(pair, table_ref, halo, around, partial_ref, edges_ref, spot_ref, kind_ref, out_ref):
    sub, lane = iotas()
    upper = sub < 4
    odd = sub % 2 == 1

    def paired(first, second):
        return jnp.where(upper, first, second)

    def across(first, second):
        near = jnp.where(upper, first, pltpu.roll(second, 4, 0))
        return near, jnp.where(upper, pltpu.roll(first, 4, 0), second)

    def unpack(packet):
        a, b = pltpu.roll(packet, 38, 1), pltpu.roll(packet, 76, 1)
        c, d = pltpu.roll(packet, 100, 1), pltpu.roll(packet, 114, 1)

        def joined(first, second, third):
            return jnp.where(lane < 38, first, jnp.where(lane < 76, second, third))

        speed = jnp.where(odd, joined(row(a, 2), row(b, 3), row(d, 6)), joined(row(a, 0), row(b, 1), row(c, 6)))
        return speed, joined(row(a, 4), row(b, 5), row(d, 7))

    def rows_from(first, second):
        near, far = across(first, second)
        (speed_a, depth_a), (speed_b, depth_b) = unpack(first), unpack(second)
        return near, far, paired(speed_a, speed_b), paired(depth_a, depth_b)

    slots = (2 * pair, 2 * pair + 1)
    south = rows_from(halo[slots[0]], halo[slots[1]])
    north = rows_from(halo[SLOTS + slots[0]], halo[SLOTS + slots[1]])
    folded = paired(*(own_row(table_ref, q, "fold") for q in slots)) > 0
    back = jnp.where(lane < IB, IB - 1 - lane, lane)
    north = [
        jnp.where(folded, sign * take(value, back), value) for value, sign in zip(north, (1.0, 1.0, -1.0, 1.0))
    ]
    bodies, speeds, depths = [], [], []
    for q in slots:
        west, east = (around[jnp.minimum(jnp.maximum(own_row(table_ref, q, name), 0), 2 * SLOTS + 4)] for name in ("west", "east"))
        bodies.append(jnp.where(lane < SIDE, west, pltpu.roll(east, SIDE, 1)))
        aux = jnp.where(lane < SIDE, pltpu.roll(west, SIDE, 1), east)
        speeds.append(jnp.where(odd, row(aux, 1), row(aux, 0)))
        depths.append(row(aux, 2))
    side_near, side_far = across(*bodies)
    side_speed, side_depth = paired(*speeds), paired(*depths)
    keep = paired(*(own_row(table_ref, q, "live") for q in slots)) > 0

    def boundary(sign, halo_near, halo_far, halo_speed, halo_depth, own):
        (x_near, x_far), (speed_near, speed_far), (wet_near, wet_far), (share_near, share_far) = own
        outer = sign * (halo_speed + speed_near) * (wetness(halo_depth) * wet_near)
        inner = sign * (speed_near + speed_far) * (wet_near * wet_far)
        lost = jnp.minimum(inner, 0.0) * halo_near
        near = -(COURANT / 12.0) * wet_near * (flux(outer, x_far, x_near, halo_near, halo_far) + lost)
        far = (COURANT / 12.0) * wet_far * lost
        return near + share_near * (swap(near) - near), far + share_far * (swap(far) - far)

    edges = [edges_ref[n] for n in range(8)]
    rows = [edges_ref[8 + n] for n in range(16)]
    side_sign = jnp.where(lane < SIDE, -1.0, 1.0)
    side = boundary(side_sign, side_near, side_far, side_speed, side_depth, [edges[2 * n : 2 * n + 2] for n in range(4)])
    add_south = boundary(-1.0, *south, list(zip(rows[0:4], rows[4:8])))
    add_north = boundary(1.0, *north, list(zip(rows[8:12], rows[12:16])))
    pieces = {}
    for start, value in zip((0, IB, (JB - 1) * IB, (JB - 2) * IB), (*add_south, *add_north)):
        first, at = start // LANES, start % LANES
        moved = pltpu.roll(value, at, 1) if at else value
        pieces.setdefault(first, []).append((moved, (lane >= at) & (lane < at + IB)))
        if at + IB > LANES:
            pieces.setdefault(first + 1, []).append((moved, lane < at + IB - LANES))
    for t in range(TILES):
        kind, index = kind_ref[:, lanes_at(t)], spot_ref[:, lanes_at(t)]
        value = partial_ref[:, lanes_at(t)]
        value = value + jnp.where(kind == 1, take(side[0], index), jnp.where(kind == 2, take(side[1], index), 0.0))
        for moved, mask in pieces.get(t, []):
            value = value + jnp.where(mask, moved, 0.0)
        value = jnp.where(keep, value, 0.0)
        width = min(LANES, CELLS - t * LANES)
        out_ref[0, :, pl.ds(t * LANES, width)] = value[0:4, :width]
        out_ref[1, :, pl.ds(t * LANES, width)] = value[4:8, :width]


def per_device(tracers, velocity, kappa, kmt, block_owner, neighbours, fold_partner):
    return exchange(block_owner, neighbours, fold_partner, tracers, velocity, kappa, kmt)


def solution(mesh):
    placed = (
        P(("blk", "sub"), None, None),
        P(("blk", "sub"), None, None),
        P(("blk", "sub"), None),
        P(("blk", "sub"), None),
        P(),
        P(),
        P(),
    )
    return jax.shard_map(
        per_device,
        mesh=mesh,
        in_specs=placed,
        out_specs=P(("blk", "sub"), None, None),
        check_vma=False,
    )
```

```python
import jax
import jax.numpy as jnp
from jax import lax
from jax.experimental import pallas as pl
from jax.experimental.pallas import tpu as pltpu
from jax.sharding import PartitionSpec as P

IB = 90
JB = 60
CELLS = IB * JB
SLOTS = 10
PAIRS = SLOTS // 2
DEVICES = 256
COURANT = 0.2
STRIDE = 4
HOPS = 7
LANES = 128
TILES = 43
FRAME = 47
SIDE = 64
PACK = SLOTS + 1
EXTRAS = 3
OWN_DOWN = HOPS * PACK
LOW_EXTRA = OWN_DOWN + PACK
OWN_UP = STRIDE * PACK
HIGH_EXTRA = OWN_UP + PACK
EMPTY = LOW_EXTRA + EXTRAS * PACK
WINDOW = EMPTY + 1
WANT = 2 * SLOTS + 2
TARGETS = STRIDE + HOPS
TABLE_ROWS = 112
EARLY = (0, 2, 4)
EDGES = 24
BIG = 63 << 20
FOLD_REACH = 14
MESH = pl.DeviceIdType.MESH
COLUMNS = ("behind", "ahead", "extra", "earlier", "later", "west", "east", "send_later", "send_earlier", "next", "previous", "fold", "live", "up")
AT = {name: number for number, name in enumerate(COLUMNS)}


def position():
    return lax.axis_index("blk") * 4 + lax.axis_index("sub")


def lanes_at(tile):
    return pl.ds(tile * LANES, LANES)


def iotas():
    return (
        lax.broadcasted_iota(jnp.int32, (8, LANES), 0),
        lax.broadcasted_iota(jnp.int32, (8, LANES), 1),
    )


def take(packed, index):
    return jnp.take_along_axis(packed, index, axis=1, mode="promise_in_bounds")


def row(value, number):
    return jnp.broadcast_to(value[number : number + 1], (8, LANES))


def table_of(owner_ref, near_ref, fold_ref, rows):
    me = position()
    strips = owner_ref.shape[0]
    number = lax.broadcasted_iota(jnp.int32, (rows, 1), 0).astype(jnp.float32)
    which = jnp.floor((number + 0.5) * (1.0 / SLOTS))
    slot = number - which * SLOTS
    onward = which < STRIDE
    hops = jnp.where(onward, which, which - STRIDE)
    device = jnp.where(onward, hops, -STRIDE * hops) + jnp.float32(1) * me
    device = jnp.where(device < 0, device + DEVICES, device)
    device = jnp.where(device >= DEVICES, device - DEVICES, device)
    code = device * SLOTS + slot
    wide = lax.broadcasted_iota(jnp.int32, (1, LANES), 1).astype(jnp.float32)

    def total(pieces):
        acc = jnp.zeros((rows, LANES), jnp.float32)
        for mask, value in pieces:
            acc = acc + jnp.where(mask, value, 0.0)
        return jnp.sum(acc, axis=1, keepdims=True)

    owners = [owner_ref[t : t + 1, :].astype(jnp.float32) for t in range(strips)]
    hits = [owner == code for owner in owners]
    first = device * SLOTS
    own_count = total([((owner >= first) & (owner < first + SLOTS), 1.0) for owner in owners])
    before_count = total([((owner >= first - SLOTS) & (owner < first), 1.0) for owner in owners])
    live = total([(hit, 1.0) for hit in hits])
    links = []
    for k in range(5):
        if k < 4:
            link = [near_ref[k : k + 1, lanes_at(t)].astype(jnp.float32) for t in range(strips)]
        else:
            link = [fold_ref[t : t + 1, :].astype(jnp.float32) for t in range(strips)]
        block = total([(hit, piece + 1.0) for hit, piece in zip(hits, link)]) - 1.0
        links.append(total([(block == wide + t * LANES, owner + 1.0) for t, owner in enumerate(owners)]) - 1.0)

    def where_is(other):
        source = jnp.floor((other + 0.5) * (1.0 / SLOTS))
        apart = source - device
        distance = jnp.abs(apart)
        far = jnp.floor((distance + 0.5) * (1.0 / STRIDE))
        rest = distance - far * STRIDE
        from_behind = (other >= 0) & (apart <= 0) & onward & (rest == hops)
        from_ahead = (other >= 0) & (apart >= 0) & ~onward & (far == hops)
        return source, other - source * SLOTS, apart, far, rest, from_behind, from_ahead

    vote = jnp.where(links[3] >= 0, jnp.where(links[3] > code, 1.0, -1.0), 0.0)
    vote = vote - jnp.where(links[2] >= 0, jnp.where(links[2] > code, 1.0, -1.0), 0.0)
    lean = count = jnp.zeros((1, LANES), jnp.float32)
    for t, owner in enumerate(owners):
        top = fold_ref[t : t + 1, :] >= 0
        lean = lean + jnp.where(top, owner - 0.5 * DEVICES * SLOTS, 0.0)
        count = count + jnp.where(top, 1.0, 0.0)
    lean, count = (jnp.sum(value, axis=1, keepdims=True) for value in (lean, count))
    vote = jnp.sum(vote, axis=0, keepdims=True)
    up = jnp.where(count > 0, lean, vote) >= 0
    empty = float(EMPTY)
    _, place, _, far, _, from_behind, _ = where_is(jnp.where(up, links[2], links[3]))
    behind = jnp.where(from_behind, far * PACK + place, empty)
    _, place, _, _, rest, _, from_ahead = where_is(jnp.where(up, links[3], links[2]))
    ahead = jnp.where(from_ahead, rest * PACK + place, empty)
    _, place, apart, far, rest, from_behind, from_ahead = where_is(links[4])
    against = jnp.where(rest > 0, HIGH_EXTRA + (rest - 1.0) * PACK, float(OWN_UP)) + place
    ahead = jnp.where(up & from_ahead, against, ahead)
    against = jnp.where(far > 0, LOW_EXTRA + (far - 1.0) * PACK, float(OWN_DOWN)) + place
    behind = jnp.where(~up & from_behind, against, behind)
    extra = jnp.where(up & from_behind & (apart < 0), far * PACK + place, empty)
    extra = jnp.where(~up & from_ahead & (apart > 0), rest * PACK + place, extra)
    sides = []
    columns = {"earlier": 0.0, "later": 0.0, "send_later": 0.0, "send_earlier": 0.0, "next": 0.0, "previous": 0.0}
    for side in range(2):
        other = links[side]
        source, place, apart, far, rest, from_behind, from_ahead = where_is(other)
        linked = other >= 0
        after = linked & (slot == own_count - 1.0) & (other == device * SLOTS + SLOTS)
        before = linked & (slot == 0) & (apart == -1) & (place + 1.0 == before_count)
        earlier = linked & (apart < 0) & ~before
        later = linked & (apart > 0) & ~after
        mine = slot * 2.0 + (side + 1.0)
        columns["earlier"] += jnp.where(earlier & from_behind, far * PACK + SLOTS - EMPTY, 0.0)
        columns["later"] += jnp.where(later & from_ahead, rest * PACK + SLOTS - EMPTY, 0.0)
        columns["send_later"] += jnp.where(later, mine, 0.0)
        columns["send_earlier"] += jnp.where(earlier, mine, 0.0)
        columns["next"] += jnp.where(after, mine, 0.0)
        columns["previous"] += jnp.where(before, mine, 0.0)
        index = jnp.where(linked & (apart == 0), place * 2.0 + (1.0 - side), 24.0)
        index = jnp.where(before, 20.0, jnp.where(after, 21.0, index))
        index = jnp.where(earlier, 22.0, jnp.where(later, 23.0, index))
        sides.append(jnp.clip(index, 0.0, 24.0))
    columns.update(
        behind=behind, ahead=ahead, extra=extra, west=sides[0], east=sides[1], live=live,
        fold=jnp.where(links[4] >= 0, 1.0, 0.0), up=jnp.where(up, 1.0, 0.0),
    )
    for name in ("behind", "ahead", "extra"):
        columns[name] = jnp.clip(columns[name], 0.0, empty)
    lane = lax.broadcasted_iota(jnp.int32, (rows, LANES), 1)
    result = jnp.zeros((rows, LANES), jnp.float32)
    for name, at in AT.items():
        result = jnp.where(lane == at, columns[name], result)
    own = number < SLOTS
    chosen = {
        name: jnp.sum(jnp.where(own, columns[name], 0.0), axis=0, keepdims=True)
        for name in ("send_later", "send_earlier", "next", "previous")
    }
    return result.astype(jnp.int32), up, chosen


def own_row(table_ref, slot, name):
    return table_ref[slot, AT[name]]


def load4(ref, half, t):
    if t < TILES - 1:
        return ref[half, :, lanes_at(t)]
    width = CELLS - t * LANES
    return jnp.pad(ref[half, :, pl.ds(t * LANES, width)], ((0, 0), (0, LANES - width)))


def load_rows(ref, t):
    if t < TILES - 1:
        return ref[:, lanes_at(t)]
    width = CELLS - t * LANES
    return jnp.pad(ref[:, pl.ds(t * LANES, width)], ((0, 0), (0, LANES - width)))


def line(tiles, start, lane):
    first = start // LANES
    r = start % LANES
    if r == 0:
        return tiles(first)
    amount = LANES - r
    return jnp.where(lane < amount, pltpu.roll(tiles(first), amount, 1), pltpu.roll(tiles(first + 1), amount, 1))


ROW_STARTS = (0, IB, (JB - 1) * IB, (JB - 2) * IB)


def pack_edges(fetch, loads, up, chosen, tracers_all, velocity_all, kmt_ref, up_ref, down_ref, next_ref, sides_ref, depth_rows, edges_all):
    sub, lane = iotas()
    flag = jnp.broadcast_to(up, (8, LANES))
    column = lane % SIDE
    base_near = column * IB + jnp.where(lane >= SIDE, IB - 1, 0)
    base_far = column * IB + jnp.where(lane >= SIDE, IB - 2, 1)
    near_tile, near_at = base_near // LANES, base_near % LANES
    far_tile, far_at = base_far // LANES, base_far % LANES
    loads["kmt"].wait()
    near = jnp.zeros((16, LANES), jnp.float32)
    index16 = jnp.concatenate([near_at, near_at], axis=0)
    tile16 = jnp.concatenate([near_tile, near_tile], axis=0)

    def padded(t):
        return jnp.pad(load_rows(kmt_ref, t), ((0, 6), (0, 0)))

    for t in range(TILES):
        near = jnp.where(tile16 == t, take(padded(t), index16), near)
    south = padded(0)
    north = line(padded, (JB - 1) * IB, lane[0:1])
    for q in range(SLOTS):
        depth_rows[0, q] = row(south, q)
        depth_rows[1, q] = row(north, q)
        depth_rows[2, q] = row(near, q)
    aux_at = lane
    for s in range(8):
        move = {6: 28, 7: 14}.get(s, 90 if s % 2 == 0 else 52)
        aux_at = jnp.where((sub == s) & (lane >= IB), lane - move, aux_at)
    lane4 = lane[0:4]

    def one_pair(pair, carry):
        for copy in fetch(pair):
            copy.wait()
        tracers_ref, velocity_ref = tracers_all.at[pl.ds(2 * pair, 2)], velocity_all.at[pl.ds(2 * pair, 2)]
        for half in range(2):
            q = 2 * pair + half

            def tracer(t):
                return load4(tracers_ref, half, t)

            def speed(t):
                return load4(velocity_ref, half, t)

            packets = []
            for kind, (near, far) in enumerate(((0, 1), (JB - 1, JB - 2))):
                body = jnp.concatenate([line(tracer, near * IB, lane4), line(tracer, far * IB, lane4)], axis=0)
                v = line(speed, near * IB, lane4)
                v0, v1 = row(v, 2), row(v, 3)
                joint = jnp.where(lane >= 76, v0, pltpu.roll(v1, LANES - 14, 1))
                aux = jnp.where(sub == 6, joint, depth_rows[kind, q])
                aux = jnp.where(sub < 2, v0, jnp.where(sub < 4, v1, aux))
                packets.append(jnp.where(lane < IB, body, take(aux, aux_at)))
            up_ref[q] = jnp.where(flag, packets[1], packets[0])
            down_ref[q] = jnp.where(flag, packets[0], packets[1])
        near = far = drift = jnp.zeros((8, LANES), jnp.float32)
        for t in range(TILES):
            x = jnp.concatenate([load4(tracers_ref, 0, t), load4(tracers_ref, 1, t)], axis=0)
            v = jnp.concatenate([load4(velocity_ref, 0, t), load4(velocity_ref, 1, t)], axis=0)
            near = jnp.where(near_tile == t, take(x, near_at), near)
            far = jnp.where(far_tile == t, take(x, far_at), far)
            drift = jnp.where(near_tile == t, take(v, near_at), drift)
        edges_all[pair, 0] = near
        edges_all[pair, 1] = far
        edges_all[pair, 2] = jnp.where(sub % 4 < 2, drift, pltpu.roll(drift, 2, 0))
        for half in range(2):
            q = 2 * pair + half
            if half == 0:
                body = jnp.where(sub < 4, near, pltpu.roll(far, 4, 0))
                aux = drift
            else:
                body = jnp.where(sub < 4, pltpu.roll(near, 4, 0), far)
                aux = pltpu.roll(drift, 4, 0)
            aux = jnp.where(sub == 2, depth_rows[2, q], aux)
            sides_ref[2 * q] = jnp.where(lane < SIDE, body, pltpu.roll(aux, SIDE, 1))
            sides_ref[2 * q + 1] = jnp.where(lane < SIDE, pltpu.roll(body, SIDE, 1), aux)
        return carry

    for pair in range(PAIRS):
        one_pair(pair, 0)
    outputs = {"send_later": (up_ref, SLOTS), "send_earlier": (down_ref, SLOTS), "next": (next_ref, 0), "previous": (next_ref, 1)}
    for name, (ref, at) in outputs.items():
        which = jnp.broadcast_to(chosen[name], (8, LANES))
        packet = jnp.zeros((8, LANES), jnp.float32)
        for number in range(2 * SLOTS):
            packet = jnp.where(which == number + 1.0, sides_ref[number], packet)
        ref[at] = packet


def packet_shape(*lead):
    return jax.ShapeDtypeStruct(lead + (8, LANES), jnp.float32)


def coordinates(index):
    index = lax.rem(index + DEVICES, DEVICES)
    return (index // 4, lax.rem(index, 4))


PARTNERS = [sign * step for step in [1, 2, 3] + [STRIDE * a for a in range(1, HOPS)] for sign in (1, -1)]
HIGH, LOW = DEVICES - FOLD_REACH, FOLD_REACH


def exchange_kernel(owner_hbm, near_hbm, fold_hbm, tracers_hbm, velocity_hbm, kappa_hbm, kmt_hbm, out_hbm, table_out, halo_ref,
                    beside_ref, sides_ref, around, spot_ref, kind_ref, out_ref, up_ref, down_ref, next_ref, window, window_ahead, message,
                    extra_message, arrived, extra_arrived, send_sem, recv_sem, extra_send, extra_recv, low_send, low_recv, later_send, later_recv,
                    last_send, last_recv, owner_ref, near_ref, fold_ref, tracers_all, velocity_all, kappa_ref, kmt_ref,
                    depth_rows, table_ref, xs, us, vs, all_ds, all_ks, gs, fe, fn, place_ref, partial_all, edges_all, load_sem,
                    pair_sem, out_sem):
    me = position()
    barrier = pltpu.get_barrier_semaphore()
    for offset in PARTNERS:
        pl.semaphore_signal(barrier, inc=1, device_id=coordinates(me + offset), device_id_type=MESH)
    sources = {
        "owner": (owner_hbm, owner_ref),
        "near": (near_hbm, near_ref),
        "fold": (fold_hbm, fold_ref),
        "kmt": (kmt_hbm, kmt_ref),
        "kappa": (kappa_hbm, kappa_ref),
    }
    loads = {
        name: pltpu.make_async_copy(source, target, load_sem.at[number])
        for number, (name, (source, target)) in enumerate(sources.items())
    }

    def fetch(pair):
        part = pl.ds(2 * pair, 2)
        return (
            pltpu.make_async_copy(tracers_hbm.at[part], tracers_all.at[part], pair_sem.at[0, pair]),
            pltpu.make_async_copy(velocity_hbm.at[part], velocity_all.at[part], pair_sem.at[1, pair]),
        )

    for name in ("owner", "near", "fold", "kmt"):
        loads[name].start()
    for pair in range(PAIRS):
        for copy in fetch(pair):
            copy.start()
    loads["kappa"].start()
    for name in ("owner", "near", "fold"):
        loads[name].wait()
    _, up, chosen = table_of(owner_ref, near_ref, fold_ref, 16)
    pack_edges(
        fetch, loads, up, chosen, tracers_all, velocity_all, kmt_ref, up_ref, down_ref, next_ref, sides_ref, depth_rows,
        edges_all,
    )
    pl.semaphore_wait(barrier, len(PARTNERS))

    def remote(source, target, sends, recvs, number, offset):
        return pltpu.make_async_remote_copy(
            src_ref=source,
            dst_ref=target,
            send_sem=sends.at[number],
            recv_sem=recvs.at[number],
            device_id=coordinates(me + offset),
            device_id_type=MESH,
        )

    plan = []
    for a in range(HOPS - 1, 0, -1):
        plan.append((up_ref, window.at[pl.ds(a * PACK, PACK)], STRIDE * a))
    plan.append((next_ref.at[0], beside_ref.at[0], 1))
    plan.append((next_ref.at[1], beside_ref.at[1], -1))
    first_down = len(plan)
    for a in (2, 1, 3):
        plan.append((down_ref, window_ahead.at[pl.ds(a * PACK, PACK)], -a))
    copies = [
        remote(source, target, send_sem, recv_sem, number, offset)
        for number, (source, target, offset) in enumerate(plan)
    ]
    for number in list(range(first_down, len(plan))) + list(range(first_down)):
        copies[number].start()

    def high_copy(k):
        target = window_ahead.at[pl.ds(HIGH_EXTRA + (k - 1) * PACK, PACK)]
        return remote(up_ref, target, extra_send, extra_recv, k - 1, -k)

    def low_copy(k):
        target = window.at[pl.ds(LOW_EXTRA + (k - 1) * PACK, PACK)]
        return remote(down_ref, target, low_send, low_recv, k - 1, STRIDE * k)

    def from_high(k):
        return (me + k >= HIGH) & (me + k < DEVICES)

    def from_low(k):
        return (me - STRIDE * k >= 0) & (me - STRIDE * k < LOW)

    nothing = jnp.zeros((PACK, 8, LANES), jnp.float32)
    for k in range(1, EXTRAS + 1):
        @pl.when(me >= HIGH)
        def _():
            high_copy(k).start()

        @pl.when(me < LOW)
        def _():
            low_copy(k).start()

        @pl.when(jnp.logical_not(from_high(k)))
        def _():
            window_ahead[pl.ds(HIGH_EXTRA + (k - 1) * PACK, PACK)] = nothing

        @pl.when(jnp.logical_not(from_low(k)))
        def _():
            window[pl.ds(LOW_EXTRA + (k - 1) * PACK, PACK)] = nothing

    window[pl.ds(0, PACK)] = up_ref[...]
    window[pl.ds(OWN_DOWN, PACK)] = down_ref[...]
    window[EMPTY] = jnp.zeros((8, LANES), jnp.float32)
    window_ahead[pl.ds(0, PACK)] = down_ref[...]
    window_ahead[pl.ds(OWN_UP, PACK)] = up_ref[...]
    for number in range(HIGH_EXTRA + EXTRAS * PACK, WINDOW):
        window_ahead[number] = jnp.zeros((8, LANES), jnp.float32)
    table, _, _ = table_of(owner_ref, near_ref, fold_ref, TABLE_ROWS)
    table_out[...] = table
    table_copy = pltpu.make_async_copy(table_out, table_ref, load_sem.at[len(sources)])
    table_copy.start()
    loads["kappa"].wait()
    prepare(kappa_ref, kmt_ref, xs, us, vs, all_ds, all_ks, fe, fn, place_ref, spot_ref, kind_ref)

    def one_pair(pair, carry):
        part = pl.ds(2 * pair, 2)
        interior(
            tracers_all.at[part], velocity_all.at[part], xs, us, vs, all_ds.at[pair], all_ks.at[pair], gs, fe, fn,
            place_ref, partial_all.at[pair], edges_all.at[pair],
        )
        return carry

    def fill(number, halo_name, wrap_name):
        ref = window if number < STRIDE else window_ahead

        def picked(index):
            return ref[jnp.minimum(jnp.maximum(index, 0), EMPTY)]

        wrap = EMPTY
        for q in range(SLOTS):
            r = number * SLOTS + q
            message[number, q] = picked(table_ref[r, AT[halo_name]])
            wrap = wrap + table_ref[r, AT[wrap_name]]
        message[number, SLOTS] = picked(wrap)

    later = []

    def forward(numbers):
        for number in numbers:
            onward = number < STRIDE
            fill(number, *(("behind", "earlier") if onward else ("ahead", "later")))
            offset = number if onward else -STRIDE * (number - STRIDE)
            copy = remote(message.at[number], arrived.at[number], later_send, later_recv, number, offset)
            copy.start()
            later.append(copy)

    lax.fori_loop(EARLY[0], EARLY[1], one_pair, 0)
    table_copy.wait()
    for copy in copies[first_down:]:
        copy.wait_recv()
    for k in range(1, EXTRAS + 1):
        @pl.when(from_high(k))
        def _():
            high_copy(k).wait_recv()

    forward([STRIDE + a for a in range(HOPS - 1, 0, -1)])
    lax.fori_loop(EARLY[1], EARLY[2], one_pair, 0)
    for copy in copies[:first_down]:
        copy.wait_recv()
    for k in range(1, EXTRAS + 1):
        @pl.when(from_low(k))
        def _():
            low_copy(k).wait_recv()

    forward([2, 1, 3])

    def last_copy(k, onward):
        offset = k if onward else -STRIDE * k
        return remote(extra_message.at[k], extra_arrived.at[k], last_send, last_recv, k, offset)

    def extra_picked(ref, row_number):
        return ref[jnp.minimum(jnp.maximum(table_ref[row_number, AT["extra"]], 0), EMPTY)]

    for k in range(STRIDE):
        for goes, number, ref in ((from_high(k), k, window), (from_low(k), STRIDE + k, window_ahead)):
            @pl.when(goes)
            def _():
                for q in range(SLOTS):
                    extra_message[k, q] = extra_picked(ref, number * SLOTS + q)
                if k > 0:
                    last_copy(k, number < STRIDE).start()

    fill(0, "behind", "earlier")
    fill(STRIDE, "ahead", "later")
    lax.fori_loop(EARLY[2], PAIRS, one_pair, 0)
    for copy in later:
        copy.wait()
    for copy in copies:
        copy.wait_send()
    for k in range(1, EXTRAS + 1):
        @pl.when(me >= HIGH)
        def _():
            high_copy(k).wait_send()

        @pl.when(me < LOW)
        def _():
            low_copy(k).wait_send()

    flag = own_row(table_ref, 0, "up") > 0
    for q in range(PACK):
        behind = message[0, q]
        for number in range(1, STRIDE):
            behind = behind + arrived[number, q]
        ahead = message[STRIDE, q]
        for number in range(STRIDE + 1, TARGETS):
            ahead = ahead + arrived[number, q]
        if q < SLOTS:
            halo_ref[q] = jnp.where(flag, behind, ahead)
            halo_ref[SLOTS + q] = jnp.where(flag, ahead, behind)
        else:
            halo_ref[2 * SLOTS] = behind
            halo_ref[2 * SLOTS + 1] = ahead
    for k in range(1, STRIDE):
        for goes, onward in ((from_high(k), True), (from_low(k), False)):
            @pl.when(goes)
            def _():
                last_copy(k, onward).wait_send()

        for comes, onward in ((me >= HIGH, True), (me < LOW, False)):
            @pl.when(comes)
            def _():
                last_copy(k, onward).wait_recv()

    @pl.when((me >= HIGH) | (me < LOW))
    def _():
        for q in range(SLOTS):
            value = extra_message[0, q]
            for k in range(1, STRIDE):
                value = value + extra_arrived[k, q]
            halo_ref[SLOTS + q] = halo_ref[SLOTS + q] + value

    finish_all(table_ref, halo_ref, sides_ref, beside_ref, partial_all, edges_all, out_hbm, around, spot_ref, kind_ref, out_ref,
               out_sem)


def exchange(block_owner, neighbours, fold_partner, tracers, velocity, kappa, kmt):
    anywhere = pl.BlockSpec(memory_space=pltpu.HBM)

    def packets(*lead):
        return pltpu.VMEM(lead + (8, LANES), jnp.float32)

    def tiles(*lead):
        return pltpu.VMEM(lead[:-1] + (8, lead[-1] * LANES), jnp.float32)

    def sems(count):
        return [pltpu.SemaphoreType.DMA((count,))] * 2

    return pl.pallas_call(
        exchange_kernel,
        out_shape=jax.ShapeDtypeStruct((SLOTS, 4, CELLS), jnp.float32),
        in_specs=[anywhere] * 7,
        out_specs=anywhere,
        scratch_shapes=[
            pltpu.VMEM((TABLE_ROWS, LANES), jnp.int32),
            packets(WANT),
            packets(2),
            packets(2 * SLOTS),
            packets(2 * SLOTS + 5),
            pltpu.VMEM((8, TILES * LANES), jnp.int32),
            pltpu.VMEM((8, TILES * LANES), jnp.int32),
            pltpu.VMEM((SLOTS, 4, CELLS), jnp.float32),
            packets(PACK),
            packets(PACK),
            packets(2),
            packets(WINDOW),
            packets(WINDOW),
            packets(TARGETS, PACK),
            packets(STRIDE, SLOTS),
            packets(TARGETS, PACK),
            packets(STRIDE, SLOTS),
            *sems(HOPS - 1 + EXTRAS + 2),
            *sems(EXTRAS),
            *sems(EXTRAS),
            *sems(TARGETS),
            *sems(STRIDE),
            pltpu.VMEM((SLOTS, LANES), jnp.int32),
            pltpu.VMEM((4, SLOTS * LANES), jnp.int32),
            pltpu.VMEM((SLOTS, LANES), jnp.int32),
            pltpu.VMEM((SLOTS, 4, CELLS), jnp.float32),
            pltpu.VMEM((SLOTS, 4, CELLS), jnp.float32),
            pltpu.VMEM((SLOTS, CELLS), jnp.float32),
            pltpu.VMEM((SLOTS, CELLS), jnp.float32),
            packets(3, SLOTS),
            pltpu.SMEM((TABLE_ROWS, LANES), jnp.int32),
            tiles(FRAME),
            tiles(FRAME),
            tiles(FRAME),
            tiles(PAIRS, FRAME),
            tiles(PAIRS, TILES),
            tiles(TILES),
            tiles(TILES + 1),
            tiles(TILES + 1),
            pltpu.VMEM((8, TILES * LANES), jnp.int32),
            tiles(PAIRS, TILES),
            packets(PAIRS, EDGES),
            pltpu.SemaphoreType.DMA((6,)),
            pltpu.SemaphoreType.DMA((2, PAIRS)),
            pltpu.SemaphoreType.DMA((PAIRS,)),
        ],
        compiler_params=pltpu.CompilerParams(collective_id=0, has_side_effects=True, vmem_limit_bytes=BIG),
        name="exchange",
    )(block_owner.reshape(-1, LANES), neighbours.T, fold_partner.reshape(-1, LANES), tracers, velocity, kappa, kmt)


def flux(w, far_a, a, b, far_b):
    return jnp.maximum(w, 0.0) * (5.0 * a + 2.0 * b - far_a) + jnp.minimum(w, 0.0) * (2.0 * a + 5.0 * b - far_b)


def wetness(d):
    sub, _ = iotas()
    return jnp.clip(d - (sub % 2).astype(jnp.float32), 0.0, 1.0)


def swap(z):
    sub, _ = iotas()
    return jnp.where(sub % 2 == 1, pltpu.roll(z, 1, 0), pltpu.roll(z, 7, 0))


def place_of(t, lane):
    flat = lane + t * LANES
    j = ((flat.astype(jnp.float32) + 0.5) * (1.0 / IB)).astype(jnp.int32)
    return j, flat - j * IB


def prepare(kappa_ref, kmt_ref, xs, us, vs, all_ds, all_ks, fe, fn, place_ref, spot_ref, kind_ref):
    sub, lane = iotas()
    zero = jnp.zeros((8, LANES), jnp.float32)
    fe[:, lanes_at(0)] = zero
    fn[:, lanes_at(0)] = zero
    for t in (0, 1, 45, 46):
        for ref in (xs, us, vs):
            ref[:, lanes_at(t)] = zero
        for p in range(PAIRS):
            all_ds[p, :, lanes_at(t)] = zero

    def one_tile(t, rows_kappa, rows_kmt):
        j, i = place_of(t, lane)
        place_ref[:, lanes_at(t)] = i
        spot_ref[:, lanes_at(t)] = j + jnp.where(i >= IB // 2, SIDE, 0)
        kind_ref[:, lanes_at(t)] = jnp.where(
            (i == 0) | (i == IB - 1), 1, jnp.where((i == 1) | (i == IB - 2), 2, 0)
        )
        for p in range(PAIRS):
            depth = jnp.where(sub < 4, row(rows_kmt, 2 * p), row(rows_kmt, 2 * p + 1))
            all_ds[p, :, lanes_at(t + 2)] = wetness(depth)
            all_ks[p, :, lanes_at(t)] = jnp.where(sub < 4, row(rows_kappa, 2 * p), row(rows_kappa, 2 * p + 1))

    for t in range(TILES):
        one_tile(t, load_rows(kappa_ref, t), load_rows(kmt_ref, t))


def interior(tracers_ref, velocity_ref, xs, us, vs, ds, ks, gs, fe, fn, place_ref, partial_ref, edges_ref):
    sub, lane = iotas()
    lower_half = sub % 4 < 2
    column = lane % SIDE
    base_near = column * IB + jnp.where(lane >= SIDE, IB - 1, 0)
    base_far = column * IB + jnp.where(lane >= SIDE, IB - 2, 1)
    bases = (base_near // LANES, base_near % LANES), (base_far // LANES, base_far % LANES)
    for t in range(TILES):
        xs[:, lanes_at(t + 2)] = jnp.concatenate([load4(tracers_ref, 0, t), load4(tracers_ref, 1, t)], axis=0)
        speed = jnp.concatenate([load4(velocity_ref, 0, t), load4(velocity_ref, 1, t)], axis=0)
        us[:, lanes_at(t + 2)] = jnp.where(lower_half, speed, pltpu.roll(speed, 2, 0))
        vs[:, lanes_at(t + 2)] = jnp.where(lower_half, pltpu.roll(speed, 6, 0), speed)
    turned = {}

    def tile_of(name, ref, tile):
        if (name, tile, 0) not in turned:
            turned[name, tile, 0] = ref[:, lanes_at(tile)]
        return turned[name, tile, 0]

    def turn(name, ref, tile, r):
        if (name, tile, r) not in turned:
            turned[name, tile, r] = pltpu.roll(tile_of(name, ref, tile), LANES - r, 1)
        return turned[name, tile, r]

    def shift(name, ref, t, s):
        tile = t + 2 + s // LANES
        r = s % LANES
        return jnp.where(lane < LANES - r, turn(name, ref, tile, r), turn(name, ref, tile + 1, r))

    zero = jnp.zeros((8, LANES), jnp.float32)
    edges = [zero] * 5
    for t in range(TILES):
        for key in [k for k in turned if k[1] < t]:
            del turned[key]
        i = place_ref[:, lanes_at(t)]
        x, u, v, wet = (
            tile_of(name, ref, t + 2) for name, ref in (("x", xs), ("u", us), ("v", vs), ("d", ds))
        )
        last = i == IB - 1
        west = jnp.where(i == 0, 0.0, shift("x", xs, t, -1))
        east = jnp.where(last, 0.0, shift("x", xs, t, 1))
        east_far = jnp.where(i >= IB - 2, 0.0, shift("x", xs, t, 2))
        wet_east = jnp.where(last, 0.0, shift("d", ds, t, 1))
        wet_north = shift("d", ds, t, IB)
        south, north, north_far = (shift("x", xs, t, s) for s in (-IB, IB, 2 * IB))
        flux_east = flux((u + shift("u", us, t, 1)) * (wet * wet_east), west, x, east, east_far)
        flux_north = flux((v + shift("v", vs, t, IB)) * (wet * wet_north), south, x, north, north_far)
        fe[:, lanes_at(t + 1)] = flux_east
        fn[:, lanes_at(t + 1)] = flux_north
    back = {}

    def turned_flux(name, ref, tile, amount):
        if (name, tile) not in back:
            back[name, tile] = pltpu.roll(ref[:, lanes_at(tile)], amount, 1)
        return back[name, tile]

    for t in range(TILES):
        i = place_ref[:, lanes_at(t)]
        x, u, wet = (ref[:, lanes_at(t + 2)] for ref in (xs, us, ds))
        flux_east, flux_north = fe[:, lanes_at(t + 1)], fn[:, lanes_at(t + 1)]
        flux_west = jnp.where(lane < 1, turned_flux("e", fe, t, 1), turned_flux("e", fe, t + 1, 1))
        flux_west = jnp.where(i == 0, 0.0, flux_west)
        flux_south = jnp.where(lane < IB, turned_flux("n", fn, t, IB), turned_flux("n", fn, t + 1, IB))
        divergence = flux_east - flux_west + (flux_north - flux_south)
        explicit = x - (wet * (COURANT / 12.0)) * divergence
        coupling = ks[:, lanes_at(t)] * wet * swap(wet)
        share = coupling / (1.0 + 2.0 * coupling)
        partial_ref[:, lanes_at(t)] = explicit + share * (swap(explicit) - explicit)
        gs[:, lanes_at(t)] = share
        values = ((1, u), (0, wet), (1, wet), (0, share), (1, share))
        for n, (k, value) in enumerate(values):
            tile, at = bases[k]
            edges[n] = jnp.where(tile == t, take(value, at), edges[n])
    for n in range(5):
        edges_ref[3 + n] = edges[n]
    for k, number in enumerate((0, 1, JB - 1, JB - 2)):
        for n, (ref, offset) in enumerate(((xs, 2), (vs, 2), (ds, 2), (gs, 0))):
            edges_ref[8 + 4 * k + n] = line(lambda t: ref[:, lanes_at(t + offset)], number * IB, lane)


def finish_all(table_ref, halo, sides_ref, beside_ref, partial_all, edges_all, out_hbm, around, spot_ref, kind_ref, out_ref,
               sems):
    for number in range(2 * SLOTS):
        around[number] = sides_ref[number]
    around[2 * SLOTS] = beside_ref[0]
    around[2 * SLOTS + 1] = beside_ref[1]
    around[2 * SLOTS + 2] = halo[2 * SLOTS]
    around[2 * SLOTS + 3] = halo[2 * SLOTS + 1]
    around[2 * SLOTS + 4] = jnp.zeros((8, LANES), jnp.float32)

    def store(pair):
        part = pl.ds(2 * pair, 2)
        return pltpu.make_async_copy(out_ref.at[part], out_hbm.at[part], sems.at[pair])

    def one_pair(pair, carry):
        finish_pair(
            pair, table_ref, halo, around, partial_all.at[pair], edges_all.at[pair], spot_ref, kind_ref,
            out_ref.at[pl.ds(2 * pair, 2)],
        )
        store(pair).start()
        return carry

    lax.fori_loop(0, PAIRS, one_pair, 0)
    for pair in range(PAIRS):
        store(pair).wait()


def finish_pair(pair, table_ref, halo, around, partial_ref, edges_ref, spot_ref, kind_ref, out_ref):
    sub, lane = iotas()
    upper = sub < 4
    odd = sub % 2 == 1

    def paired(first, second):
        return jnp.where(upper, first, second)

    def across(first, second):
        near = jnp.where(upper, first, pltpu.roll(second, 4, 0))
        return near, jnp.where(upper, pltpu.roll(first, 4, 0), second)

    def unpack(packet):
        a, b = pltpu.roll(packet, 38, 1), pltpu.roll(packet, 76, 1)
        c, d = pltpu.roll(packet, 100, 1), pltpu.roll(packet, 114, 1)

        def joined(first, second, third):
            return jnp.where(lane < 38, first, jnp.where(lane < 76, second, third))

        speed = jnp.where(odd, joined(row(a, 2), row(b, 3), row(d, 6)), joined(row(a, 0), row(b, 1), row(c, 6)))
        return speed, joined(row(a, 4), row(b, 5), row(d, 7))

    def rows_from(first, second):
        near, far = across(first, second)
        (speed_a, depth_a), (speed_b, depth_b) = unpack(first), unpack(second)
        return near, far, paired(speed_a, speed_b), paired(depth_a, depth_b)

    slots = (2 * pair, 2 * pair + 1)
    south = rows_from(halo[slots[0]], halo[slots[1]])
    north = rows_from(halo[SLOTS + slots[0]], halo[SLOTS + slots[1]])
    folded = paired(*(own_row(table_ref, q, "fold") for q in slots)) > 0
    back = jnp.where(lane < IB, IB - 1 - lane, lane)
    north = [
        jnp.where(folded, sign * take(value, back), value) for value, sign in zip(north, (1.0, 1.0, -1.0, 1.0))
    ]
    bodies, speeds, depths = [], [], []
    for q in slots:
        west, east = (around[jnp.minimum(jnp.maximum(own_row(table_ref, q, name), 0), 2 * SLOTS + 4)] for name in ("west", "east"))
        bodies.append(jnp.where(lane < SIDE, west, pltpu.roll(east, SIDE, 1)))
        aux = jnp.where(lane < SIDE, pltpu.roll(west, SIDE, 1), east)
        speeds.append(jnp.where(odd, row(aux, 1), row(aux, 0)))
        depths.append(row(aux, 2))
    side_near, side_far = across(*bodies)
    side_speed, side_depth = paired(*speeds), paired(*depths)
    keep = paired(*(own_row(table_ref, q, "live") for q in slots)) > 0

    def boundary(sign, halo_near, halo_far, halo_speed, halo_depth, own):
        (x_near, x_far), (speed_near, speed_far), (wet_near, wet_far), (share_near, share_far) = own
        outer = sign * (halo_speed + speed_near) * (wetness(halo_depth) * wet_near)
        inner = sign * (speed_near + speed_far) * (wet_near * wet_far)
        lost = jnp.minimum(inner, 0.0) * halo_near
        near = -(COURANT / 12.0) * wet_near * (flux(outer, x_far, x_near, halo_near, halo_far) + lost)
        far = (COURANT / 12.0) * wet_far * lost
        return near + share_near * (swap(near) - near), far + share_far * (swap(far) - far)

    edges = [edges_ref[n] for n in range(8)]
    rows = [edges_ref[8 + n] for n in range(16)]
    side_sign = jnp.where(lane < SIDE, -1.0, 1.0)
    side = boundary(side_sign, side_near, side_far, side_speed, side_depth, [edges[2 * n : 2 * n + 2] for n in range(4)])
    add_south = boundary(-1.0, *south, list(zip(rows[0:4], rows[4:8])))
    add_north = boundary(1.0, *north, list(zip(rows[8:12], rows[12:16])))
    pieces = {}
    for start, value in zip((0, IB, (JB - 1) * IB, (JB - 2) * IB), (*add_south, *add_north)):
        first, at = start // LANES, start % LANES
        moved = pltpu.roll(value, at, 1) if at else value
        pieces.setdefault(first, []).append((moved, (lane >= at) & (lane < at + IB)))
        if at + IB > LANES:
            pieces.setdefault(first + 1, []).append((moved, lane < at + IB - LANES))
    for t in range(TILES):
        kind, index = kind_ref[:, lanes_at(t)], spot_ref[:, lanes_at(t)]
        value = partial_ref[:, lanes_at(t)]
        value = value + jnp.where(kind == 1, take(side[0], index), jnp.where(kind == 2, take(side[1], index), 0.0))
        for moved, mask in pieces.get(t, []):
            value = value + jnp.where(mask, moved, 0.0)
        value = jnp.where(keep, value, 0.0)
        width = min(LANES, CELLS - t * LANES)
        out_ref[0, :, pl.ds(t * LANES, width)] = value[0:4, :width]
        out_ref[1, :, pl.ds(t * LANES, width)] = value[4:8, :width]


def per_device(tracers, velocity, kappa, kmt, block_owner, neighbours, fold_partner):
    return exchange(block_owner, neighbours, fold_partner, tracers, velocity, kappa, kmt)


def solution(mesh):
    placed = (
        P(("blk", "sub"), None, None),
        P(("blk", "sub"), None, None),
        P(("blk", "sub"), None),
        P(("blk", "sub"), None),
        P(),
        P(),
        P(),
    )
    return jax.shard_map(
        per_device,
        mesh=mesh,
        in_specs=placed,
        out_specs=P(("blk", "sub"), None, None),
        check_vma=False,
    )
```
